32 devices in a mesh: section: 4 (over y, x), seq: 8 (over z, core).
Axes of the slice: x: 2, y: 2, z: 4, core: 2. Of those that a mesh axis runs over, the one named last changes fastest.
Arguments:
- frames_in: bfloat16 [4, 16, 128, 1024], P(None, 'seq'), may hold values from -6 to 6
- order: int32 [4], replicated, may hold values from 0 to 3, each once
- owner: int32 [128], replicated, may hold values from 0 to 7, as said below
- qkv_weight: bfloat16 [4, 1024, 3072], P('section'), may hold values from -1 to 1
- out_weight: bfloat16 [4, 1024, 1024], P('section'), may hold values from -0.1875 to 0.1875
- gains: float32 [4, 1024], P('section'), may hold values from 0.1 to 1.9
Outputs:
- layers_out: bfloat16 [4, 16, 256, 1024], P('section', None, 'seq')
The draws below stay inside these ranges and needn't reach their ends.
Inputs may be any that keep to these rules, and one draw needn't show every extreme that they name: `owner`: no device owns more than 32 rows, and some device owns exactly 32.
All inputs are finite; a program needn't handle non-finite values.
Results may differ from the reference program's by a relative error of at most 0.02.
Values may be sent and summed in bfloat16 or wider, within the bound.
No kernel may reach another device: no remote copies, remote signals or barrier semaphores. Data moves between devices by JAX's collectives and lax.ppermute only.
A program may use at most 128 MiB of HBM per device.

```python
import jax
import jax.numpy as jnp
from jax import lax

D = 1024
HEADS = 16
HEAD_DIM = 64
IMG_ROWS = 128
FRAMES = 4
COLS = 4
LINES = 16
MAX_ROWS = 32
CLIPS = 4
LAYERS = 4
N_SEQ = 8


def draw_owner(key, part):
    per_device = IMG_ROWS // N_SEQ
    first_key, second_key = jax.random.split(jax.random.fold_in(key, 7))
    devices = jax.random.permutation(first_key, N_SEQ).astype(jnp.int32)
    pattern = jnp.array([2 * per_device, per_device + per_device // 2, per_device // 2, 0], dtype=jnp.int32)
    counts = pattern[jnp.arange(N_SEQ, dtype=jnp.int32) % 4]
    ends = jnp.cumsum(counts)
    position = jnp.arange(IMG_ROWS, dtype=jnp.int32)
    placed = jnp.sum((position[:, None] >= ends[None, :]).astype(jnp.int32), axis=1)
    sorted_owner = devices[placed]
    shuffle = jax.random.permutation(second_key, IMG_ROWS).astype(jnp.int32)
    owner = jnp.zeros((IMG_ROWS,), jnp.int32).at[shuffle].set(sorted_owner)
    return owner.astype(jnp.int32)


def draw_qkv_weight(key, part):
    base_key = jax.random.fold_in(jax.random.fold_in(key, 31), 0)
    spread = D ** (-0.5)
    matrix = jax.random.normal(base_key, (LAYERS, D, 3 * D), jnp.float32) * spread
    return jnp.clip(matrix, -1.0, 1.0).astype(jnp.bfloat16)


def block_scale(own_key, extent, shards, least, high):
    factor_of = 1.0
    for dim, parts in shards:
        heights = jax.random.uniform(jax.random.fold_in(jax.random.fold_in(own_key, 6), dim), (parts,), jnp.float32, least / len(shards), high / len(shards))
        factor_of = factor_of * jnp.repeat(jnp.exp(heights), extent[dim] // parts).reshape((-1,) + (1,) * (len(extent) - 1 - dim))
    return factor_of


def normal_values(rng, extent, scale, bound, shards=(), kind=jnp.bfloat16):
    values = scale * jax.random.normal(rng, extent, jnp.float32)
    if shards:
        values = values * block_scale(rng, extent, shards, -0.22, 0.18)
    return jnp.clip(values, -bound, bound).astype(kind)


def setup_inputs(seed: int = 0) -> dict:
    keys = jax.random.split(jax.random.key(seed), 7)
    return {
        "frames_in": normal_values(keys[0], (CLIPS, LINES, IMG_ROWS, D), 1.0, 6.0, ((1, 8),)),
        "order": jax.random.permutation(keys[1], CLIPS).astype(jnp.int32),
        "owner": draw_owner(jax.random.fold_in(keys[6], 71), 0),
        "qkv_weight": draw_qkv_weight(jax.random.fold_in(keys[6], 71), 0),
        "out_weight": normal_values(keys[4], (LAYERS, D, D), D ** -0.5, 0.1875, ((0, 4),)),
        "gains": jnp.clip(1.0 + 0.18 * jax.random.normal(keys[5], (LAYERS, D), jnp.float32), 0.1, 1.9),
    }


def scaled_norm(volume, gain_row):
    values = volume.astype(jnp.float32)
    mean_square = lax.optimization_barrier(jnp.mean(values * values, axis=-1, keepdims=True))
    return (values * lax.rsqrt(mean_square + 1e-06) * gain_row.astype(jnp.float32)).astype(jnp.bfloat16)

def attention_layer(volume, gain_row, qkv_mat, out_mat, causal):
    extent_a, length, extent_c, features = volume.shape
    normed = scaled_norm(volume, gain_row)
    packed = jnp.dot(normed.reshape(-1, features), qkv_mat, preferred_element_type=jnp.float32)
    packed = packed.astype(jnp.bfloat16).reshape(extent_a, length, extent_c, 3, HEADS, HEAD_DIM)
    queries = packed[:, :, :, 0].astype(jnp.float32)
    key_rows = packed[:, :, :, 1].astype(jnp.float32)
    values = packed[:, :, :, 2].astype(jnp.float32)
    scores = jnp.einsum('alchd,amchd->achlm', queries, key_rows) * HEAD_DIM ** (-0.5)
    if causal:
        allowed = jnp.arange(length)[:, None] >= jnp.arange(length)[None, :]
        scores = jnp.where(allowed, scores, -1e+30)
    weights = jax.nn.softmax(scores, axis=-1).astype(jnp.bfloat16)
    context = jnp.einsum('achlm,amchd->alchd', weights.astype(jnp.float32), values)
    context = context.astype(jnp.bfloat16).reshape(-1, features)
    update = jnp.dot(context, out_mat, preferred_element_type=jnp.float32).reshape(volume.shape)
    return (volume.astype(jnp.float32) + update).astype(jnp.bfloat16)

def reference(frames_in, order, owner, qkv_weight, out_weight, gains):
    position = jnp.arange(IMG_ROWS, dtype=jnp.int32)
    alike = (owner[:, None] == owner[None, :]) & (position[:, None] < position[None, :])
    slot_of = lax.optimization_barrier(jnp.sum(alike.astype(jnp.int32), axis=0))
    device_ids = jnp.arange(N_SEQ, dtype=jnp.int32)
    slot_ids = jnp.arange(MAX_ROWS, dtype=jnp.int32)
    match = (owner[None, None, :] == device_ids[:, None, None]) & (slot_of[None, None, :] == slot_ids[None, :, None])
    chosen = lax.optimization_barrier(jnp.sum(jnp.where(match, position[None, None, :], 0), axis=2)).reshape(-1).astype(jnp.int32)
    present = jnp.any(match, axis=2).reshape(-1)
    outputs = []
    for turn in range(CLIPS):
        clip_lines = lax.dynamic_index_in_dim(frames_in, order[turn], 0, keepdims=False)
        mixed = attention_layer(clip_lines[:, :, None, :], gains[0], qkv_weight[0], out_weight[0], False)[:, :, 0, :]
        mixed = attention_layer(mixed.reshape(1, FRAMES, COLS * IMG_ROWS, D), gains[1], qkv_weight[1], out_weight[1], False)
        mixed = mixed.reshape(LINES, IMG_ROWS, D)
        for layer in (2, 3):
            mixed = attention_layer(mixed.reshape(FRAMES, COLS, IMG_ROWS, D), gains[layer], qkv_weight[layer], out_weight[layer], True)
            mixed = mixed.reshape(LINES, IMG_ROWS, D)
        picked = jnp.take(mixed, chosen, axis=1)
        picked = jnp.where(present[None, :, None], picked, jnp.zeros((), jnp.bfloat16))
        outputs.append(picked)
    return jnp.stack(outputs[::-1])
```

```python
import functools

import jax
import jax.numpy as jnp
from jax import lax
from jax.experimental import pallas as pl
from jax.experimental.pallas import tpu as pltpu
from jax.sharding import PartitionSpec as P

HEADS = 16
FRAMES = 4
GROUP = 4
VMEM_BYTES = 40 * 1024 * 1024


def scaled_norm(values, gain_row):
    mean_square = jnp.mean(values * values, axis=-1, keepdims=True)
    return (values * lax.rsqrt(mean_square + 1e-06) * gain_row).astype(jnp.bfloat16)


def group_context(normed, q_ref, k_ref, v_ref, head_size, length, bias):
    def projected(ref):
        return jnp.dot(normed, ref[...], preferred_element_type=jnp.float32).astype(jnp.bfloat16)

    queries, key_rows, values = projected(q_ref), projected(k_ref), projected(v_ref)
    width = queries.shape[1]
    heads = width // head_size
    lane_head = lax.broadcasted_iota(jnp.int32, (length, width), 1) // head_size
    zero = jnp.zeros((length, width), jnp.bfloat16)
    contexts = []
    for start in range(0, normed.shape[0], length):
        block = slice(start, start + length)

        def per_head(part):
            return jnp.concatenate([jnp.where(lane_head == h, part, zero) for h in range(heads)], axis=0)

        scores = lax.dot_general(
            queries[block],
            per_head(key_rows[block]),
            (((1,), (1,)), ((), ())),
            preferred_element_type=jnp.float32,
        ) * head_size ** (-0.5)
        weights = []
        for h in range(heads):
            own = scores[:, h * length : (h + 1) * length]
            if bias is not None:
                own = own + bias
            grown = jnp.exp(own - jnp.max(own, axis=-1, keepdims=True))
            share = 1.0 / jnp.sum(grown, axis=-1, keepdims=True)
            weights.append((grown * share).astype(jnp.bfloat16))
        context = jnp.dot(
            jnp.concatenate(weights, axis=1),
            per_head(values[block]),
            preferred_element_type=jnp.float32,
        )
        contexts.append(context.astype(jnp.bfloat16))
    return contexts[0] if len(contexts) == 1 else jnp.concatenate(contexts, axis=0)


def column_kernel(head_size, length, order_ref, x_ref, gain_ref, q_ref, k_ref, v_ref, o_ref, spread_ref, y_ref, normed, total):
    step = pl.program_id(0)

    @pl.when(step == 0)
    def _():
        normed[...] = scaled_norm(x_ref[0].astype(jnp.float32), gain_ref[...])
        total[...] = x_ref[0].astype(jnp.float32)

    context = group_context(normed[...], q_ref, k_ref, v_ref, head_size, length, None)
    total[...] += jnp.dot(context, o_ref[...], preferred_element_type=jnp.float32)

    @pl.when(step == pl.num_programs(0) - 1)
    def _():
        y_ref[...] = jnp.dot(
            spread_ref[...], total[...].astype(jnp.bfloat16), preferred_element_type=jnp.float32
        ).astype(jnp.bfloat16)


def row_bias(section, length, rows, columns):
    query = lax.broadcasted_iota(jnp.int32, (length, length), 0)
    key = lax.broadcasted_iota(jnp.int32, (length, length), 1)
    same_row = (query % rows) == (key % rows)
    query_line, key_line = query // rows, key // rows
    query_col, key_col = query_line % columns, key_line % columns
    across_frames = query_col == key_col
    across_columns = ((query_line // columns) == (key_line // columns)) & (key_col <= query_col)
    chosen = jnp.where(section == 1, across_frames.astype(jnp.int32), across_columns.astype(jnp.int32))
    return jnp.where(same_row & (chosen == 1), 0.0, -1e30)


def tick_kernel(head_size, rows, columns, packs, flag_ref, x_ref, f_ref, gain_ref, q_ref, k_ref, v_ref, o_ref, *rest):
    if packs:
        pack_ref, y_ref, normed, total, bias = rest
    else:
        y_ref, normed, total, bias = rest
    step = pl.program_id(0)
    last = pl.num_programs(0) - 1
    length = x_ref.shape[0]
    section, mode = flag_ref[0], flag_ref[1]

    @pl.when(mode == 0)
    def _():
        @pl.when(step == 0)
        def _():
            normed[...] = scaled_norm(x_ref[...].astype(jnp.float32), gain_ref[...])
            total[...] = x_ref[...].astype(jnp.float32)
            bias[...] = row_bias(section, length, rows, columns)

        context = group_context(normed[...], q_ref, k_ref, v_ref, head_size, length, bias[...])
        total[...] += jnp.dot(context, o_ref[...], preferred_element_type=jnp.float32)

    def given(value):
        if packs:
            value = jnp.dot(pack_ref[...], value, preferred_element_type=jnp.float32).astype(jnp.bfloat16)
        y_ref[...] = value

    @pl.when((step == last) & (mode == 0))
    def _():
        given(total[...].astype(jnp.bfloat16))

    @pl.when((step == last) & (mode == 1))
    def _():
        given(f_ref[...])

    @pl.when((step == last) & (mode == 2))
    def _():
        given(x_ref[...])


def weight_specs(features, width, groups):
    return [
        pl.BlockSpec((1, features), lambda g, s: (0, 0)),
        pl.BlockSpec((features, width), lambda g, s: (0, g)),
        pl.BlockSpec((features, width), lambda g, s: (0, g + groups)),
        pl.BlockSpec((features, width), lambda g, s: (0, g + 2 * groups)),
        pl.BlockSpec((width, features), lambda g, s: (g, 0)),
    ]


def cost(positions, features):
    return pl.CostEstimate(
        flops=10 * positions * features * features,
        bytes_accessed=8 * features * features + 8 * positions * features,
        transcendentals=HEADS * positions * positions,
    )


def column_pass(frames, turn, weights, spread, lines_dev):
    clips, positions, features = frames.shape
    gain_row, qkv_mat, out_mat = weights
    head_size = features // HEADS
    width = GROUP * head_size
    groups = features // width
    length = positions // lines_dev
    return pl.pallas_call(
        functools.partial(column_kernel, head_size, length),
        out_shape=jax.ShapeDtypeStruct((positions, features), jnp.bfloat16),
        grid_spec=pltpu.PrefetchScalarGridSpec(
            num_scalar_prefetch=1,
            grid=(groups,),
            in_specs=[pl.BlockSpec((1, positions, features), lambda g, s: (s[0], 0, 0))]
            + weight_specs(features, width, groups)
            + [pl.BlockSpec(spread.shape, lambda g, s: (0, 0))],
            out_specs=pl.BlockSpec((positions, features), lambda g, s: (0, 0)),
            scratch_shapes=[
                pltpu.VMEM((positions, features), jnp.bfloat16),
                pltpu.VMEM((positions, features), jnp.float32),
            ],
        ),
        compiler_params=pltpu.CompilerParams(vmem_limit_bytes=VMEM_BYTES),
        cost_estimate=cost(positions, features),
        name="column_pass",
    )(turn, frames, gain_row, qkv_mat, qkv_mat, qkv_mat, out_mat, spread)


def tick_pass(flags, x, f, weights, rows, columns, pack=None):
    positions, features = x.shape
    gain_row, qkv_mat, out_mat = weights
    head_size = features // HEADS
    width = GROUP * head_size
    groups = features // width
    whole = pl.BlockSpec((positions, features), lambda g, s: (0, 0))
    out_rows = positions if pack is None else pack.shape[0]
    extra = [] if pack is None else [pack]
    return pl.pallas_call(
        functools.partial(tick_kernel, head_size, rows, columns, pack is not None),
        out_shape=jax.ShapeDtypeStruct((out_rows, features), jnp.bfloat16),
        grid_spec=pltpu.PrefetchScalarGridSpec(
            num_scalar_prefetch=1,
            grid=(groups,),
            in_specs=[whole, whole]
            + weight_specs(features, width, groups)
            + [pl.BlockSpec(a.shape, lambda g, s: (0, 0)) for a in extra],
            out_specs=pl.BlockSpec((out_rows, features), lambda g, s: (0, 0)),
            scratch_shapes=[
                pltpu.VMEM((positions, features), jnp.bfloat16),
                pltpu.VMEM((positions, features), jnp.float32),
                pltpu.VMEM((positions, positions), jnp.float32),
            ],
        ),
        compiler_params=pltpu.CompilerParams(vmem_limit_bytes=VMEM_BYTES),
        cost_estimate=cost(positions, features),
        name="tick_pass",
    )(flags, x, f, gain_row, qkv_mat, qkv_mat, qkv_mat, out_mat, *extra)


def settle_kernel(*refs):
    *parts, out_ref = refs
    half = len(parts) // 2
    total = None
    for place_ref, part_ref in zip(parts[:half], parts[half:]):
        term = jnp.dot(place_ref[...], part_ref[...], preferred_element_type=jnp.float32)
        total = term if total is None else total + term
    out_ref[...] = total.astype(jnp.bfloat16)


def settle(places, parts):
    rows, features = places[0].shape[0], parts[0].shape[1]
    depth = sum(p.shape[0] for p in parts)
    return pl.pallas_call(
        settle_kernel,
        out_shape=jax.ShapeDtypeStruct((rows, features), jnp.bfloat16),
        compiler_params=pltpu.CompilerParams(vmem_limit_bytes=VMEM_BYTES),
        cost_estimate=pl.CostEstimate(
            flops=2 * rows * depth * features, bytes_accessed=2 * (rows + depth) * features, transcendentals=0
        ),
        name="settle",
    )(*places, *parts)


def local(frames_in, order, owner, qkv_weight, out_weight, gains):
    sections = lax.axis_size("section")
    peers = lax.axis_size("seq")
    section = lax.axis_index("section")
    me = lax.axis_index("seq")
    clips, lines_dev, img_rows, features = frames_in.shape
    lines = lines_dev * peers
    columns = lines // FRAMES
    max_rows = 2 * img_rows // peers
    chunks = lines_dev
    strides = peers * chunks
    rows = img_rows // strides
    most = -(-max_rows // strides)
    weights = (gains, qkv_weight[0], out_weight[0])
    frames = frames_in.reshape(clips, lines_dev * img_rows, features)

    position = jnp.arange(img_rows, dtype=jnp.int32)
    before = (owner[None, :] < owner[:, None]) | (
        (owner[None, :] == owner[:, None]) & (position[None, :] < position[:, None])
    )
    rank = jnp.sum(before.astype(jnp.int32), axis=1)
    device_ids = jnp.arange(peers, dtype=jnp.int32)
    starts = jnp.sum((owner[None, :] < device_ids[:, None]).astype(jnp.int32), axis=1)
    ends = jnp.sum((owner[None, :] <= device_ids[:, None]).astype(jnp.int32), axis=1)

    out_id = jnp.arange(lines_dev * img_rows, dtype=jnp.int32)
    out_i = out_id % rows
    out_line = out_id // rows % lines_dev
    out_chunk = out_id // (rows * lines_dev) % chunks
    out_peer = out_id // (rows * lines_dev * chunks)
    wanted = out_i * strides + out_chunk * peers + out_peer
    spread = (
        (out_line[:, None] == (out_id // img_rows)[None, :])
        & (wanted[:, None] == jnp.tile(rank, lines_dev)[None, :])
    ).astype(jnp.bfloat16)

    send_id = jnp.arange(peers * most * lines, dtype=jnp.int32)
    send_line = send_id % lines
    send_n = send_id // lines % most
    send_start = jnp.repeat(starts, most * lines)
    send_end = jnp.repeat(ends, most * lines)
    packs = []
    for chunk in range(chunks):
        residue = chunk * peers + me
        place = send_start + (residue - send_start) % strides + strides * send_n
        row_of = jnp.where(place < send_end, place // strides, -1)
        packs.append(
            (
                (send_line[:, None] == (position // rows)[None, :])
                & (row_of[:, None] == (position % rows)[None, :])
            ).astype(jnp.bfloat16)
        )

    slot_id = jnp.arange(lines * max_rows, dtype=jnp.int32)
    my_start = lax.dynamic_index_in_dim(starts, me, 0, keepdims=False)
    places = []
    for chunk in range(chunks):
        residue = chunk * peers + send_id // (lines * most)
        slot_of = (residue - my_start) % strides + strides * send_n
        places.append(
            (
                ((slot_id // max_rows)[:, None] == send_line[None, :])
                & ((slot_id % max_rows)[:, None] == slot_of[None, :])
            ).astype(jnp.bfloat16)
        )

    homes = [1, 0, 2, 3]
    fresh = []
    for clip in range(clips):
        turn = order[sections - 1 - homes[clip]].reshape(1)
        mixed = column_pass(frames, turn, weights, spread, lines_dev)
        swapped = lax.all_to_all(
            mixed.reshape(peers, chunks * lines_dev * rows, features), "seq", split_axis=0, concat_axis=0, tiled=True
        ).reshape(peers, chunks, lines_dev * rows, features)
        fresh.append([swapped[:, chunk].reshape(img_rows, features) for chunk in range(chunks)])

    ticks = clips + sections - 2
    send = list(fresh[0])
    held = [None] * chunks
    for tick in range(ticks):
        pairs = []
        if tick <= clips:
            pairs.append((0, 1))
        if 1 <= tick <= clips:
            pairs.append((1, 2))
        if 2 <= tick <= clips + 1:
            pairs.append((2, 3))
        if tick in (3, 4):
            pairs.append((3, 0))
        if tick == 5:
            pairs.append((3, 2))
        final = tick == ticks - 1
        for chunk in range(chunks):
            x = lax.ppermute(send[chunk], "section", pairs)
            if final:
                mode = jnp.where(section < 2, 1, jnp.where(section == 2, 2, 0))
                f = held[chunk]
            elif tick + 1 < clips:
                mode = jnp.where(section == 0, 1, 0)
                f = fresh[tick + 1][chunk]
            else:
                mode = jnp.where(section == 0, 2, 0)
                f = x
            flags = jnp.stack([section, mode]).astype(jnp.int32)
            send[chunk] = tick_pass(flags, x, f, weights, rows, columns, packs[chunk] if final else None)
            held[chunk] = x

    arrived = []
    for chunk in range(chunks):
        swapped = lax.all_to_all(
            send[chunk].reshape(peers, most * lines, features), "seq", split_axis=0, concat_axis=0, tiled=True
        )
        arrived.append(swapped.reshape(peers * most * lines, features))
    return settle(places, arrived).reshape(1, lines, max_rows, features)


def solution(mesh):
    placed = (
        P(None, "seq", None, None),
        P(),
        P(),
        P("section", None, None),
        P("section", None, None),
        P("section", None),
    )
    return jax.shard_map(
        local,
        mesh=mesh,
        in_specs=placed,
        out_specs=P("section", None, "seq", None),
        check_vma=False,
    )
```

```python
import functools

import jax
import jax.numpy as jnp
from jax import lax
from jax.experimental import pallas as pl
from jax.experimental.pallas import tpu as pltpu
from jax.sharding import PartitionSpec as P

HEADS = 16
FRAMES = 4
GROUP = 4
VMEM_BYTES = 32 * 1024 * 1024
IN_VMEM = pl.BlockSpec(memory_space=pltpu.VMEM)
IN_SMEM = pl.BlockSpec(memory_space=pltpu.SMEM)


def iota(shape, dim):
    return lax.broadcasted_iota(jnp.int32, shape, dim)


def scaled_norm(values, gain_row):
    mean_square = jnp.mean(values * values, axis=-1, keepdims=True)
    return (values * lax.rsqrt(mean_square + 1e-06) * gain_row).astype(jnp.bfloat16)


def layer(x, weights, length, bias):
    gain_ref, qkv_ref, out_ref = weights
    positions, features = x.shape
    head_size = features // HEADS
    width = GROUP * head_size
    groups = features // width
    values = x.astype(jnp.float32)
    normed = scaled_norm(values, gain_ref[...])
    lane_head = lax.div(iota((length, width), 1), head_size)
    zero = jnp.zeros((length, width), jnp.bfloat16)
    ones = jnp.concatenate([(lane_head == h).astype(jnp.bfloat16) for h in range(GROUP)], axis=0)

    def per_head(part):
        return jnp.concatenate([jnp.where(lane_head == h, part, zero) for h in range(GROUP)], axis=0)

    def projections(g):
        return [
            jnp.dot(
                normed,
                qkv_ref[:, part * features + g * width : part * features + (g + 1) * width],
                preferred_element_type=jnp.float32,
            ).astype(jnp.bfloat16)
            for part in range(3)
        ]

    def attended(queries, key_rows, value_rows):
        scores = lax.dot_general(
            queries, per_head(key_rows), (((1,), (1,)), ((), ())), preferred_element_type=jnp.float32
        ) * head_size ** (-0.5)
        grown = []
        for h in range(GROUP):
            own = scores[:, h * length : (h + 1) * length]
            if bias is not None:
                own = own + bias
            grown.append(jnp.exp(own - jnp.max(own, axis=-1, keepdims=True)).astype(jnp.bfloat16))
        grown = jnp.concatenate(grown, axis=1)
        weighted = jnp.dot(grown, per_head(value_rows), preferred_element_type=jnp.float32)
        total = jnp.dot(grown, ones, preferred_element_type=jnp.float32)
        return (weighted / total).astype(jnp.bfloat16)

    contexts = []
    upcoming = projections(0)
    for g in range(groups):
        current, upcoming = upcoming, projections(g + 1) if g + 1 < groups else None
        blocks = [
            attended(*(part[start : start + length] for part in current)) for start in range(0, positions, length)
        ]
        contexts.append(blocks[0] if len(blocks) == 1 else jnp.concatenate(blocks, axis=0))
    context = jnp.concatenate(contexts, axis=1)
    return (values + jnp.dot(context, out_ref[...], preferred_element_type=jnp.float32)).astype(jnp.bfloat16)


def moved(one_hot, rows):
    return jnp.dot(one_hot.astype(jnp.bfloat16), rows, preferred_element_type=jnp.float32).astype(jnp.bfloat16)


def spread_matrix(owner_row, lines_dev, peers, chunks):
    img_rows = owner_row.shape[1]
    strides = peers * chunks
    rows = img_rows // strides
    square = (img_rows, img_rows)
    across = jnp.broadcast_to(owner_row, square).astype(jnp.float32)
    down = across.T
    before = (down < across) | ((down == across) & (iota(square, 0) < iota(square, 1)))
    rank = jnp.sum(before.astype(jnp.float32), axis=0, keepdims=True).astype(jnp.int32)
    shape = (lines_dev * img_rows, img_rows)
    place = iota(shape, 0)
    i = lax.rem(place, rows)
    line = lax.rem(lax.div(place, rows), lines_dev)
    chunk = lax.rem(lax.div(place, rows * lines_dev), chunks)
    peer = lax.div(place, rows * lines_dev * chunks)
    hit = (i * strides + chunk * peers + peer) == rank
    return jnp.concatenate(
        [jnp.where(hit & (line == own), 1.0, 0.0) for own in range(lines_dev)], axis=1
    )


def column_kernel(lines_dev, peers, chunks, order_ref, frames_ref, owner_ref, gain_ref, qkv_ref, out_ref, y_ref):
    x = frames_ref[order_ref[0]]
    y = layer(x, (gain_ref, qkv_ref, out_ref), x.shape[0] // lines_dev, None)
    y_ref[...] = moved(spread_matrix(owner_ref[...], lines_dev, peers, chunks), y)


def row_bias(section, length, rows, columns):
    query, key = iota((length, length), 0), iota((length, length), 1)
    same_row = lax.rem(query, rows) == lax.rem(key, rows)
    query_line, key_line = lax.div(query, rows), lax.div(key, rows)
    query_col, key_col = lax.rem(query_line, columns), lax.rem(key_line, columns)
    across_frames = query_col == key_col
    across_columns = (lax.div(query_line, columns) == lax.div(key_line, columns)) & (key_col <= query_col)
    first = jnp.broadcast_to(section == 1, (length, length))
    allowed = same_row & ((first & across_frames) | (~first & across_columns))
    return jnp.where(allowed, 0.0, -1e30)


def pack_matrix(owner_row, residue, lines, rows, strides, most, peers):
    img_rows = owner_row.shape[1]
    shape = (peers * most * lines, img_rows)
    place = iota(shape, 0)
    line = lax.rem(place, lines)
    n = lax.rem(lax.div(place, lines), most)
    peer = lax.div(place, lines * most)
    owners = jnp.broadcast_to(owner_row, shape)
    start = jnp.sum((owners < peer).astype(jnp.float32), axis=1, keepdims=True).astype(jnp.int32)
    end = jnp.sum((owners <= peer).astype(jnp.float32), axis=1, keepdims=True).astype(jnp.int32)
    rank = start + lax.rem(residue - start + img_rows, strides) + strides * n
    here = iota(shape, 1)
    hit = (lax.div(rank, strides) == lax.rem(here, rows)) & (line == lax.div(here, rows)) & (rank < end)
    return jnp.where(hit, 1.0, 0.0)


def tick_kernel(dims, chunk, flag_ref, x_ref, f_ref, owner_ref, gain_ref, qkv_ref, out_ref, y_ref):
    rows, columns, lines, strides, most, peers = dims
    length = x_ref.shape[0]
    section, me, mode = flag_ref[0], flag_ref[1], flag_ref[2]

    def give(value):
        if chunk is not None:
            value = moved(
                pack_matrix(owner_ref[...], chunk * peers + me, lines, rows, strides, most, peers), value
            )
        y_ref[...] = value

    @pl.when(mode == 0)
    def _():
        give(layer(x_ref[...], (gain_ref, qkv_ref, out_ref), length, row_bias(section, length, rows, columns)))

    @pl.when(mode == 1)
    def _():
        give(f_ref[...])

    @pl.when(mode == 2)
    def _():
        give(x_ref[...])


def cost(positions, features):
    return pl.CostEstimate(
        flops=10 * positions * features * features,
        bytes_accessed=8 * features * features + 8 * positions * features,
        transcendentals=HEADS * positions * positions,
    )


def in_vmem(arrays):
    return [pltpu.with_memory_space_constraint(a, pltpu.VMEM) for a in arrays]


def load_kernel(*refs):
    count = len(refs) // 3
    copies = [
        pltpu.make_async_copy(refs[i], refs[count + i], refs[2 * count + i]) for i in range(count)
    ]
    for copy in copies:
        copy.start()
    for copy in copies:
        copy.wait()


def loaded(arrays):
    return pl.pallas_call(
        load_kernel,
        out_shape=[pltpu.VMEM(a.shape, a.dtype) for a in arrays],
        in_specs=[pl.BlockSpec(memory_space=pltpu.HBM) for _ in arrays],
        out_specs=[IN_VMEM for _ in arrays],
        scratch_shapes=[pltpu.SemaphoreType.DMA for _ in arrays],
        compiler_params=pltpu.CompilerParams(vmem_limit_bytes=1024 * 1024),
        name="loaded",
    )(*arrays)


def column_pass(turn, frames, owner_row, weights, lines_dev, peers):
    _, positions, features = frames.shape
    return pl.pallas_call(
        functools.partial(column_kernel, lines_dev, peers, lines_dev),
        out_shape=jax.ShapeDtypeStruct((positions, features), jnp.bfloat16),
        in_specs=[IN_SMEM] + [IN_VMEM] * 5,
        out_specs=IN_VMEM,
        compiler_params=pltpu.CompilerParams(vmem_limit_bytes=VMEM_BYTES),
        cost_estimate=cost(positions, features),
        name="column_pass",
    )(turn, *in_vmem([frames]), owner_row, *in_vmem(weights))


def tick_pass(flags, x, f, owner_row, weights, dims, chunk=None):
    positions, features = x.shape
    _, _, lines, _, most, peers = dims
    out_rows = positions if chunk is None else peers * most * lines
    return pl.pallas_call(
        functools.partial(tick_kernel, dims, chunk),
        out_shape=jax.ShapeDtypeStruct((out_rows, features), jnp.bfloat16),
        in_specs=[IN_SMEM] + [IN_VMEM] * 6,
        out_specs=IN_VMEM,
        compiler_params=pltpu.CompilerParams(vmem_limit_bytes=VMEM_BYTES),
        cost_estimate=cost(positions, features),
        name="tick_pass",
    )(flags, x, f, owner_row, *in_vmem(weights))


def settle_kernel(dims, max_rows, flag_ref, owner_ref, *refs):
    rows, columns, lines, strides, most, peers = dims
    *parts, out_ref = refs
    me = flag_ref[1]
    owners = owner_ref[...]
    total = None
    for chunk, part_ref in enumerate(parts):
        shape = (lines * max_rows, peers * most * lines)
        slot_place, part_place = iota(shape, 0), iota(shape, 1)
        start = jnp.sum((owners < me).astype(jnp.float32), axis=1, keepdims=True).astype(jnp.int32)
        residue = chunk * peers + lax.div(part_place, lines * most)
        slot = lax.rem(residue - start + strides * peers * max_rows, strides) + strides * lax.rem(
            lax.div(part_place, lines), most
        )
        hit = (slot == lax.rem(slot_place, max_rows)) & (lax.rem(part_place, lines) == lax.div(slot_place, max_rows))
        term = jnp.dot(
            jnp.where(hit, 1.0, 0.0).astype(jnp.bfloat16), part_ref[...], preferred_element_type=jnp.float32
        )
        total = term if total is None else total + term
    out_ref[...] = total.astype(jnp.bfloat16)


def settle(flags, owner_row, parts, dims, max_rows):
    rows, features = dims[2] * max_rows, parts[0].shape[1]
    depth = sum(p.shape[0] for p in parts)
    return pl.pallas_call(
        functools.partial(settle_kernel, dims, max_rows),
        out_shape=jax.ShapeDtypeStruct((rows, features), jnp.bfloat16),
        in_specs=[IN_SMEM] + [IN_VMEM] * (1 + len(parts)),
        out_specs=IN_VMEM,
        compiler_params=pltpu.CompilerParams(vmem_limit_bytes=VMEM_BYTES),
        cost_estimate=pl.CostEstimate(
            flops=2 * rows * depth * features, bytes_accessed=2 * (rows + depth) * features, transcendentals=0
        ),
        name="settle",
    )(flags, owner_row, *parts)


def swapped(x, peers):
    parts = x.reshape(peers, -1, x.shape[-1])
    return lax.all_to_all(parts, "seq", split_axis=0, concat_axis=0, tiled=True)


def local(frames_in, order, owner, qkv_weight, out_weight, gains):
    sections = lax.axis_size("section")
    peers = lax.axis_size("seq")
    section = lax.axis_index("section")
    me = lax.axis_index("seq")
    clips, lines_dev, img_rows, features = frames_in.shape
    lines = lines_dev * peers
    columns = lines // FRAMES
    max_rows = 2 * img_rows // peers
    chunks = lines_dev
    strides = peers * chunks
    rows = img_rows // strides
    most = -(-max_rows // strides)
    dims = (rows, columns, lines, strides, most, peers)
    owner_row = owner.reshape(1, img_rows)
    *weights, frames = loaded(
        [gains, qkv_weight[0], out_weight[0], frames_in.reshape(clips, lines_dev * img_rows, features)]
    )

    homes = [1, 0, 2, 3]
    fresh = []
    for clip in range(clips):
        turn = order[sections - 1 - homes[clip]].reshape(1)
        mixed = column_pass(turn, frames, owner_row, weights, lines_dev, peers)
        received = swapped(mixed, peers).reshape(peers, chunks, lines_dev * rows, features)
        fresh.append([received[:, chunk].reshape(img_rows, features) for chunk in range(chunks)])

    ticks = clips + sections - 2
    send = list(fresh[0])
    held = [None] * chunks
    for tick in range(ticks):
        pairs = []
        if tick <= clips:
            pairs.append((0, 1))
        if 1 <= tick <= clips:
            pairs.append((1, 2))
        if 2 <= tick <= clips + 1:
            pairs.append((2, 3))
        if tick in (3, 4):
            pairs.append((3, 0))
        if tick == 5:
            pairs.append((3, 2))
        final = tick == ticks - 1
        for chunk in range(chunks):
            x = lax.ppermute(send[chunk], "section", pairs)
            if final:
                mode = jnp.where(section < 2, 1, jnp.where(section == 2, 2, 0))
                f = held[chunk]
            elif tick + 1 < clips:
                mode = jnp.where(section == 0, 1, 0)
                f = fresh[tick + 1][chunk]
            else:
                mode = jnp.where(section == 0, 2, 0)
                f = x
            flags = jnp.stack([section, me, mode]).astype(jnp.int32)
            send[chunk] = tick_pass(flags, x, f, owner_row, weights, dims, chunk if final else None)
            held[chunk] = x

    arrived = [swapped(part, peers).reshape(-1, features) for part in send]
    return settle(flags, owner_row, arrived, dims, max_rows).reshape(1, lines, max_rows, features)


def solution(mesh):
    placed = (
        P(None, "seq", None, None),
        P(),
        P(),
        P("section", None, None),
        P("section", None, None),
        P("section", None),
    )
    return jax.shard_map(
        local,
        mesh=mesh,
        in_specs=placed,
        out_specs=P("section", None, "seq", None),
        check_vma=False,
    )
```

```python
import functools

import jax
import jax.numpy as jnp
from jax import lax
from jax.experimental import pallas as pl
from jax.experimental.pallas import tpu as pltpu
from jax.sharding import PartitionSpec as P

HEADS = 16
FRAMES = 4
GROUP = 4
CORES = 2
LOG2_E = 1.4426950408889634
VMEM_BYTES = 32 * 1024 * 1024
IN_VMEM = pl.BlockSpec(memory_space=pltpu.VMEM)
IN_SMEM = pl.BlockSpec(memory_space=pltpu.SMEM)
ANYWHERE = pl.BlockSpec(memory_space=pl.ANY)


def iota(shape, dim):
    return lax.broadcasted_iota(jnp.int32, shape, dim)


def scaled_norm(values, gain_row):
    mean_square = jnp.mean(values * values, axis=-1, keepdims=True)
    return (values * lax.rsqrt(mean_square + 1e-06) * gain_row).astype(jnp.bfloat16)


def layer(x, weights, length, bias):
    gain_ref, qkv_ref, out_ref = weights
    positions, features = x.shape
    head_size = features // HEADS
    width = GROUP * head_size
    groups = features // width
    values = x.astype(jnp.float32)
    normed = scaled_norm(values, gain_ref[...])
    own_lanes = [(lax.div(iota((1, width), 1), head_size) == h).astype(jnp.bfloat16) for h in range(GROUP)]
    ones = jnp.concatenate([jnp.broadcast_to(lanes, (length, width)) for lanes in own_lanes], axis=0)
    scale = head_size ** (-0.5) * LOG2_E

    def per_head(part):
        return jnp.concatenate([part * lanes for lanes in own_lanes], axis=0)

    def projections(g):
        return [
            jnp.dot(
                normed,
                qkv_ref[:, part * features + g * width : part * features + (g + 1) * width],
                preferred_element_type=jnp.float32,
            ).astype(jnp.bfloat16)
            for part in range(3)
        ]

    def attended(queries, key_rows, value_rows):
        scores = lax.dot_general(
            queries, per_head(key_rows), (((1,), (1,)), ((), ())), preferred_element_type=jnp.float32
        ) * scale
        grown = []
        for h in range(GROUP):
            own = scores[:, h * length : (h + 1) * length]
            if bias is not None:
                own = own + bias
            grown.append(jnp.exp2(own - jnp.max(own, axis=-1, keepdims=True)).astype(jnp.bfloat16))
        grown = jnp.concatenate(grown, axis=1)
        weighted = jnp.dot(grown, per_head(value_rows), preferred_element_type=jnp.float32)
        total = jnp.dot(grown, ones, preferred_element_type=jnp.float32)
        share = pl.reciprocal(total, approx=True)
        share = share * (2.0 - total * share)
        return (weighted * share).astype(jnp.bfloat16)

    contexts = []
    upcoming = projections(0)
    for g in range(groups):
        current, upcoming = upcoming, projections(g + 1) if g + 1 < groups else None
        blocks = [
            attended(*(part[start : start + length] for part in current)) for start in range(0, positions, length)
        ]
        contexts.append(blocks[0] if len(blocks) == 1 else jnp.concatenate(blocks, axis=0))
    context = jnp.concatenate(contexts, axis=1)
    return (values + jnp.dot(context, out_ref[...], preferred_element_type=jnp.float32)).astype(jnp.bfloat16)


def moved(hit, rows):
    one_hot = jnp.where(hit, 1.0, 0.0).astype(jnp.bfloat16)
    return jnp.dot(one_hot, rows, preferred_element_type=jnp.float32).astype(jnp.bfloat16)


def digits(place, *sizes):
    found = []
    for size in reversed(sizes):
        found.append(lax.rem(place, size))
        place = lax.div(place, size)
    return [place] + found[::-1]


def ranks(owner_row):
    img_rows = owner_row.shape[1]
    square = (img_rows, img_rows)
    across = jnp.broadcast_to(owner_row, square).astype(jnp.float32)
    down = across.T
    before = (down < across) | ((down == across) & (iota(square, 0) < iota(square, 1)))
    return jnp.sum(before.astype(jnp.float32), axis=0, keepdims=True).astype(jnp.int32)


def spread_rows(y, rank, my_core, dims):
    rows, _, _, strides, _, peers = dims
    chunks = strides // peers
    positions, img_rows = y.shape[0], rank.shape[1]
    lines_dev = positions // img_rows
    shape = (positions, img_rows)
    core, group, chunk, line, i = digits(iota(shape, 0), peers // CORES, chunks, lines_dev, rows)
    core = lax.rem(core + my_core, CORES)
    hit = (i * strides + chunk * peers + group * CORES + core) == rank
    return moved(jnp.concatenate([hit & (line == own) for own in range(lines_dev)], axis=1), y)


def column_kernel(dims, turn_place, flag_ref, order_ref, frames_ref, owner_ref, gain_ref, qkv_ref, out_ref, *rest):
    mine_ref, other_ref = rest[-2:]

    @pl.when(flag_ref[0] == 0)
    def _():
        x = frames_ref[order_ref[turn_place]]
        y = layer(x, (gain_ref, qkv_ref, out_ref), owner_ref.shape[1], None)
        y = spread_rows(y, ranks(owner_ref[...]), lax.rem(flag_ref[1], CORES), dims)
        mine_ref[...] = y[: y.shape[0] // CORES]
        other_ref[...] = y[y.shape[0] // CORES :]


def merge_kernel(dims, flag_ref, mine_ref, other_ref, *part_refs):
    rows, _, lines, strides, _, peers = dims
    chunks = strides // peers
    lines_dev = lines // peers

    @pl.when(flag_ref[0] == 0)
    def _():
        both = jnp.concatenate([mine_ref[...], other_ref[...]], axis=0)
        shape = (both.shape[0], both.shape[0])
        my_core, my_group = lax.rem(flag_ref[1], CORES), lax.div(flag_ref[1], CORES)
        apart, chunk, core, inner = digits(iota(shape, 0), chunks, CORES, lines_dev * rows)
        far, from_group, from_chunk, from_inner = digits(
            iota(shape, 1), peers // CORES, chunks, lines_dev * rows
        )
        from_core = lax.rem(far + my_core, CORES)
        hit = (
            ((apart ^ my_group) == from_group)
            & (chunk == from_chunk)
            & (core == from_core)
            & (inner == from_inner)
        )
        sent = moved(hit, both)
        size = sent.shape[0] // len(part_refs)
        for d, part_ref in enumerate(part_refs):
            part_ref[...] = sent[d * size : (d + 1) * size]


def gathered_chunk(part_refs, chunk, me, dims):
    rows, _, lines, strides, _, peers = dims
    chunks = strides // peers
    parts = jnp.concatenate([ref[...] for ref in part_refs], axis=0)
    shape = (lines * rows, parts.shape[0])
    inner_size = lines // (peers // CORES) * rows
    group, inner = digits(iota(shape, 0), inner_size)
    apart, from_chunk, from_inner = digits(iota(shape, 1), chunks, inner_size)
    my_group = lax.div(me, CORES)
    return moved(((group ^ my_group) == apart) & (from_chunk == chunk) & (from_inner == inner), parts)


def row_bias(section, length, rows, columns):
    query, key = iota((length, length), 0), iota((length, length), 1)
    same_row = lax.rem(query, rows) == lax.rem(key, rows)
    query_line, key_line = lax.div(query, rows), lax.div(key, rows)
    query_col, key_col = lax.rem(query_line, columns), lax.rem(key_line, columns)
    across_frames = query_col == key_col
    across_columns = (lax.div(query_line, columns) == lax.div(key_line, columns)) & (key_col <= query_col)
    first = jnp.broadcast_to(section == 1, (length, length))
    allowed = same_row & ((first & across_frames) | (~first & across_columns))
    return jnp.where(allowed, 0.0, -1e30)


def packed_rows(y, owner_row, residue, dims):
    rows, _, lines, strides, most, peers = dims
    img_rows = owner_row.shape[1]
    shape = (peers * most * lines, img_rows)
    peer, n, line = digits(iota(shape, 0), most, lines)
    owners = jnp.broadcast_to(owner_row, shape)
    start = jnp.sum((owners < peer).astype(jnp.float32), axis=1, keepdims=True).astype(jnp.int32)
    end = jnp.sum((owners <= peer).astype(jnp.float32), axis=1, keepdims=True).astype(jnp.int32)
    rank = start + lax.rem(residue - start + img_rows, strides) + strides * n
    from_line, i = digits(iota(shape, 1), rows)
    return moved((lax.div(rank, strides) == i) & (line == from_line) & (rank < end), y)


def tick_kernel(dims, chunk, given, first, final, flag_ref, x_ref, owner_ref, gain_ref, qkv_ref, out_ref, *rest):
    rows, columns, lines, strides, most, peers = dims
    y_ref, given_refs = rest[-1], rest[:given]
    section, me = flag_ref[0], flag_ref[1]

    def worked():
        weights = (gain_ref, qkv_ref, out_ref)
        return layer(x_ref[...], weights, x_ref.shape[0], row_bias(section, x_ref.shape[0], rows, columns))

    def packed(value):
        return packed_rows(value, owner_ref[...], chunk * peers + me, dims)

    if final:
        @pl.when(section > first)
        def _():
            y_ref[...] = packed(worked())

        @pl.when(section == first)
        def _():
            y_ref[...] = packed(x_ref[...])

        @pl.when(section < first)
        def _():
            y_ref[...] = packed(given_refs[0][...])

        return

    @pl.when(section > 0)
    def _():
        y_ref[...] = worked()

    @pl.when(section == 0)
    def _():
        y_ref[...] = gathered_chunk(given_refs, chunk, me, dims) if given else x_ref[...]


def cost(positions, features):
    return pl.CostEstimate(
        flops=10 * positions * features * features,
        bytes_accessed=8 * features * features + 8 * positions * features,
        transcendentals=HEADS * positions * positions,
    )


def in_vmem(arrays):
    return [pltpu.with_memory_space_constraint(a, pltpu.VMEM) for a in arrays]


def load_kernel(*refs):
    count = len(refs) // 3
    copies = [
        pltpu.make_async_copy(refs[i], refs[count + i], refs[2 * count + i]) for i in range(count)
    ]
    for copy in copies:
        copy.start()
    for copy in copies:
        copy.wait()


def loaded(arrays):
    return pl.pallas_call(
        load_kernel,
        out_shape=[pltpu.VMEM(a.shape, a.dtype) for a in arrays],
        in_specs=[pl.BlockSpec(memory_space=pltpu.HBM) for _ in arrays],
        out_specs=[IN_VMEM for _ in arrays],
        scratch_shapes=[pltpu.SemaphoreType.DMA for _ in arrays],
        compiler_params=pltpu.CompilerParams(vmem_limit_bytes=1024 * 1024),
        name="loaded",
    )(*(pltpu.with_memory_space_constraint(a, pltpu.HBM) for a in arrays))


def options():
    return pltpu.CompilerParams(vmem_limit_bytes=VMEM_BYTES)


def column_pass(place, order, frames, owner_row, weights, dims, turn_place, after):
    _, positions, features = frames.shape
    half = jax.ShapeDtypeStruct((positions // CORES, features), jnp.bfloat16)
    return pl.pallas_call(
        functools.partial(column_kernel, dims, turn_place),
        out_shape=[half, half],
        in_specs=[IN_SMEM] * 2 + [IN_VMEM] * 5 + [ANYWHERE] * len(after),
        out_specs=[IN_VMEM] * 2,
        compiler_params=options(),
        cost_estimate=cost(positions, features),
        name="column_pass",
    )(place, order, *in_vmem([frames]), owner_row, *in_vmem(weights), *after)


def merge(place, mine, other, dims):
    positions, features = mine.shape
    groups = dims[-1] // CORES
    part = jax.ShapeDtypeStruct((CORES * positions // groups, features), jnp.bfloat16)
    return pl.pallas_call(
        functools.partial(merge_kernel, dims),
        out_shape=[part] * groups,
        in_specs=[IN_SMEM] + [IN_VMEM] * 2,
        out_specs=[IN_VMEM] * groups,
        compiler_params=options(),
        cost_estimate=pl.CostEstimate(
            flops=8 * positions * positions * features, bytes_accessed=8 * positions * features, transcendentals=0
        ),
        name="merge",
    )(place, mine, other)


def gather_kernel(dims, count, flag_ref, *refs):
    @pl.when(flag_ref[0] == 0)
    def _():
        for chunk, out_ref in enumerate(refs[count:]):
            out_ref[...] = gathered_chunk(refs[:count], chunk, flag_ref[1], dims)


def gather(place, parts, dims, chunks):
    positions, features = dims[0] * dims[2], parts[0].shape[1]
    return pl.pallas_call(
        functools.partial(gather_kernel, dims, len(parts)),
        out_shape=[jax.ShapeDtypeStruct((positions, features), jnp.bfloat16)] * chunks,
        in_specs=[IN_SMEM] + [IN_VMEM] * len(parts),
        out_specs=[IN_VMEM] * chunks,
        compiler_params=options(),
        cost_estimate=pl.CostEstimate(
            flops=8 * positions * positions * features, bytes_accessed=8 * positions * features, transcendentals=0
        ),
        name="gather",
    )(place, *parts)


def tick_pass(place, x, given, owner_row, weights, dims, chunk, first, final, after):
    positions, features = x.shape
    _, _, lines, _, most, peers = dims
    out_rows = peers * most * lines if final else positions
    return pl.pallas_call(
        functools.partial(tick_kernel, dims, chunk, len(given), first, final),
        out_shape=jax.ShapeDtypeStruct((out_rows, features), jnp.bfloat16),
        in_specs=[IN_SMEM] + [IN_VMEM] * (5 + len(given)) + [ANYWHERE] * len(after),
        out_specs=IN_VMEM,
        compiler_params=options(),
        cost_estimate=cost(positions, features),
        name="tick_pass",
    )(place, x, owner_row, *in_vmem(weights), *given, *after)


def settle_kernel(dims, max_rows, flag_ref, owner_ref, *refs):
    rows, columns, lines, strides, most, peers = dims
    *parts, out_ref = refs
    me = flag_ref[1]
    owners = owner_ref[...]
    total = None
    for chunk, part_ref in enumerate(parts):
        shape = (lines * max_rows, peers * most * lines)
        slot_place, part_place = iota(shape, 0), iota(shape, 1)
        start = jnp.sum((owners < me).astype(jnp.float32), axis=1, keepdims=True).astype(jnp.int32)
        residue = chunk * peers + lax.div(part_place, lines * most)
        slot = lax.rem(residue - start + strides * peers * max_rows, strides) + strides * lax.rem(
            lax.div(part_place, lines), most
        )
        hit = (slot == lax.rem(slot_place, max_rows)) & (lax.rem(part_place, lines) == lax.div(slot_place, max_rows))
        term = jnp.dot(
            jnp.where(hit, 1.0, 0.0).astype(jnp.bfloat16), part_ref[...], preferred_element_type=jnp.float32
        )
        total = term if total is None else total + term
    out_ref[...] = total.astype(jnp.bfloat16)


def settle(flags, owner_row, parts, dims, max_rows):
    rows, features = dims[2] * max_rows, parts[0].shape[1]
    depth = sum(p.shape[0] for p in parts)
    return pl.pallas_call(
        functools.partial(settle_kernel, dims, max_rows),
        out_shape=jax.ShapeDtypeStruct((rows, features), jnp.bfloat16),
        in_specs=[IN_SMEM] + [IN_VMEM] * (1 + len(parts)),
        out_specs=IN_VMEM,
        compiler_params=pltpu.CompilerParams(vmem_limit_bytes=VMEM_BYTES),
        cost_estimate=pl.CostEstimate(
            flops=2 * rows * depth * features, bytes_accessed=2 * (rows + depth) * features, transcendentals=0
        ),
        name="settle",
    )(flags, owner_row, *parts)


def swapped(x, peers):
    parts = x.reshape(peers, -1, x.shape[-1])
    return lax.all_to_all(parts, "seq", split_axis=0, concat_axis=0, tiled=True)


def local(frames_in, order, owner, qkv_weight, out_weight, gains):
    sections = lax.axis_size("section")
    peers = lax.axis_size("seq")
    section = lax.axis_index("section")
    me = lax.axis_index("seq")
    clips, lines_dev, img_rows, features = frames_in.shape
    lines = lines_dev * peers
    columns = lines // FRAMES
    max_rows = 2 * img_rows // peers
    chunks = lines_dev
    strides = peers * chunks
    rows = img_rows // strides
    most = -(-max_rows // strides)
    dims = (rows, columns, lines, strides, most, peers)
    owner_row = owner.reshape(1, img_rows)
    *weights, frames = loaded(
        [gains, qkv_weight[0], out_weight[0], frames_in.reshape(clips, lines_dev * img_rows, features)]
    )
    place = jnp.stack([section, me]).astype(jnp.int32)
    groups = peers // CORES

    def column_clip(clip, after):
        mine, other = column_pass(
            place, order, frames, owner_row, weights, dims, sections - 1 - homes[clip], after
        )
        other = lax.ppermute(other, ("section", "seq"), [(p, p ^ 1) for p in range(peers)])
        parts = list(merge(place, mine, other, dims))
        return parts[:1] + [
            lax.ppermute(
                parts[d],
                ("section", "seq"),
                [(p, (p // CORES ^ d) * CORES + p % CORES) for p in range(peers)],
            )
            for d in range(1, groups)
        ]

    homes = [1, 0, 2, 3]
    fresh = [column_clip(0, [])]
    fresh.append(column_clip(1, [fresh[0][0]]))
    ticks = clips + sections - 2
    send = list(gather(place, fresh[0], dims, chunks))
    held = [None] * chunks
    for tick in range(ticks):
        pairs = []
        if tick <= clips:
            pairs.append((0, 1))
        if 1 <= tick <= clips:
            pairs.append((1, 2))
        if 2 <= tick <= clips + 1:
            pairs.append((2, 3))
        if tick in (3, 4):
            pairs.append((3, 0))
        if tick == 5:
            pairs.append((3, 2))
        final = tick == ticks - 1
        if tick + 2 < clips:
            fresh.append(column_clip(tick + 2, [send[-1]]))
        for chunk in range(chunks):
            x = lax.ppermute(send[chunk], "section", pairs)
            if final:
                given = [held[chunk]]
            elif tick + 1 < clips:
                given = fresh[tick + 1]
            else:
                given = []
            send[chunk] = tick_pass(
                place, x, given, owner_row, weights, dims, chunk, 2, final, [send[chunk - 1]]
            )
            held[chunk] = x

    arrived = [swapped(part, peers).reshape(-1, features) for part in send]
    return settle(place, owner_row, arrived, dims, max_rows).reshape(1, lines, max_rows, features)


def solution(mesh):
    placed = (
        P(None, "seq", None, None),
        P(),
        P(),
        P("section", None, None),
        P("section", None, None),
        P("section", None),
    )
    return jax.shard_map(
        local,
        mesh=mesh,
        in_specs=placed,
        out_specs=P("section", None, "seq", None),
        check_vma=False,
    )
```

```python
import functools

import jax
import jax.numpy as jnp
from jax import lax
from jax.experimental import pallas as pl
from jax.experimental.pallas import tpu as pltpu
from jax.sharding import PartitionSpec as P

HEADS = 16
FRAMES = 4
GROUP = 4
CORES = 2
LOG2_E = 1.4426950408889634
VMEM_BYTES = 32 * 1024 * 1024
IN_VMEM = pl.BlockSpec(memory_space=pltpu.VMEM)
IN_SMEM = pl.BlockSpec(memory_space=pltpu.SMEM)
ANYWHERE = pl.BlockSpec(memory_space=pl.ANY)


def iota(shape, dim):
    return lax.broadcasted_iota(jnp.int32, shape, dim)


def scaled_norm(values, gain_row):
    mean_square = jnp.mean(values * values, axis=-1, keepdims=True)
    return (values * lax.rsqrt(mean_square + 1e-06) * gain_row).astype(jnp.bfloat16)


def layer(x, weights, length, bias):
    gain_ref, qkv_ref, out_ref = weights
    positions, features = x.shape
    head_size = features // HEADS
    width = GROUP * head_size
    groups = features // width
    values = x.astype(jnp.float32)
    normed = scaled_norm(values, gain_ref[...])
    own_lanes = [(lax.div(iota((1, width), 1), head_size) == h).astype(jnp.bfloat16) for h in range(GROUP)]
    ones = jnp.concatenate([jnp.broadcast_to(lanes, (length, width)) for lanes in own_lanes], axis=0)
    scale = head_size ** (-0.5) * LOG2_E

    def per_head(part):
        return jnp.concatenate([part * lanes for lanes in own_lanes], axis=0)

    def projections(g):
        return [
            jnp.dot(
                normed,
                qkv_ref[:, part * features + g * width : part * features + (g + 1) * width],
                preferred_element_type=jnp.float32,
            ).astype(jnp.bfloat16)
            for part in range(3)
        ]

    def attended(queries, key_rows, value_rows):
        scores = lax.dot_general(
            queries, per_head(key_rows), (((1,), (1,)), ((), ())), preferred_element_type=jnp.float32
        ) * scale
        grown = []
        for h in range(GROUP):
            own = scores[:, h * length : (h + 1) * length]
            if bias is not None:
                own = own + bias
            grown.append(jnp.exp2(own - jnp.max(own, axis=-1, keepdims=True)).astype(jnp.bfloat16))
        grown = jnp.concatenate(grown, axis=1)
        weighted = jnp.dot(grown, per_head(value_rows), preferred_element_type=jnp.float32)
        total = jnp.dot(grown, ones, preferred_element_type=jnp.float32)
        share = pl.reciprocal(total, approx=True)
        share = share * (2.0 - total * share)
        return (weighted * share).astype(jnp.bfloat16)

    contexts = []
    upcoming = projections(0)
    for g in range(groups):
        current, upcoming = upcoming, projections(g + 1) if g + 1 < groups else None
        blocks = [
            attended(*(part[start : start + length] for part in current)) for start in range(0, positions, length)
        ]
        contexts.append(blocks[0] if len(blocks) == 1 else jnp.concatenate(blocks, axis=0))
    context = jnp.concatenate(contexts, axis=1)
    return (values + jnp.dot(context, out_ref[...], preferred_element_type=jnp.float32)).astype(jnp.bfloat16)


def moved(hit, rows):
    one_hot = jnp.where(hit, 1.0, 0.0).astype(jnp.bfloat16)
    return jnp.dot(one_hot, rows, preferred_element_type=jnp.float32).astype(jnp.bfloat16)


def digits(place, *sizes):
    found = []
    for size in reversed(sizes):
        found.append(lax.rem(place, size))
        place = lax.div(place, size)
    return [place] + found[::-1]


def ranks(owner_row):
    img_rows = owner_row.shape[1]
    square = (img_rows, img_rows)
    across = jnp.broadcast_to(owner_row, square).astype(jnp.float32)
    down = across.T
    before = (down < across) | ((down == across) & (iota(square, 0) < iota(square, 1)))
    return jnp.sum(before.astype(jnp.float32), axis=0, keepdims=True).astype(jnp.int32)


def spread_rows(y, rank, my_core, dims):
    rows, _, _, strides, _, peers = dims
    chunks = strides // peers
    positions, img_rows = y.shape[0], rank.shape[1]
    lines_dev = positions // img_rows
    shape = (positions, img_rows)
    core, group, chunk, line, i = digits(iota(shape, 0), peers // CORES, chunks, lines_dev, rows)
    core = lax.rem(core + my_core, CORES)
    hit = (i * strides + chunk * peers + group * CORES + core) == rank
    return moved(jnp.concatenate([hit & (line == own) for own in range(lines_dev)], axis=1), y)


def column_kernel(turn_places, flag_ref, order_ref, frames_ref, owner_ref, gain_ref, qkv_ref, out_ref, *rest):
    y_ref = rest[-1]

    @pl.when(flag_ref[0] == 0)
    def _():
        for clip, turn_place in enumerate(turn_places):
            x = frames_ref[order_ref[turn_place]]
            y_ref[clip] = layer(x, (gain_ref, qkv_ref, out_ref), owner_ref.shape[1], None)


def spread_kernel(dims, flag_ref, y_ref, owner_ref, *rest):
    mine_ref, other_ref = rest[-2:]

    @pl.when(flag_ref[0] == 0)
    def _():
        rank = ranks(owner_ref[...])
        for clip in range(y_ref.shape[0]):
            y = spread_rows(y_ref[clip], rank, lax.rem(flag_ref[1], CORES), dims)
            mine_ref[clip] = y[: y.shape[0] // CORES]
            other_ref[clip] = y[y.shape[0] // CORES :]


def merge_kernel(dims, joined, flag_ref, mine_ref, other_ref, *part_refs):
    rows, _, lines, strides, _, peers = dims
    groups, chunks = peers // CORES, strides // peers
    lines_dev = lines // peers

    @pl.when(flag_ref[0] == 0)
    def _():
        size = 2 * mine_ref.shape[1]
        shape = (size, size)
        my_core, my_group = lax.rem(flag_ref[1], CORES), lax.div(flag_ref[1], CORES)
        apart, chunk, core, inner = digits(iota(shape, 0), chunks, CORES, lines_dev * rows)
        far, from_group, from_chunk, from_inner = digits(iota(shape, 1), groups, chunks, lines_dev * rows)
        from_core = lax.rem(far + my_core, CORES)
        hit = (
            ((apart ^ my_group) == from_group)
            & (chunk == from_chunk)
            & (core == from_core)
            & (inner == from_inner)
        )
        size = size // groups
        for clip in range(mine_ref.shape[0]):
            sent = moved(hit, jnp.concatenate([mine_ref[clip], other_ref[clip]], axis=0))
            for d in range(groups):
                part = sent[d * size : (d + 1) * size]
                if joined:
                    part_refs[d][clip * size : (clip + 1) * size, :] = part
                else:
                    part_refs[clip * groups + d][...] = part


def gathered_chunk(part_refs, chunk, chunks, me, dims):
    rows, _, lines, strides, _, peers = dims
    parts = jnp.concatenate([ref[...] for ref in part_refs], axis=0)
    shape = (lines * rows, parts.shape[0])
    inner_size = lines // (peers // CORES) * rows
    group, inner = digits(iota(shape, 0), inner_size)
    apart, from_chunk, from_inner = digits(iota(shape, 1), chunks, inner_size)
    my_group = lax.div(me, CORES)
    return moved(((group ^ my_group) == apart) & (from_chunk == chunk) & (from_inner == inner), parts)


def row_bias(section, length, rows, columns):
    query, key = iota((length, length), 0), iota((length, length), 1)
    same_row = lax.rem(query, rows) == lax.rem(key, rows)
    query_line, key_line = lax.div(query, rows), lax.div(key, rows)
    query_col, key_col = lax.rem(query_line, columns), lax.rem(key_line, columns)
    across_frames = query_col == key_col
    across_columns = (lax.div(query_line, columns) == lax.div(key_line, columns)) & (key_col <= query_col)
    first = jnp.broadcast_to(section == 1, (length, length))
    allowed = same_row & ((first & across_frames) | (~first & across_columns))
    return jnp.where(allowed, 0.0, -1e30)


def packed_rows(y, owner_row, residue, dims):
    rows, _, lines, strides, most, peers = dims
    img_rows = owner_row.shape[1]
    shape = (peers * most * lines, img_rows)
    peer, n, line = digits(iota(shape, 0), most, lines)
    owners = jnp.broadcast_to(owner_row, shape)
    start = jnp.sum((owners < peer).astype(jnp.float32), axis=1, keepdims=True).astype(jnp.int32)
    end = jnp.sum((owners <= peer).astype(jnp.float32), axis=1, keepdims=True).astype(jnp.int32)
    rank = start + lax.rem(residue - start + img_rows, strides) + strides * n
    from_line, i = digits(iota(shape, 1), rows)
    return moved((lax.div(rank, strides) == i) & (line == from_line) & (rank < end), y)


def tick_kernel(dims, chunk, piece, tick, given, final, flag_ref, x_ref, owner_ref, gain_ref, qkv_ref, out_ref, *rest):
    rows, columns, lines, strides, most, peers = dims
    y_ref, given_refs = rest[-1], rest[:given]
    section, me = flag_ref[0], flag_ref[1]

    def worked(x):
        bias = row_bias(section, x.shape[0], rows, columns)
        return layer(x, (gain_ref, qkv_ref, out_ref), x.shape[0], bias)

    def packed(value):
        return packed_rows(value, owner_ref[...], chunk * peers + me, dims)

    if final:

        @pl.when(section > 2)
        def _():
            y_ref[...] = packed(worked(x_ref[...]))

        @pl.when(section == 2)
        def _():
            y_ref[...] = packed(x_ref[...])

        @pl.when(section < 2)
        def _():
            y_ref[...] = packed(given_refs[0][...])

        return

    if given:

        @pl.when(section == 1)
        def _():
            y_ref[...] = worked(gathered_chunk(given_refs, *piece, me, dims))

    if tick:

        @pl.when((section > 1) & (section <= tick + 1))
        def _():
            y_ref[...] = worked(x_ref[...])

        @pl.when(section == 0)
        def _():
            y_ref[...] = x_ref[...]


def cost(positions, features):
    return pl.CostEstimate(flops=positions, bytes_accessed=features, transcendentals=0)


def in_vmem(arrays):
    return [pltpu.with_memory_space_constraint(a, pltpu.VMEM) for a in arrays]


def load_kernel(*refs):
    count = len(refs) // 3
    copies = [
        pltpu.make_async_copy(refs[i], refs[count + i], refs[2 * count + i]) for i in range(count)
    ]
    for copy in copies:
        copy.start()
    for copy in copies:
        copy.wait()


def loaded(arrays):
    return pl.pallas_call(
        load_kernel,
        out_shape=[pltpu.VMEM(a.shape, a.dtype) for a in arrays],
        in_specs=[pl.BlockSpec(memory_space=pltpu.HBM) for _ in arrays],
        out_specs=[IN_VMEM for _ in arrays],
        scratch_shapes=[pltpu.SemaphoreType.DMA for _ in arrays],
        compiler_params=pltpu.CompilerParams(vmem_limit_bytes=1024 * 1024),
        name="loaded",
    )(*(pltpu.with_memory_space_constraint(a, pltpu.HBM) for a in arrays))


def options():
    return pltpu.CompilerParams(vmem_limit_bytes=VMEM_BYTES)


def column_pass(place, order, frames, owner_row, weights, turn_places, after):
    _, positions, features = frames.shape
    return pl.pallas_call(
        functools.partial(column_kernel, turn_places),
        out_shape=jax.ShapeDtypeStruct((len(turn_places), positions, features), jnp.bfloat16),
        in_specs=[IN_SMEM] * 2 + [IN_VMEM] * 5 + [ANYWHERE] * len(after),
        out_specs=IN_VMEM,
        compiler_params=options(),
        cost_estimate=cost(positions, features),
        name="column_pass",
    )(place, order, *in_vmem([frames]), owner_row, *in_vmem(weights), *after)


def spread(place, y, owner_row, dims, after):
    clips, positions, features = y.shape
    half = jax.ShapeDtypeStruct((clips, positions // CORES, features), jnp.bfloat16)
    return pl.pallas_call(
        functools.partial(spread_kernel, dims),
        out_shape=[half, half],
        in_specs=[IN_SMEM] + [IN_VMEM] * 2 + [ANYWHERE] * len(after),
        out_specs=[IN_VMEM] * 2,
        compiler_params=options(),
        cost_estimate=cost(positions, features),
        name="spread",
    )(place, y, owner_row, *after)


def merge(place, mine, other, dims, joined):
    clips, positions, features = mine.shape
    groups = dims[-1] // CORES
    rows = CORES * positions // groups
    part = jax.ShapeDtypeStruct((rows * (clips if joined else 1), features), jnp.bfloat16)
    count = groups * (1 if joined else clips)
    parts = pl.pallas_call(
        functools.partial(merge_kernel, dims, joined),
        out_shape=[part] * count,
        in_specs=[IN_SMEM] + [IN_VMEM] * 2,
        out_specs=[IN_VMEM] * count,
        compiler_params=options(),
        cost_estimate=cost(positions, features),
        name="merge",
    )(place, mine, other)
    return [parts[start : start + groups] for start in range(0, count, groups)]


def tick_pass(place, x, given, owner_row, weights, dims, chunk, piece, tick, final, after):
    rows, _, lines, _, most, peers = dims
    positions, features = rows * lines, x.shape[1]
    out_rows = peers * most * lines if final else positions
    return pl.pallas_call(
        functools.partial(tick_kernel, dims, chunk, piece, tick, len(given), final),
        out_shape=jax.ShapeDtypeStruct((out_rows, features), jnp.bfloat16),
        in_specs=[IN_SMEM] + [IN_VMEM] * (5 + len(given)) + [ANYWHERE] * len(after),
        out_specs=IN_VMEM,
        compiler_params=options(),
        cost_estimate=cost(positions, features),
        name="tick_pass",
    )(place, x, owner_row, *in_vmem(weights), *given, *after)


def settle_kernel(dims, max_rows, flag_ref, owner_ref, *refs):
    rows, columns, lines, strides, most, peers = dims
    *parts, out_ref = refs
    me = flag_ref[1]
    owners = owner_ref[...]
    total = None
    for chunk, part_ref in enumerate(parts):
        shape = (lines * max_rows, peers * most * lines)
        slot_place, part_place = iota(shape, 0), iota(shape, 1)
        start = jnp.sum((owners < me).astype(jnp.float32), axis=1, keepdims=True).astype(jnp.int32)
        residue = chunk * peers + lax.div(part_place, lines * most)
        slot = lax.rem(residue - start + strides * peers * max_rows, strides) + strides * lax.rem(
            lax.div(part_place, lines), most
        )
        hit = (slot == lax.rem(slot_place, max_rows)) & (lax.rem(part_place, lines) == lax.div(slot_place, max_rows))
        term = jnp.dot(
            jnp.where(hit, 1.0, 0.0).astype(jnp.bfloat16), part_ref[...], preferred_element_type=jnp.float32
        )
        total = term if total is None else total + term
    out_ref[...] = total.astype(jnp.bfloat16)


def settle(flags, owner_row, parts, dims, max_rows):
    rows, features = dims[2] * max_rows, parts[0].shape[1]
    depth = sum(p.shape[0] for p in parts)
    return pl.pallas_call(
        functools.partial(settle_kernel, dims, max_rows),
        out_shape=jax.ShapeDtypeStruct((rows, features), jnp.bfloat16),
        in_specs=[IN_SMEM] + [IN_VMEM] * (1 + len(parts)),
        out_specs=IN_VMEM,
        compiler_params=pltpu.CompilerParams(vmem_limit_bytes=VMEM_BYTES),
        cost_estimate=pl.CostEstimate(
            flops=2 * rows * depth * features, bytes_accessed=2 * (rows + depth) * features, transcendentals=0
        ),
        name="settle",
    )(flags, owner_row, *parts)


def swapped(x, peers):
    parts = x.reshape(peers, -1, x.shape[-1])
    return lax.all_to_all(parts, "seq", split_axis=0, concat_axis=0, tiled=True)


def local(frames_in, order, owner, qkv_weight, out_weight, gains):
    sections = lax.axis_size("section")
    peers = lax.axis_size("seq")
    section = lax.axis_index("section")
    me = lax.axis_index("seq")
    clips, lines_dev, img_rows, features = frames_in.shape
    lines = lines_dev * peers
    columns = lines // FRAMES
    max_rows = 2 * img_rows // peers
    chunks = lines_dev
    strides = peers * chunks
    rows = img_rows // strides
    most = -(-max_rows // strides)
    dims = (rows, columns, lines, strides, most, peers)
    owner_row = owner.reshape(1, img_rows)
    *weights, frames = loaded(
        [gains, qkv_weight[0], out_weight[0], frames_in.reshape(clips, lines_dev * img_rows, features)]
    )
    place = jnp.stack([section, me]).astype(jnp.int32)
    groups = peers // CORES

    homes = [1, 0, 2, 3]

    def column_clips(first, last, joined, after, arrived):
        turn_places = [sections - 1 - home for home in homes[first:last]]
        y = column_pass(place, order, frames, owner_row, weights, turn_places, after)
        mine, other = spread(place, y, owner_row, dims, arrived)
        other = lax.ppermute(other, ("section", "seq"), [(p, p ^ 1) for p in range(peers)])
        sets = merge(place, mine, other, dims, joined)
        pieces = [
            [
                lax.ppermute(
                    part,
                    ("section", "seq"),
                    [(p, peers + (p // CORES ^ d) * CORES + p % CORES) for p in range(peers)],
                )
                for d, part in enumerate(parts)
            ]
            for parts in sets
        ]
        return pieces, [sets[0][0]]

    early = clips // 2
    (joint,), after = column_clips(0, early, True, [], [])
    later, after = column_clips(early, clips, False, after, joint)
    fresh = [joint] * early + later
    ticks = clips + sections - 2
    send, held = [None] * chunks, [None] * chunks
    for tick in range(ticks):
        pairs = []
        if tick == clips:
            pairs.append((0, 1))
        if 1 <= tick <= clips:
            pairs.append((1, 2))
        if 2 <= tick <= clips + 1:
            pairs.append((2, 3))
        if tick in (3, 4):
            pairs.append((3, 0))
        if tick == 5:
            pairs.append((3, 2))
        final = tick == ticks - 1
        for chunk in range(chunks):
            x = lax.ppermute(send[chunk], "section", pairs) if tick else joint[0]
            given = [held[chunk]] if final else fresh[tick] if tick < clips else []
            if chunk == 1 and 1 <= tick < clips - 1:
                after = after + fresh[tick + 1]
            piece = (tick * chunks + chunk, early * chunks) if tick < early else (chunk, chunks)
            send[chunk] = tick_pass(
                place, x, given, owner_row, weights, dims, chunk, piece, tick, final, after
            )
            after = [send[chunk]]
            held[chunk] = x

    arrived = [swapped(part, peers).reshape(-1, features) for part in send]
    return settle(place, owner_row, arrived, dims, max_rows).reshape(1, lines, max_rows, features)


def solution(mesh):
    placed = (
        P(None, "seq", None, None),
        P(),
        P(),
        P("section", None, None),
        P("section", None, None),
        P("section", None),
    )
    return jax.shard_map(
        local,
        mesh=mesh,
        in_specs=placed,
        out_specs=P("section", None, "seq", None),
        check_vma=False,
    )
```

```python
import functools

import jax
import jax.numpy as jnp
from jax import lax
from jax.experimental import pallas as pl
from jax.experimental.pallas import tpu as pltpu
from jax.sharding import PartitionSpec as P

HEADS = 16
FRAMES = 4
GROUP = 4
CORES = 2
LOG2_E = 1.4426950408889634
VMEM_BYTES = 32 * 1024 * 1024
IN_VMEM = pl.BlockSpec(memory_space=pltpu.VMEM)
IN_SMEM = pl.BlockSpec(memory_space=pltpu.SMEM)
ANYWHERE = pl.BlockSpec(memory_space=pl.ANY)


def iota(shape, dim):
    return lax.broadcasted_iota(jnp.int32, shape, dim)


def scaled_norm(values, gain_row):
    mean_square = jnp.mean(values * values, axis=-1, keepdims=True)
    return (values * lax.rsqrt(mean_square + 1e-06) * gain_row).astype(jnp.bfloat16)


def layer(x, weights, length, bias):
    gain_ref, qkv_ref, out_ref = weights
    positions, features = x.shape
    head_size = features // HEADS
    width = GROUP * head_size
    groups = features // width
    values = x.astype(jnp.float32)
    normed = scaled_norm(values, gain_ref[...])
    own_lanes = [(lax.div(iota((1, width), 1), head_size) == h).astype(jnp.bfloat16) for h in range(GROUP)]
    ones = jnp.concatenate([jnp.broadcast_to(lanes, (length, width)) for lanes in own_lanes], axis=0)
    scale = head_size ** (-0.5) * LOG2_E

    def per_head(part):
        return jnp.concatenate([part * lanes for lanes in own_lanes], axis=0)

    def projections(g):
        return [
            jnp.dot(
                normed,
                qkv_ref[:, part * features + g * width : part * features + (g + 1) * width],
                preferred_element_type=jnp.float32,
            ).astype(jnp.bfloat16)
            for part in range(3)
        ]

    def attended(queries, key_rows, value_rows):
        scores = lax.dot_general(
            queries, per_head(key_rows), (((1,), (1,)), ((), ())), preferred_element_type=jnp.float32
        ) * scale
        grown = []
        for h in range(GROUP):
            own = scores[:, h * length : (h + 1) * length]
            if bias is not None:
                own = own + bias
            grown.append(jnp.exp2(own - jnp.max(own, axis=-1, keepdims=True)).astype(jnp.bfloat16))
        grown = jnp.concatenate(grown, axis=1)
        weighted = jnp.dot(grown, per_head(value_rows), preferred_element_type=jnp.float32)
        total = jnp.dot(grown, ones, preferred_element_type=jnp.float32)
        share = pl.reciprocal(total, approx=True)
        share = share * (2.0 - total * share)
        return (weighted * share).astype(jnp.bfloat16)

    contexts = []
    upcoming = projections(0)
    for g in range(groups):
        current, upcoming = upcoming, projections(g + 1) if g + 1 < groups else None
        blocks = [
            attended(*(part[start : start + length] for part in current)) for start in range(0, positions, length)
        ]
        contexts.append(blocks[0] if len(blocks) == 1 else jnp.concatenate(blocks, axis=0))
    context = jnp.concatenate(contexts, axis=1)
    return (values + jnp.dot(context, out_ref[...], preferred_element_type=jnp.float32)).astype(jnp.bfloat16)


def moved(hit, rows):
    one_hot = jnp.where(hit, 1.0, 0.0).astype(jnp.bfloat16)
    return jnp.dot(one_hot, rows, preferred_element_type=jnp.float32).astype(jnp.bfloat16)


def digits(place, *sizes):
    found = []
    for size in reversed(sizes):
        found.append(lax.rem(place, size))
        place = lax.div(place, size)
    return [place] + found[::-1]


def ranks(owner_row):
    img_rows = owner_row.shape[1]
    square = (img_rows, img_rows)
    across = jnp.broadcast_to(owner_row, square).astype(jnp.float32)
    down = across.T
    before = (down < across) | ((down == across) & (iota(square, 0) < iota(square, 1)))
    return jnp.sum(before.astype(jnp.float32), axis=0, keepdims=True).astype(jnp.int32)


def spread_rows(y, rank, my_core, dims):
    rows, _, _, strides, _, peers = dims
    chunks = strides // peers
    positions, img_rows = y.shape[0], rank.shape[1]
    lines_dev = positions // img_rows
    shape = (positions, img_rows)
    core, group, chunk, line, i = digits(iota(shape, 0), peers // CORES, chunks, lines_dev, rows)
    core = lax.rem(core + my_core, CORES)
    hit = (i * strides + chunk * peers + group * CORES + core) == rank
    return moved(jnp.concatenate([hit & (line == own) for own in range(lines_dev)], axis=1), y)


def column_kernel(turn_places, flag_ref, order_ref, frames_ref, owner_ref, gain_ref, qkv_ref, out_ref, *rest):
    y_ref = rest[-1]

    @pl.when(flag_ref[0] == 0)
    def _():
        for clip, turn_place in enumerate(turn_places):
            x = frames_ref[order_ref[turn_place]]
            y_ref[clip] = layer(x, (gain_ref, qkv_ref, out_ref), owner_ref.shape[1], None)


def spread_kernel(dims, flag_ref, y_ref, owner_ref, *rest):
    mine_ref, other_ref = rest[-2:]

    @pl.when(flag_ref[0] == 0)
    def _():
        rank = ranks(owner_ref[...])
        for clip in range(y_ref.shape[0]):
            y = spread_rows(y_ref[clip], rank, lax.rem(flag_ref[1], CORES), dims)
            mine_ref[clip] = y[: y.shape[0] // CORES]
            other_ref[clip] = y[y.shape[0] // CORES :]


def merge_kernel(dims, flag_ref, *refs):
    rows, _, lines, strides, _, peers = dims
    groups, chunks = peers // CORES, strides // peers
    halves, part_refs = refs[:-groups], refs[-groups:]
    lines_dev = lines // peers

    @pl.when(flag_ref[0] == 0)
    def _():
        size = CORES * halves[0].shape[1]
        shape = (size, size)
        my_core, my_group = lax.rem(flag_ref[1], CORES), lax.div(flag_ref[1], CORES)
        apart, chunk, core, inner = digits(iota(shape, 0), chunks, CORES, lines_dev * rows)
        far, from_group, from_chunk, from_inner = digits(iota(shape, 1), groups, chunks, lines_dev * rows)
        from_core = lax.rem(far + my_core, CORES)
        hit = (
            ((apart ^ my_group) == from_group)
            & (chunk == from_chunk)
            & (core == from_core)
            & (inner == from_inner)
        )
        size = size // groups
        pairs = [(mine[c], other[c]) for mine, other in zip(halves[::2], halves[1::2]) for c in range(mine.shape[0])]
        for clip, pair in enumerate(pairs):
            sent = moved(hit, jnp.concatenate(pair, axis=0))
            for d, part_ref in enumerate(part_refs):
                part_ref[clip * size : (clip + 1) * size, :] = sent[d * size : (d + 1) * size]


def gathered_chunk(part_refs, chunk, chunks, me, dims):
    rows, _, lines, strides, _, peers = dims
    parts = jnp.concatenate([ref[...] for ref in part_refs], axis=0)
    shape = (lines * rows, parts.shape[0])
    inner_size = lines // (peers // CORES) * rows
    group, inner = digits(iota(shape, 0), inner_size)
    apart, from_chunk, from_inner = digits(iota(shape, 1), chunks, inner_size)
    my_group = lax.div(me, CORES)
    return moved(((group ^ my_group) == apart) & (from_chunk == chunk) & (from_inner == inner), parts)


def row_bias(section, length, rows, columns):
    query, key = iota((length, length), 0), iota((length, length), 1)
    same_row = lax.rem(query, rows) == lax.rem(key, rows)
    query_line, key_line = lax.div(query, rows), lax.div(key, rows)
    query_col, key_col = lax.rem(query_line, columns), lax.rem(key_line, columns)
    across_frames = query_col == key_col
    across_columns = (lax.div(query_line, columns) == lax.div(key_line, columns)) & (key_col <= query_col)
    first = jnp.broadcast_to(section == 1, (length, length))
    allowed = same_row & ((first & across_frames) | (~first & across_columns))
    return jnp.where(allowed, 0.0, -1e30)


def packed_rows(y, owner_row, residue, dims):
    rows, _, lines, strides, most, peers = dims
    img_rows = owner_row.shape[1]
    shape = (peers * most * lines, img_rows)
    peer, n, line = digits(iota(shape, 0), most, lines)
    owners = jnp.broadcast_to(owner_row, shape)
    start = jnp.sum((owners < peer).astype(jnp.float32), axis=1, keepdims=True).astype(jnp.int32)
    end = jnp.sum((owners <= peer).astype(jnp.float32), axis=1, keepdims=True).astype(jnp.int32)
    rank = start + lax.rem(residue - start + img_rows, strides) + strides * n
    from_line, i = digits(iota(shape, 1), rows)
    return moved((lax.div(rank, strides) == i) & (line == from_line) & (rank < end), y)


def tick_kernel(dims, chunk, piece, tick, given, final, flag_ref, x_ref, owner_ref, gain_ref, qkv_ref, out_ref, *rest):
    rows, columns, lines, strides, most, peers = dims
    y_ref, given_refs = rest[-1], rest[:given]
    section, me = flag_ref[0], flag_ref[1]

    def worked(x):
        bias = row_bias(section, x.shape[0], rows, columns)
        return layer(x, (gain_ref, qkv_ref, out_ref), x.shape[0], bias)

    def packed(value):
        return packed_rows(value, owner_ref[...], chunk * peers + me, dims)

    if final:

        @pl.when(section > 2)
        def _():
            y_ref[...] = packed(worked(x_ref[...]))

        @pl.when(section == 2)
        def _():
            y_ref[...] = packed(x_ref[...])

        @pl.when(section < 2)
        def _():
            y_ref[...] = packed(given_refs[0][...])

        return

    if given:

        @pl.when(section == 1)
        def _():
            y_ref[...] = worked(gathered_chunk(given_refs, *piece, me, dims))

    if tick:

        @pl.when((section > 1) & (section <= tick + 1))
        def _():
            y_ref[...] = worked(x_ref[...])

        @pl.when(section == 0)
        def _():
            y_ref[...] = x_ref[...]


def cost(positions, features):
    return pl.CostEstimate(flops=positions, bytes_accessed=features, transcendentals=0)


def in_vmem(arrays):
    return [pltpu.with_memory_space_constraint(a, pltpu.VMEM) for a in arrays]


def load_kernel(*refs):
    count = len(refs) // 3
    copies = [
        pltpu.make_async_copy(refs[i], refs[count + i], refs[2 * count + i]) for i in range(count)
    ]
    for copy in copies:
        copy.start()
    for copy in copies:
        copy.wait()


def loaded(arrays):
    return pl.pallas_call(
        load_kernel,
        out_shape=[pltpu.VMEM(a.shape, a.dtype) for a in arrays],
        in_specs=[pl.BlockSpec(memory_space=pltpu.HBM) for _ in arrays],
        out_specs=[IN_VMEM for _ in arrays],
        scratch_shapes=[pltpu.SemaphoreType.DMA for _ in arrays],
        compiler_params=pltpu.CompilerParams(vmem_limit_bytes=1024 * 1024),
        name="loaded",
    )(*(pltpu.with_memory_space_constraint(a, pltpu.HBM) for a in arrays))


def options():
    return pltpu.CompilerParams(vmem_limit_bytes=VMEM_BYTES)


def column_pass(place, order, frames, owner_row, weights, turn_places, after):
    _, positions, features = frames.shape
    return pl.pallas_call(
        functools.partial(column_kernel, turn_places),
        out_shape=jax.ShapeDtypeStruct((len(turn_places), positions, features), jnp.bfloat16),
        in_specs=[IN_SMEM] * 2 + [IN_VMEM] * 5 + [ANYWHERE] * len(after),
        out_specs=IN_VMEM,
        compiler_params=options(),
        cost_estimate=cost(positions, features),
        name="column_pass",
    )(place, order, *in_vmem([frames]), owner_row, *in_vmem(weights), *after)


def spread(place, y, owner_row, dims, after):
    clips, positions, features = y.shape
    half = jax.ShapeDtypeStruct((clips, positions // CORES, features), jnp.bfloat16)
    return pl.pallas_call(
        functools.partial(spread_kernel, dims),
        out_shape=[half, half],
        in_specs=[IN_SMEM] + [IN_VMEM] * 2 + [ANYWHERE] * len(after),
        out_specs=[IN_VMEM] * 2,
        compiler_params=options(),
        cost_estimate=cost(positions, features),
        name="spread",
    )(place, y, owner_row, *after)


def merge(place, halves, dims):
    positions, features = halves[0].shape[1:]
    groups = dims[-1] // CORES
    clips = sum(half.shape[0] for half in halves[::2])
    part = jax.ShapeDtypeStruct((clips * CORES * positions // groups, features), jnp.bfloat16)
    return pl.pallas_call(
        functools.partial(merge_kernel, dims),
        out_shape=[part] * groups,
        in_specs=[IN_SMEM] + [IN_VMEM] * len(halves),
        out_specs=[IN_VMEM] * groups,
        compiler_params=options(),
        cost_estimate=cost(positions, features),
        name="merge",
    )(place, *halves)


def tick_pass(place, x, given, owner_row, weights, dims, chunk, piece, tick, final, after):
    rows, _, lines, _, most, peers = dims
    positions, features = rows * lines, x.shape[1]
    out_rows = peers * most * lines if final else positions
    return pl.pallas_call(
        functools.partial(tick_kernel, dims, chunk, piece, tick, len(given), final),
        out_shape=jax.ShapeDtypeStruct((out_rows, features), jnp.bfloat16),
        in_specs=[IN_SMEM] + [IN_VMEM] * (5 + len(given)) + [ANYWHERE] * len(after),
        out_specs=IN_VMEM,
        compiler_params=options(),
        cost_estimate=cost(positions, features),
        name="tick_pass",
    )(place, x, owner_row, *in_vmem(weights), *given, *after)


def settle_kernel(dims, max_rows, flag_ref, owner_ref, *refs):
    rows, columns, lines, strides, most, peers = dims
    *parts, out_ref = refs
    me = flag_ref[1]
    owners = owner_ref[...]
    total = None
    for chunk, part_ref in enumerate(parts):
        shape = (lines * max_rows, peers * most * lines)
        slot_place, part_place = iota(shape, 0), iota(shape, 1)
        start = jnp.sum((owners < me).astype(jnp.float32), axis=1, keepdims=True).astype(jnp.int32)
        residue = chunk * peers + lax.div(part_place, lines * most)
        slot = lax.rem(residue - start + strides * peers * max_rows, strides) + strides * lax.rem(
            lax.div(part_place, lines), most
        )
        hit = (slot == lax.rem(slot_place, max_rows)) & (lax.rem(part_place, lines) == lax.div(slot_place, max_rows))
        term = jnp.dot(
            jnp.where(hit, 1.0, 0.0).astype(jnp.bfloat16), part_ref[...], preferred_element_type=jnp.float32
        )
        total = term if total is None else total + term
    out_ref[...] = total.astype(jnp.bfloat16)


def settle(flags, owner_row, parts, dims, max_rows):
    rows, features = dims[2] * max_rows, parts[0].shape[1]
    depth = sum(p.shape[0] for p in parts)
    return pl.pallas_call(
        functools.partial(settle_kernel, dims, max_rows),
        out_shape=jax.ShapeDtypeStruct((rows, features), jnp.bfloat16),
        in_specs=[IN_SMEM] + [IN_VMEM] * (1 + len(parts)),
        out_specs=IN_VMEM,
        compiler_params=pltpu.CompilerParams(vmem_limit_bytes=VMEM_BYTES),
        cost_estimate=pl.CostEstimate(
            flops=2 * rows * depth * features, bytes_accessed=2 * (rows + depth) * features, transcendentals=0
        ),
        name="settle",
    )(flags, owner_row, *parts)


def swapped(x, peers):
    parts = x.reshape(peers, -1, x.shape[-1])
    return lax.all_to_all(parts, "seq", split_axis=0, concat_axis=0, tiled=True)


def local(frames_in, order, owner, qkv_weight, out_weight, gains):
    sections = lax.axis_size("section")
    peers = lax.axis_size("seq")
    section = lax.axis_index("section")
    me = lax.axis_index("seq")
    clips, lines_dev, img_rows, features = frames_in.shape
    lines = lines_dev * peers
    columns = lines // FRAMES
    max_rows = 2 * img_rows // peers
    chunks = lines_dev
    strides = peers * chunks
    rows = img_rows // strides
    most = -(-max_rows // strides)
    dims = (rows, columns, lines, strides, most, peers)
    owner_row = owner.reshape(1, img_rows)
    *weights, frames = loaded(
        [gains, qkv_weight[0], out_weight[0], frames_in.reshape(clips, lines_dev * img_rows, features)]
    )
    place = jnp.stack([section, me]).astype(jnp.int32)
    groups = peers // CORES

    homes = [1, 0, 2, 3]

    def column_clips(first, last, after, arrived):
        turn_places = [sections - 1 - home for home in homes[first:last]]
        y = column_pass(place, order, frames, owner_row, weights, turn_places, after)
        mine, other = spread(place, y, owner_row, dims, arrived)
        return mine, lax.ppermute(other, ("section", "seq"), [(p, p ^ 1) for p in range(peers)])

    def hop(halves):
        parts = merge(place, halves, dims)
        return parts[0], [
            lax.ppermute(
                part,
                ("section", "seq"),
                [(p, peers + (p // CORES ^ d) * CORES + p % CORES) for p in range(peers)],
            )
            for d, part in enumerate(parts)
        ]

    early = clips // 2
    first, fresh = hop(column_clips(0, early, [], []))
    third = column_clips(early, early + 1, [first], fresh[:1])
    fourth = column_clips(early + 1, clips, third[:1], fresh[1:-1])
    last, later = hop([*third, *fourth])
    after = [last]
    ticks = clips + sections - 2
    send, held = [None] * chunks, [None] * chunks
    for tick in range(ticks):
        pairs = []
        if tick == clips:
            pairs.append((0, 1))
        if 1 <= tick <= clips:
            pairs.append((1, 2))
        if 2 <= tick <= clips + 1:
            pairs.append((2, 3))
        if tick in (3, 4):
            pairs.append((3, 0))
        if tick == 5:
            pairs.append((3, 2))
        final = tick == ticks - 1
        for chunk in range(chunks):
            x = lax.ppermute(send[chunk], "section", pairs) if tick else fresh[0]
            given = [held[chunk]] if final else [] if tick >= clips else fresh if tick < early else later
            piece = (tick % early * chunks + chunk, early * chunks)
            half_tick = tick * chunks + chunk
            if 0 < half_tick < early * chunks:
                after = after + later[half_tick - 1 : half_tick]
            send[chunk] = tick_pass(
                place, x, given, owner_row, weights, dims, chunk, piece, tick, final, after
            )
            after = [send[chunk]]
            held[chunk] = x

    arrived = [swapped(part, peers).reshape(-1, features) for part in send]
    return settle(place, owner_row, arrived, dims, max_rows).reshape(1, lines, max_rows, features)


def solution(mesh):
    placed = (
        P(None, "seq", None, None),
        P(),
        P(),
        P("section", None, None),
        P("section", None, None),
        P("section", None),
    )
    return jax.shard_map(
        local,
        mesh=mesh,
        in_specs=placed,
        out_specs=P("section", None, "seq", None),
        check_vma=False,
    )
```

```python
import functools

import jax
import jax.numpy as jnp
from jax import lax
from jax.experimental import pallas as pl
from jax.experimental.pallas import tpu as pltpu
from jax.sharding import PartitionSpec as P

HEADS = 16
FRAMES = 4
GROUP = 4
CORES = 2
LOG2_E = 1.4426950408889634
VMEM_BYTES = 32 * 1024 * 1024
IN_VMEM = pl.BlockSpec(memory_space=pltpu.VMEM)
IN_SMEM = pl.BlockSpec(memory_space=pltpu.SMEM)
ANYWHERE = pl.BlockSpec(memory_space=pl.ANY)


def iota(shape, dim):
    return lax.broadcasted_iota(jnp.int32, shape, dim)


def scaled_norm(values, gain_row):
    mean_square = jnp.mean(values * values, axis=-1, keepdims=True)
    return (values * lax.rsqrt(mean_square + 1e-06) * gain_row).astype(jnp.bfloat16)


def layer(x, weights, length, bias):
    gain_ref, qkv_ref, out_ref = weights
    positions, features = x.shape
    head_size = features // HEADS
    width = GROUP * head_size
    groups = features // width
    values = x.astype(jnp.float32)
    normed = scaled_norm(values, gain_ref[...])
    own_lanes = [(lax.div(iota((1, width), 1), head_size) == h).astype(jnp.bfloat16) for h in range(GROUP)]
    ones = jnp.concatenate([jnp.broadcast_to(lanes, (length, width)) for lanes in own_lanes], axis=0)
    scale = head_size ** (-0.5) * LOG2_E

    def per_head(part):
        return jnp.concatenate([part * lanes for lanes in own_lanes], axis=0)

    def projections(g):
        return [
            jnp.dot(
                normed,
                qkv_ref[:, part * features + g * width : part * features + (g + 1) * width],
                preferred_element_type=jnp.float32,
            ).astype(jnp.bfloat16)
            for part in range(3)
        ]

    def attended(queries, key_rows, value_rows):
        scores = lax.dot_general(
            queries, per_head(key_rows), (((1,), (1,)), ((), ())), preferred_element_type=jnp.float32
        ) * scale
        grown = []
        for h in range(GROUP):
            own = scores[:, h * length : (h + 1) * length]
            if bias is not None:
                own = own + bias
            grown.append(jnp.exp2(own - jnp.max(own, axis=-1, keepdims=True)).astype(jnp.bfloat16))
        grown = jnp.concatenate(grown, axis=1)
        weighted = jnp.dot(grown, per_head(value_rows), preferred_element_type=jnp.float32)
        total = jnp.dot(grown, ones, preferred_element_type=jnp.float32)
        share = pl.reciprocal(total, approx=True)
        share = share * (2.0 - total * share)
        return (weighted * share).astype(jnp.bfloat16)

    contexts = []
    upcoming = projections(0)
    for g in range(groups):
        current, upcoming = upcoming, projections(g + 1) if g + 1 < groups else None
        blocks = [
            attended(*(part[start : start + length] for part in current)) for start in range(0, positions, length)
        ]
        contexts.append(blocks[0] if len(blocks) == 1 else jnp.concatenate(blocks, axis=0))
    context = jnp.concatenate(contexts, axis=1)
    return (values + jnp.dot(context, out_ref[...], preferred_element_type=jnp.float32)).astype(jnp.bfloat16)


def moved(hit, rows):
    one_hot = jnp.where(hit, 1.0, 0.0).astype(jnp.bfloat16)
    return jnp.dot(one_hot, rows, preferred_element_type=jnp.float32).astype(jnp.bfloat16)


def digits(place, *sizes):
    found = []
    for size in reversed(sizes):
        found.append(lax.rem(place, size))
        place = lax.div(place, size)
    return [place] + found[::-1]


def ranks(owner_row):
    img_rows = owner_row.shape[1]
    square = (img_rows, img_rows)
    across = jnp.broadcast_to(owner_row, square).astype(jnp.float32)
    down = across.T
    before = (down < across) | ((down == across) & (iota(square, 0) < iota(square, 1)))
    return jnp.sum(before.astype(jnp.float32), axis=0, keepdims=True).astype(jnp.int32)


def spread_rows(y, rank, my_core, dims):
    rows, _, _, strides, _, peers = dims
    chunks = strides // peers
    positions, img_rows = y.shape[0], rank.shape[1]
    lines_dev = positions // img_rows
    shape = (positions, img_rows)
    core, group, chunk, line, i = digits(iota(shape, 0), peers // CORES, chunks, lines_dev, rows)
    core = lax.rem(core + my_core, CORES)
    hit = (i * strides + chunk * peers + group * CORES + core) == rank
    return moved(jnp.concatenate([hit & (line == own) for own in range(lines_dev)], axis=1), y)


def column_kernel(dims, turn_place, flag_ref, order_ref, frames_ref, owner_ref, gain_ref, qkv_ref, out_ref, *rest):
    mine_ref, other_ref = rest[-2:]

    @pl.when(flag_ref[0] == 0)
    def _():
        x = frames_ref[order_ref[turn_place]]
        y = layer(x, (gain_ref, qkv_ref, out_ref), owner_ref.shape[1], None)
        y = spread_rows(y, ranks(owner_ref[...]), lax.rem(flag_ref[1], CORES), dims)
        mine_ref[...] = y[: y.shape[0] // CORES]
        other_ref[...] = y[y.shape[0] // CORES :]


def merge_kernel(dims, flag_ref, mine_ref, other_ref, *rest):
    rows, _, lines, strides, _, peers = dims
    groups, chunks = peers // CORES, strides // peers
    lines_dev = lines // peers
    part_refs = rest[-groups:]

    @pl.when(flag_ref[0] == 0)
    def _():
        size = CORES * mine_ref.shape[0]
        shape = (size, size)
        my_core, my_group = lax.rem(flag_ref[1], CORES), lax.div(flag_ref[1], CORES)
        apart, chunk, core, inner = digits(iota(shape, 0), chunks, CORES, lines_dev * rows)
        far, from_group, from_chunk, from_inner = digits(iota(shape, 1), groups, chunks, lines_dev * rows)
        from_core = lax.rem(far + my_core, CORES)
        hit = (
            ((apart ^ my_group) == from_group)
            & (chunk == from_chunk)
            & (core == from_core)
            & (inner == from_inner)
        )
        size = size // groups
        sent = moved(hit, jnp.concatenate([mine_ref[...], other_ref[...]], axis=0))
        for d, part_ref in enumerate(part_refs):
            part_ref[...] = sent[d * size : (d + 1) * size]


def gate_kernel(*refs):
    refs[-1][0] = 0


def gathered_chunk(part_refs, chunk, chunks, me, dims):
    rows, _, lines, strides, _, peers = dims
    parts = jnp.concatenate([ref[...] for ref in part_refs], axis=0)
    shape = (lines * rows, parts.shape[0])
    inner_size = lines // (peers // CORES) * rows
    group, inner = digits(iota(shape, 0), inner_size)
    apart, from_chunk, from_inner = digits(iota(shape, 1), chunks, inner_size)
    my_group = lax.div(me, CORES)
    return moved(((group ^ my_group) == apart) & (from_chunk == chunk) & (from_inner == inner), parts)


def row_bias(section, length, rows, columns):
    query, key = iota((length, length), 0), iota((length, length), 1)
    same_row = lax.rem(query, rows) == lax.rem(key, rows)
    query_line, key_line = lax.div(query, rows), lax.div(key, rows)
    query_col, key_col = lax.rem(query_line, columns), lax.rem(key_line, columns)
    across_frames = query_col == key_col
    across_columns = (lax.div(query_line, columns) == lax.div(key_line, columns)) & (key_col <= query_col)
    first = jnp.broadcast_to(section == 1, (length, length))
    allowed = same_row & ((first & across_frames) | (~first & across_columns))
    return jnp.where(allowed, 0.0, -1e30)


def packed_rows(y, owner_row, residue, dims):
    rows, _, lines, strides, most, peers = dims
    img_rows = owner_row.shape[1]
    shape = (peers * most * lines, img_rows)
    peer, n, line = digits(iota(shape, 0), most, lines)
    owners = jnp.broadcast_to(owner_row, shape)
    start = jnp.sum((owners < peer).astype(jnp.float32), axis=1, keepdims=True).astype(jnp.int32)
    end = jnp.sum((owners <= peer).astype(jnp.float32), axis=1, keepdims=True).astype(jnp.int32)
    rank = start + lax.rem(residue - start + img_rows, strides) + strides * n
    from_line, i = digits(iota(shape, 1), rows)
    return moved((lax.div(rank, strides) == i) & (line == from_line) & (rank < end), y)


def stored(y, y_refs):
    size = y.shape[0] // len(y_refs)
    for n, y_ref in enumerate(y_refs):
        y_ref[...] = y[n * size : (n + 1) * size]


def frame_kernel(dims, work, count, flag_ref, gain_ref, qkv_ref, out_ref, *refs):
    rows, columns, lines, strides, _, peers = dims
    piece_refs, y_refs = refs[: peers // CORES], refs[-count:]

    @pl.when(flag_ref[0] == 1)
    def _():
        parts = [gathered_chunk(piece_refs, chunk, strides // peers, flag_ref[1], dims) for chunk in work]
        x = jnp.concatenate(parts, axis=0)
        length = rows * lines
        bias = row_bias(flag_ref[0], length, rows, columns)
        stored(layer(x, (gain_ref, qkv_ref, out_ref), length, bias), y_refs)


def row_kernel(dims, tick, inputs, kept, count, flag_ref, gain_ref, qkv_ref, out_ref, *refs):
    rows, columns, lines, _, _, _ = dims
    x_refs, y_refs = refs[:inputs], refs[-count:]
    section = flag_ref[0]

    @pl.when((section > 1) & (section <= tick + 1))
    def _():
        x = jnp.concatenate([ref[...] for ref in x_refs], axis=0)
        length = rows * lines
        bias = row_bias(section, length, rows, columns)
        stored(layer(x, (gain_ref, qkv_ref, out_ref), length, bias), y_refs)

    @pl.when(section <= 1)
    def _():
        for from_ref, y_ref in zip(refs[inputs : inputs + kept] or x_refs, y_refs):
            y_ref[...] = from_ref[...]

    if kept and tick > 2:

        @pl.when(section == 0)
        def _():
            for x_ref, y_ref in zip(x_refs, y_refs):
                y_ref[...] = x_ref[...]


def final_kernel(dims, chunk, flag_ref, gain_ref, qkv_ref, out_ref, x_ref, held_ref, owner_ref, *rest):
    rows, columns, _, _, _, peers = dims
    y_ref = rest[-1]
    section = flag_ref[0]

    def packed(value):
        return packed_rows(value, owner_ref[...], chunk * peers + flag_ref[1], dims)

    @pl.when(section > 2)
    def _():
        bias = row_bias(section, x_ref.shape[0], rows, columns)
        y_ref[...] = packed(layer(x_ref[...], (gain_ref, qkv_ref, out_ref), x_ref.shape[0], bias))

    @pl.when(section == 2)
    def _():
        y_ref[...] = packed(x_ref[...])

    @pl.when(section < 2)
    def _():
        y_ref[...] = packed(held_ref[...])


def cost(positions, features):
    return pl.CostEstimate(flops=10**13, bytes_accessed=8 * positions * features, transcendentals=0)


def in_vmem(arrays):
    return [pltpu.with_memory_space_constraint(a, pltpu.VMEM) for a in arrays]


def load_kernel(*refs):
    count = len(refs) // 3
    copies = [
        pltpu.make_async_copy(refs[i], refs[count + i], refs[2 * count + i]) for i in range(count)
    ]
    for copy in copies:
        copy.start()
    for copy in copies:
        copy.wait()


def loaded(arrays):
    return pl.pallas_call(
        load_kernel,
        out_shape=[pltpu.VMEM(a.shape, a.dtype) for a in arrays],
        in_specs=[pl.BlockSpec(memory_space=pltpu.HBM) for _ in arrays],
        out_specs=[IN_VMEM for _ in arrays],
        scratch_shapes=[pltpu.SemaphoreType.DMA for _ in arrays],
        compiler_params=pltpu.CompilerParams(vmem_limit_bytes=1024 * 1024),
        name="loaded",
    )(*(pltpu.with_memory_space_constraint(a, pltpu.HBM) for a in arrays))


def options():
    return pltpu.CompilerParams(vmem_limit_bytes=VMEM_BYTES)


def column_pass(place, order, frames, owner_row, weights, dims, turn_place, after):
    _, positions, features = frames.shape
    half = jax.ShapeDtypeStruct((positions // CORES, features), jnp.bfloat16)
    return pl.pallas_call(
        functools.partial(column_kernel, dims, turn_place),
        out_shape=[half, half],
        in_specs=[IN_SMEM] * 2 + [IN_VMEM] * 5 + [ANYWHERE] * len(after),
        out_specs=[IN_VMEM] * 2,
        compiler_params=options(),
        cost_estimate=cost(positions, features),
        name="column_pass",
    )(place, order, *in_vmem([frames]), owner_row, *in_vmem(weights), *after)


def merge(place, mine, other, dims, after):
    positions, features = mine.shape
    groups = dims[-1] // CORES
    part = jax.ShapeDtypeStruct((CORES * positions // groups, features), jnp.bfloat16)
    return pl.pallas_call(
        functools.partial(merge_kernel, dims),
        out_shape=[part] * groups,
        in_specs=[IN_SMEM] + [IN_VMEM] * 2 + [ANYWHERE] * len(after),
        out_specs=[IN_VMEM] * groups,
        compiler_params=options(),
        cost_estimate=cost(positions, features),
        name="merge",
    )(place, mine, other, *after)


def gate(arrays):
    return pl.pallas_call(
        gate_kernel,
        out_shape=jax.ShapeDtypeStruct((1,), jnp.int32),
        in_specs=[ANYWHERE] * len(arrays),
        out_specs=IN_SMEM,
        compiler_params=options(),
        cost_estimate=cost(1, 1),
        name="gate",
    )(*arrays)


def frame_pass(place, pieces, weights, dims, work, count, after):
    positions, features = dims[0] * dims[2] * len(work) // count, pieces[0].shape[1]
    return pl.pallas_call(
        functools.partial(frame_kernel, dims, work, count),
        out_shape=[jax.ShapeDtypeStruct((positions, features), jnp.bfloat16)] * count,
        in_specs=[IN_SMEM] + [IN_VMEM] * (3 + len(pieces)) + [ANYWHERE] * len(after),
        out_specs=[IN_VMEM] * count,
        compiler_params=options(),
        cost_estimate=cost(positions, features),
        name="frame_pass",
    )(place, *in_vmem(weights), *pieces, *after)


def row_pass(place, x, y, weights, dims, tick, after):
    count, features = len(y) or len(x), x[0].shape[1]
    positions = sum(a.shape[0] for a in x) // count
    return pl.pallas_call(
        functools.partial(row_kernel, dims, tick, len(x), len(y), count),
        out_shape=[jax.ShapeDtypeStruct((positions, features), jnp.bfloat16)] * count,
        in_specs=[IN_SMEM] + [IN_VMEM] * (3 + len(x) + len(y)) + [ANYWHERE] * len(after),
        out_specs=[IN_VMEM] * count,
        compiler_params=options(),
        cost_estimate=cost(positions, features),
        name="row_pass",
    )(place, *in_vmem(weights), *x, *y, *after)


def final_pass(place, x, held, owner_row, weights, dims, chunk, after):
    positions, features = x.shape
    _, _, lines, _, most, peers = dims
    return pl.pallas_call(
        functools.partial(final_kernel, dims, chunk),
        out_shape=jax.ShapeDtypeStruct((peers * most * lines, features), jnp.bfloat16),
        in_specs=[IN_SMEM] + [IN_VMEM] * 6 + [ANYWHERE] * len(after),
        out_specs=IN_VMEM,
        compiler_params=options(),
        cost_estimate=cost(positions, features),
        name="final_pass",
    )(place, *in_vmem(weights), x, held, owner_row, *after)


def settle_kernel(dims, max_rows, flag_ref, owner_ref, *refs):
    rows, columns, lines, strides, most, peers = dims
    *parts, out_ref = refs
    me = flag_ref[1]
    owners = owner_ref[...]
    total = None
    for chunk, part_ref in enumerate(parts):
        shape = (lines * max_rows, peers * most * lines)
        slot_place, part_place = iota(shape, 0), iota(shape, 1)
        start = jnp.sum((owners < me).astype(jnp.float32), axis=1, keepdims=True).astype(jnp.int32)
        residue = chunk * peers + lax.div(part_place, lines * most)
        slot = lax.rem(residue - start + strides * peers * max_rows, strides) + strides * lax.rem(
            lax.div(part_place, lines), most
        )
        hit = (slot == lax.rem(slot_place, max_rows)) & (lax.rem(part_place, lines) == lax.div(slot_place, max_rows))
        term = jnp.dot(
            jnp.where(hit, 1.0, 0.0).astype(jnp.bfloat16), part_ref[...], preferred_element_type=jnp.float32
        )
        total = term if total is None else total + term
    out_ref[...] = total.astype(jnp.bfloat16)


def settle(flags, owner_row, parts, dims, max_rows):
    rows, features = dims[2] * max_rows, parts[0].shape[1]
    depth = sum(p.shape[0] for p in parts)
    return pl.pallas_call(
        functools.partial(settle_kernel, dims, max_rows),
        out_shape=jax.ShapeDtypeStruct((rows, features), jnp.bfloat16),
        in_specs=[IN_SMEM] + [IN_VMEM] * (1 + len(parts)),
        out_specs=IN_VMEM,
        compiler_params=pltpu.CompilerParams(vmem_limit_bytes=VMEM_BYTES),
        cost_estimate=pl.CostEstimate(
            flops=2 * rows * depth * features, bytes_accessed=2 * (rows + depth) * features, transcendentals=0
        ),
        name="settle",
    )(flags, owner_row, *parts)


def swapped(x, peers):
    parts = x.reshape(peers, -1, x.shape[-1])
    return lax.all_to_all(parts, "seq", split_axis=0, concat_axis=0, tiled=True)


def local(frames_in, order, owner, qkv_weight, out_weight, gains):
    sections = lax.axis_size("section")
    peers = lax.axis_size("seq")
    section = lax.axis_index("section")
    me = lax.axis_index("seq")
    clips, lines_dev, img_rows, features = frames_in.shape
    lines = lines_dev * peers
    columns = lines // FRAMES
    max_rows = 2 * img_rows // peers
    chunks = lines_dev
    strides = peers * chunks
    rows = img_rows // strides
    most = -(-max_rows // strides)
    dims = (rows, columns, lines, strides, most, peers)
    owner_row = owner.reshape(1, img_rows)
    *weights, frames = loaded(
        [gains, qkv_weight[0], out_weight[0], frames_in.reshape(clips, lines_dev * img_rows, features)]
    )
    place = jnp.stack([section, me]).astype(jnp.int32)
    groups = peers // CORES

    homes = [1, 0, 2, 3]

    def column_clip(clip, after):
        mine, other = column_pass(
            place, order, frames, owner_row, weights, dims, sections - 1 - homes[clip], after
        )
        return mine, lax.ppermute(other, ("section", "seq"), [(p, p ^ 1) for p in range(peers)])

    def hop(mine, other, after):
        parts = merge(place, mine, other, dims, after)
        return parts[0], [
            lax.ppermute(
                part,
                ("section", "seq"),
                [(p, peers + (p // CORES ^ d) * CORES + p % CORES) for p in range(peers)],
            )
            for d, part in enumerate(parts)
        ]

    def relay(parts, tick):
        pairs = []
        if tick == clips:
            pairs.append((0, 1))
        if 1 <= tick <= clips:
            pairs.append((1, 2))
        if 2 <= tick <= clips + 1:
            pairs.append((2, 3))
        if tick in (3, 4):
            pairs.append((3, 0))
        if tick == 5:
            pairs.append((3, 2))
        return [lax.ppermute(part, "section", pairs) for part in parts]

    all_chunks = list(range(chunks))
    sent, pieces = hop(*column_clip(0, []), [])
    after, y = [sent], []
    for tick in range(clips - 1):
        halves = column_clip(tick + 1, after)
        sent, upcoming = hop(*halves, [gate([*pieces, *y])])
        split = tick == clips - 2
        fresh = frame_pass(place, pieces, weights, dims, all_chunks, chunks if split else 1, [sent])
        y = row_pass(place, relay(y, tick), fresh, weights, dims, tick, []) if tick else fresh
        pieces, after = upcoming, [sent]

    y, held, ready = list(y), [None] * chunks, [y[-1]]
    for tick in range(clips - 1, clips + sections - 2):
        for chunk in all_chunks:
            (x,) = relay([y[chunk]], tick)
            if tick == clips + sections - 3:
                y[chunk] = final_pass(place, x, held[chunk], owner_row, weights, dims, chunk, ready)
            else:
                fresh = frame_pass(place, pieces, weights, dims, [chunk], 1, ready) if tick < clips else []
                (y[chunk],) = row_pass(place, [x], fresh, weights, dims, tick, ready)
            held[chunk], ready = x, [y[chunk]]

    arrived = [swapped(part, peers).reshape(-1, features) for part in y]
    return settle(place, owner_row, arrived, dims, max_rows).reshape(1, lines, max_rows, features)


def solution(mesh):
    placed = (
        P(None, "seq", None, None),
        P(),
        P(),
        P("section", None, None),
        P("section", None, None),
        P("section", None),
    )
    return jax.shard_map(
        local,
        mesh=mesh,
        in_specs=placed,
        out_specs=P("section", None, "seq", None),
        check_vma=False,
    )
```

```python
import functools

import jax
import jax.numpy as jnp
from jax import lax
from jax.experimental import pallas as pl
from jax.experimental.pallas import tpu as pltpu
from jax.sharding import PartitionSpec as P

HEADS = 16
FRAMES = 4
GROUP = 4
CORES = 2
LOG2_E = 1.4426950408889634
VMEM_BYTES = 32 * 1024 * 1024
IN_VMEM = pl.BlockSpec(memory_space=pltpu.VMEM)
IN_SMEM = pl.BlockSpec(memory_space=pltpu.SMEM)
ANYWHERE = pl.BlockSpec(memory_space=pl.ANY)


def iota(shape, dim):
    return lax.broadcasted_iota(jnp.int32, shape, dim)


def scaled_norm(values, gain_row):
    mean_square = jnp.mean(values * values, axis=-1, keepdims=True)
    return (values * lax.rsqrt(mean_square + 1e-06) * gain_row).astype(jnp.bfloat16)


def layer(x, weights, length, bias):
    gain_ref, qkv_ref, out_ref = weights
    positions, features = x.shape
    head_size = features // HEADS
    width = GROUP * head_size
    groups = features // width
    values = x.astype(jnp.float32)
    normed = scaled_norm(values, gain_ref[...])
    own_lanes = [(lax.div(iota((1, width), 1), head_size) == h).astype(jnp.bfloat16) for h in range(GROUP)]
    ones = jnp.concatenate([jnp.broadcast_to(lanes, (length, width)) for lanes in own_lanes], axis=0)
    scale = head_size ** (-0.5) * LOG2_E

    def per_head(part):
        return jnp.concatenate([part * lanes for lanes in own_lanes], axis=0)

    def projections(g):
        return [
            jnp.dot(
                normed,
                qkv_ref[:, part * features + g * width : part * features + (g + 1) * width],
                preferred_element_type=jnp.float32,
            ).astype(jnp.bfloat16)
            for part in range(3)
        ]

    def attended(queries, key_rows, value_rows):
        scores = lax.dot_general(
            queries, per_head(key_rows), (((1,), (1,)), ((), ())), preferred_element_type=jnp.float32
        ) * scale
        grown = []
        for h in range(GROUP):
            own = scores[:, h * length : (h + 1) * length]
            if bias is not None:
                own = own + bias
            grown.append(jnp.exp2(own - jnp.max(own, axis=-1, keepdims=True)).astype(jnp.bfloat16))
        grown = jnp.concatenate(grown, axis=1)
        weighted = jnp.dot(grown, per_head(value_rows), preferred_element_type=jnp.float32)
        total = jnp.dot(grown, ones, preferred_element_type=jnp.float32)
        share = pl.reciprocal(total, approx=True)
        share = share * (2.0 - total * share)
        return (weighted * share).astype(jnp.bfloat16)

    contexts = []
    upcoming = projections(0)
    for g in range(groups):
        current, upcoming = upcoming, projections(g + 1) if g + 1 < groups else None
        blocks = [
            attended(*(part[start : start + length] for part in current)) for start in range(0, positions, length)
        ]
        contexts.append(blocks[0] if len(blocks) == 1 else jnp.concatenate(blocks, axis=0))
    context = jnp.concatenate(contexts, axis=1)
    return (values + jnp.dot(context, out_ref[...], preferred_element_type=jnp.float32)).astype(jnp.bfloat16)


def moved(hit, rows):
    one_hot = jnp.where(hit, 1.0, 0.0).astype(jnp.bfloat16)
    return jnp.dot(one_hot, rows, preferred_element_type=jnp.float32).astype(jnp.bfloat16)


def digits(place, *sizes):
    found = []
    for size in reversed(sizes):
        found.append(lax.rem(place, size))
        place = lax.div(place, size)
    return [place] + found[::-1]


def ranks(owner_row):
    img_rows = owner_row.shape[1]
    square = (img_rows, img_rows)
    across = jnp.broadcast_to(owner_row, square).astype(jnp.float32)
    down = across.T
    before = (down < across) | ((down == across) & (iota(square, 0) < iota(square, 1)))
    return jnp.sum(before.astype(jnp.float32), axis=0, keepdims=True).astype(jnp.int32)


def spread_rows(y, rank, my_core, dims):
    rows, _, _, strides, _, peers = dims
    chunks = strides // peers
    positions, img_rows = y.shape[0], rank.shape[1]
    lines_dev = positions // img_rows
    shape = (positions, img_rows)
    core, group, chunk, line, i = digits(iota(shape, 0), peers // CORES, chunks, lines_dev, rows)
    core = lax.rem(core + my_core, CORES)
    hit = (i * strides + chunk * peers + group * CORES + core) == rank
    return moved(jnp.concatenate([hit & (line == own) for own in range(lines_dev)], axis=1), y)


def column_kernel(dims, turn_place, flag_ref, order_ref, frames_ref, owner_ref, gain_ref, qkv_ref, out_ref, *rest):
    mine_ref, other_ref = rest[-2:]

    @pl.when(flag_ref[0] == 0)
    def _():
        x = frames_ref[order_ref[turn_place]]
        y = layer(x, (gain_ref, qkv_ref, out_ref), owner_ref.shape[1], None)
        y = spread_rows(y, ranks(owner_ref[...]), lax.rem(flag_ref[1], CORES), dims)
        mine_ref[...] = y[: y.shape[0] // CORES]
        other_ref[...] = y[y.shape[0] // CORES :]


def merge_kernel(dims, flag_ref, mine_ref, other_ref, *rest):
    rows, _, lines, strides, _, peers = dims
    groups, chunks = peers // CORES, strides // peers
    lines_dev = lines // peers
    part_refs = rest[-groups:]

    @pl.when(flag_ref[0] == 0)
    def _():
        size = CORES * mine_ref.shape[0]
        shape = (size, size)
        my_core, my_group = lax.rem(flag_ref[1], CORES), lax.div(flag_ref[1], CORES)
        apart, chunk, core, inner = digits(iota(shape, 0), chunks, CORES, lines_dev * rows)
        far, from_group, from_chunk, from_inner = digits(iota(shape, 1), groups, chunks, lines_dev * rows)
        from_core = lax.rem(far + my_core, CORES)
        hit = (
            ((apart ^ my_group) == from_group)
            & (chunk == from_chunk)
            & (core == from_core)
            & (inner == from_inner)
        )
        size = size // groups
        sent = moved(hit, jnp.concatenate([mine_ref[...], other_ref[...]], axis=0))
        for d, part_ref in enumerate(part_refs):
            part_ref[...] = sent[d * size : (d + 1) * size]


def gate_kernel(*refs):
    refs[-1][0] = 0


def gathered_chunk(part_refs, chunk, chunks, me, dims):
    rows, _, lines, strides, _, peers = dims
    parts = jnp.concatenate([ref[...] for ref in part_refs], axis=0)
    shape = (lines * rows, parts.shape[0])
    inner_size = lines // (peers // CORES) * rows
    group, inner = digits(iota(shape, 0), inner_size)
    apart, from_chunk, from_inner = digits(iota(shape, 1), chunks, inner_size)
    my_group = lax.div(me, CORES)
    return moved(((group ^ my_group) == apart) & (from_chunk == chunk) & (from_inner == inner), parts)


def row_bias(section, length, rows, columns):
    query, key = iota((length, length), 0), iota((length, length), 1)
    same_row = lax.rem(query, rows) == lax.rem(key, rows)
    query_line, key_line = lax.div(query, rows), lax.div(key, rows)
    query_col, key_col = lax.rem(query_line, columns), lax.rem(key_line, columns)
    across_frames = query_col == key_col
    across_columns = (lax.div(query_line, columns) == lax.div(key_line, columns)) & (key_col <= query_col)
    first = jnp.broadcast_to(section == 1, (length, length))
    allowed = same_row & ((first & across_frames) | (~first & across_columns))
    return jnp.where(allowed, 0.0, -1e30)


def packed_rows(y, owner_row, me, dims):
    rows, _, lines, strides, most, peers = dims
    img_rows = owner_row.shape[1]
    chunks = strides // peers
    shape = (peers * chunks * most * lines, y.shape[0])
    peer, chunk, n, line = digits(iota(shape, 0), chunks, most, lines)
    owners = jnp.broadcast_to(owner_row, (shape[0], img_rows))
    first = peer[:, :1]
    start = jnp.sum((owners < first).astype(jnp.float32), axis=1, keepdims=True).astype(jnp.int32)
    end = jnp.sum((owners <= first).astype(jnp.float32), axis=1, keepdims=True).astype(jnp.int32)
    rank = start + lax.rem(chunk * peers + me - start + img_rows, strides) + strides * n
    from_chunk, from_line, i = digits(iota(shape, 1), lines, rows)
    hit = (lax.div(rank, strides) == i) & (line == from_line) & (chunk == from_chunk) & (rank < end)
    return moved(hit, y)


def stored(y, y_refs):
    size = y.shape[0] // len(y_refs)
    for n, y_ref in enumerate(y_refs):
        y_ref[...] = y[n * size : (n + 1) * size]


def frame_kernel(dims, work, count, flag_ref, gain_ref, qkv_ref, out_ref, *refs):
    rows, columns, lines, strides, _, peers = dims
    piece_refs, y_refs = refs[: peers // CORES], refs[-count:]

    @pl.when(flag_ref[0] == 1)
    def _():
        parts = [gathered_chunk(piece_refs, chunk, strides // peers, flag_ref[1], dims) for chunk in work]
        x = jnp.concatenate(parts, axis=0)
        length = rows * lines
        bias = row_bias(flag_ref[0], length, rows, columns)
        stored(layer(x, (gain_ref, qkv_ref, out_ref), length, bias), y_refs)


def row_kernel(dims, tick, inputs, kept, count, flag_ref, gain_ref, qkv_ref, out_ref, *refs):
    rows, columns, lines, _, _, _ = dims
    x_refs, y_refs = refs[:inputs], refs[-count:]
    section = flag_ref[0]

    @pl.when((section > 1) & (section <= tick + 1))
    def _():
        x = jnp.concatenate([ref[...] for ref in x_refs], axis=0)
        length = rows * lines
        bias = row_bias(section, length, rows, columns)
        stored(layer(x, (gain_ref, qkv_ref, out_ref), length, bias), y_refs)

    @pl.when(section <= 1)
    def _():
        for from_ref, y_ref in zip(refs[inputs : inputs + kept] or x_refs, y_refs):
            y_ref[...] = from_ref[...]

    if kept and tick > 2:

        @pl.when(section == 0)
        def _():
            for x_ref, y_ref in zip(x_refs, y_refs):
                y_ref[...] = x_ref[...]


def final_kernel(dims, count, flag_ref, gain_ref, qkv_ref, out_ref, owner_ref, *refs):
    rows, columns, lines, _, _, _ = dims
    y_ref = refs[-1]
    section = flag_ref[0]

    def packed(value):
        y_ref[...] = packed_rows(value, owner_ref[...], flag_ref[1], dims)

    def joined(part_refs):
        return jnp.concatenate([ref[...] for ref in part_refs], axis=0)

    @pl.when(section > 2)
    def _():
        length = rows * lines
        bias = row_bias(section, length, rows, columns)
        packed(layer(joined(refs[:count]), (gain_ref, qkv_ref, out_ref), length, bias))

    @pl.when(section == 2)
    def _():
        packed(joined(refs[:count]))

    @pl.when(section < 2)
    def _():
        packed(joined(refs[count : 2 * count]))


def cost(positions, features):
    return pl.CostEstimate(flops=10**10, bytes_accessed=positions * features, transcendentals=0)


def in_vmem(arrays):
    return [pltpu.with_memory_space_constraint(a, pltpu.VMEM) for a in arrays]


def load_kernel(*refs):
    count = len(refs) // 3
    copies = [
        pltpu.make_async_copy(refs[i], refs[count + i], refs[2 * count + i]) for i in range(count)
    ]
    for copy in copies:
        copy.start()
    for copy in copies:
        copy.wait()


def loaded(arrays):
    return pl.pallas_call(
        load_kernel,
        out_shape=[pltpu.VMEM(a.shape, a.dtype) for a in arrays],
        in_specs=[pl.BlockSpec(memory_space=pltpu.HBM) for _ in arrays],
        out_specs=[IN_VMEM for _ in arrays],
        scratch_shapes=[pltpu.SemaphoreType.DMA for _ in arrays],
        compiler_params=pltpu.CompilerParams(vmem_limit_bytes=1024 * 1024),
        name="loaded",
    )(*(pltpu.with_memory_space_constraint(a, pltpu.HBM) for a in arrays))


def options():
    return pltpu.CompilerParams(vmem_limit_bytes=VMEM_BYTES)


def column_pass(place, order, frames, owner_row, weights, dims, turn_place, after):
    _, positions, features = frames.shape
    half = pltpu.VMEM((positions // CORES, features), jnp.bfloat16)
    return pl.pallas_call(
        functools.partial(column_kernel, dims, turn_place),
        out_shape=[half, half],
        in_specs=[IN_SMEM] * 2 + [IN_VMEM] * 5 + [ANYWHERE] * len(after),
        out_specs=[IN_VMEM] * 2,
        compiler_params=options(),
        cost_estimate=cost(positions, features),
        name="column_pass",
    )(place, order, *in_vmem([frames]), owner_row, *in_vmem(weights), *after)


def merge(place, mine, other, dims, after):
    positions, features = mine.shape
    groups = dims[-1] // CORES
    part = pltpu.VMEM((CORES * positions // groups, features), jnp.bfloat16)
    return pl.pallas_call(
        functools.partial(merge_kernel, dims),
        out_shape=[part] * groups,
        in_specs=[IN_SMEM] + [IN_VMEM] * 2 + [ANYWHERE] * len(after),
        out_specs=[IN_VMEM] * groups,
        compiler_params=options(),
        cost_estimate=cost(positions, features),
        name="merge",
    )(place, *in_vmem([mine, other]), *after)


def gate(arrays):
    return pl.pallas_call(
        gate_kernel,
        out_shape=jax.ShapeDtypeStruct((1,), jnp.int32),
        in_specs=[ANYWHERE] * len(arrays),
        out_specs=IN_SMEM,
        compiler_params=options(),
        cost_estimate=cost(1, 1),
        name="gate",
    )(*arrays)


def frame_pass(place, pieces, weights, dims, work, count, after):
    positions, features = dims[0] * dims[2] * len(work) // count, pieces[0].shape[1]
    return pl.pallas_call(
        functools.partial(frame_kernel, dims, work, count),
        out_shape=[pltpu.VMEM((positions, features), jnp.bfloat16)] * count,
        in_specs=[IN_SMEM] + [IN_VMEM] * (3 + len(pieces)) + [ANYWHERE] * len(after),
        out_specs=[IN_VMEM] * count,
        compiler_params=options(),
        cost_estimate=cost(positions, features),
        name="frame_pass",
    )(place, *in_vmem([*weights, *pieces]), *after)


def row_pass(place, x, y, weights, dims, tick, after):
    count, features = len(y) or len(x), x[0].shape[1]
    positions = sum(a.shape[0] for a in x) // count
    return pl.pallas_call(
        functools.partial(row_kernel, dims, tick, len(x), len(y), count),
        out_shape=[pltpu.VMEM((positions, features), jnp.bfloat16)] * count,
        in_specs=[IN_SMEM] + [IN_VMEM] * (3 + len(x) + len(y)) + [ANYWHERE] * len(after),
        out_specs=[IN_VMEM] * count,
        compiler_params=options(),
        cost_estimate=cost(positions, features),
        name="row_pass",
    )(place, *in_vmem([*weights, *x, *y]), *after)


def final_pass(place, x, held, owner_row, weights, dims):
    positions, features = x[0].shape
    _, _, lines, strides, most, _ = dims
    return pl.pallas_call(
        functools.partial(final_kernel, dims, len(x)),
        out_shape=jax.ShapeDtypeStruct((strides * most * lines, features), jnp.bfloat16),
        in_specs=[IN_SMEM] + [IN_VMEM] * (4 + 2 * len(x)),
        out_specs=IN_VMEM,
        compiler_params=options(),
        cost_estimate=cost(positions, features),
        name="final_pass",
    )(place, *in_vmem(weights), owner_row, *in_vmem([*x, *held]))


def settle_kernel(dims, max_rows, flag_ref, owner_ref, part_ref, out_ref):
    rows, columns, lines, strides, most, peers = dims
    shape = (out_ref.shape[0], part_ref.shape[0])
    start = jnp.sum((owner_ref[...] < flag_ref[1]).astype(jnp.float32), axis=1, keepdims=True).astype(jnp.int32)
    peer, chunk, n, line = digits(iota((1, shape[1]), 1), strides // peers, most, lines)
    slot = lax.rem(chunk * peers + peer - start + owner_ref.shape[1], strides) + strides * n
    out_line, out_slot = digits(iota((shape[0], 1), 0), max_rows)
    out_ref[...] = moved((slot == out_slot) & (line == out_line), part_ref[...])


def settle(place, owner_row, part, dims, max_rows):
    rows, features = dims[2] * max_rows, part.shape[1]
    return pl.pallas_call(
        functools.partial(settle_kernel, dims, max_rows),
        out_shape=jax.ShapeDtypeStruct((rows, features), jnp.bfloat16),
        in_specs=[IN_SMEM] + [IN_VMEM] * 2,
        out_specs=IN_VMEM,
        compiler_params=options(),
        cost_estimate=cost(rows, features),
        name="settle",
    )(place, owner_row, part)


def swapped(x, peers):
    parts = x.reshape(peers, -1, x.shape[-1])
    return lax.all_to_all(parts, "seq", split_axis=0, concat_axis=0, tiled=True)


def local(frames_in, order, owner, qkv_weight, out_weight, gains):
    sections = lax.axis_size("section")
    peers = lax.axis_size("seq")
    section = lax.axis_index("section")
    me = lax.axis_index("seq")
    clips, lines_dev, img_rows, features = frames_in.shape
    lines = lines_dev * peers
    columns = lines // FRAMES
    max_rows = 2 * img_rows // peers
    chunks = lines_dev
    strides = peers * chunks
    rows = img_rows // strides
    most = -(-max_rows // strides)
    dims = (rows, columns, lines, strides, most, peers)
    owner_row = owner.reshape(1, img_rows)
    *weights, frames = loaded(
        [gains, qkv_weight[0], out_weight[0], frames_in.reshape(clips, lines_dev * img_rows, features)]
    )
    place = jnp.stack([section, me]).astype(jnp.int32)
    groups = peers // CORES

    homes = [1, 0, 2, 3]

    def column_clip(clip, after):
        mine, other = column_pass(
            place, order, frames, owner_row, weights, dims, sections - 1 - homes[clip], after
        )
        return mine, lax.ppermute(other, ("section", "seq"), [(p, p ^ 1) for p in range(peers)])

    def hop(mine, other, after):
        parts = merge(place, mine, other, dims, after)
        return parts[0], [
            lax.ppermute(
                part,
                ("section", "seq"),
                [(p, peers + (p // CORES ^ d) * CORES + p % CORES) for p in range(peers)],
            )
            for d, part in enumerate(parts)
        ]

    def relay(parts, tick):
        pairs = []
        if tick == clips:
            pairs.append((0, 1))
        if 1 <= tick <= clips:
            pairs.append((1, 2))
        if 2 <= tick <= clips + 1:
            pairs.append((2, 3))
        if tick in (3, 4):
            pairs.append((3, 0))
        if tick == 5:
            pairs.append((3, 2))
        return [lax.ppermute(part, "section", pairs) for part in parts]

    all_chunks = list(range(chunks))
    sent, pieces = hop(*column_clip(0, []), [])
    after, y = [sent], []
    for tick in range(clips - 1):
        halves = column_clip(tick + 1, after)
        sent, upcoming = hop(*halves, [gate([*pieces, *y])])
        split = tick == clips - 2
        fresh = frame_pass(place, pieces, weights, dims, all_chunks, chunks if split else 1, [sent])
        y = row_pass(place, relay(y, tick), fresh, weights, dims, tick, []) if tick else fresh
        pieces, after = upcoming, [sent]

    y, held, ready = list(y), [None] * chunks, [y[-1]]
    for tick in range(clips - 1, clips + sections - 3):
        for chunk in all_chunks:
            (x,) = relay([y[chunk]], tick)
            fresh = frame_pass(place, pieces, weights, dims, [chunk], 1, ready) if tick < clips else []
            (y[chunk],) = row_pass(place, [x], fresh, weights, dims, tick, ready)
            held[chunk], ready = x, [y[chunk]]
    x = relay(y, clips + sections - 3)
    packed = final_pass(place, x, held, owner_row, weights, dims)
    arrived = swapped(packed, peers).reshape(-1, features)
    return settle(place, owner_row, arrived, dims, max_rows).reshape(1, lines, max_rows, features)


def solution(mesh):
    placed = (
        P(None, "seq", None, None),
        P(),
        P(),
        P("section", None, None),
        P("section", None, None),
        P("section", None),
    )
    return jax.shard_map(
        local,
        mesh=mesh,
        in_specs=placed,
        out_specs=P("section", None, "seq", None),
        check_vma=False,
    )
```

```python
import functools

import jax
import jax.numpy as jnp
from jax import lax
from jax.experimental import pallas as pl
from jax.experimental.pallas import tpu as pltpu
from jax.sharding import PartitionSpec as P

HEADS = 16
FRAMES = 4
GROUP = 4
CORES = 2
LOG2_E = 1.4426950408889634
VMEM_BYTES = 32 * 1024 * 1024
IN_VMEM = pl.BlockSpec(memory_space=pltpu.VMEM)
IN_SMEM = pl.BlockSpec(memory_space=pltpu.SMEM)
ANYWHERE = pl.BlockSpec(memory_space=pl.ANY)


def iota(shape, dim):
    return lax.broadcasted_iota(jnp.int32, shape, dim)


def scaled_norm(values, gain_row):
    mean_square = jnp.mean(values * values, axis=-1, keepdims=True)
    return (values * lax.rsqrt(mean_square + 1e-06) * gain_row).astype(jnp.bfloat16)


def layer(x, weights, length, bias):
    gain_ref, qkv_ref, out_ref = weights
    positions, features = x.shape
    head_size = features // HEADS
    width = GROUP * head_size
    groups = features // width
    values = x.astype(jnp.float32)
    normed = scaled_norm(values, gain_ref[...])
    own_lanes = [(lax.div(iota((1, width), 1), head_size) == h).astype(jnp.bfloat16) for h in range(GROUP)]
    ones = jnp.concatenate([jnp.broadcast_to(lanes, (length, width)) for lanes in own_lanes], axis=0)
    scale = head_size ** (-0.5) * LOG2_E

    def per_head(part):
        return jnp.concatenate([part * lanes for lanes in own_lanes], axis=0)

    def projections(g):
        return [
            jnp.dot(
                normed,
                qkv_ref[:, part * features + g * width : part * features + (g + 1) * width],
                preferred_element_type=jnp.float32,
            ).astype(jnp.bfloat16)
            for part in range(3)
        ]

    def attended(queries, key_rows, value_rows):
        scores = lax.dot_general(
            queries, per_head(key_rows), (((1,), (1,)), ((), ())), preferred_element_type=jnp.float32
        ) * scale
        grown = []
        for h in range(GROUP):
            own = scores[:, h * length : (h + 1) * length]
            if bias is not None:
                own = own + bias
            grown.append(jnp.exp2(own - jnp.max(own, axis=-1, keepdims=True)).astype(jnp.bfloat16))
        grown = jnp.concatenate(grown, axis=1)
        weighted = jnp.dot(grown, per_head(value_rows), preferred_element_type=jnp.float32)
        total = jnp.dot(grown, ones, preferred_element_type=jnp.float32)
        share = pl.reciprocal(total, approx=True)
        share = share * (2.0 - total * share)
        return (weighted * share).astype(jnp.bfloat16)

    contexts = []
    upcoming = projections(0)
    for g in range(groups):
        current, upcoming = upcoming, projections(g + 1) if g + 1 < groups else None
        blocks = [
            attended(*(part[start : start + length] for part in current)) for start in range(0, positions, length)
        ]
        contexts.append(blocks[0] if len(blocks) == 1 else jnp.concatenate(blocks, axis=0))
    context = jnp.concatenate(contexts, axis=1)
    return (values + jnp.dot(context, out_ref[...], preferred_element_type=jnp.float32)).astype(jnp.bfloat16)


def moved(hit, rows):
    one_hot = jnp.where(hit, 1.0, 0.0).astype(jnp.bfloat16)
    return jnp.dot(one_hot, rows, preferred_element_type=jnp.float32).astype(jnp.bfloat16)


def digits(place, *sizes):
    found = []
    for size in reversed(sizes):
        found.append(lax.rem(place, size))
        place = lax.div(place, size)
    return [place] + found[::-1]


def ranks(owner_row):
    img_rows = owner_row.shape[1]
    square = (img_rows, img_rows)
    across = jnp.broadcast_to(owner_row, square).astype(jnp.float32)
    down = across.T
    before = (down < across) | ((down == across) & (iota(square, 0) < iota(square, 1)))
    return jnp.sum(before.astype(jnp.float32), axis=0, keepdims=True).astype(jnp.int32)


def spread_rows(y, rank, my_core, dims):
    rows, _, _, strides, _, peers = dims
    chunks = strides // peers
    positions, img_rows = y.shape[0], rank.shape[1]
    lines_dev = positions // img_rows
    shape = (positions, img_rows)
    core, group, chunk, line, i = digits(iota(shape, 0), peers // CORES, chunks, lines_dev, rows)
    core = lax.rem(core + my_core, CORES)
    hit = (i * strides + chunk * peers + group * CORES + core) == rank
    return moved(jnp.concatenate([hit & (line == own) for own in range(lines_dev)], axis=1), y)


def column_kernel(dims, turn_places, flag_ref, order_ref, frames_ref, owner_ref, gain_ref, qkv_ref, out_ref, *rest):
    mine_ref, other_ref = rest[-2:]

    @pl.when(flag_ref[0] == 0)
    def _():
        rank = ranks(owner_ref[...])
        for clip, turn_place in enumerate(turn_places):
            x = frames_ref[order_ref[turn_place]]
            y = layer(x, (gain_ref, qkv_ref, out_ref), owner_ref.shape[1], None)
            y = spread_rows(y, rank, lax.rem(flag_ref[1], CORES), dims)
            mine_ref[clip] = y[: y.shape[0] // CORES]
            other_ref[clip] = y[y.shape[0] // CORES :]


def merge_kernel(dims, clip, flag_ref, mine_ref, other_ref, *rest):
    rows, _, lines, strides, _, peers = dims
    groups, chunks = peers // CORES, strides // peers
    lines_dev = lines // peers
    part_refs = rest[-groups:]

    @pl.when(flag_ref[0] == 0)
    def _():
        size = CORES * mine_ref.shape[1]
        shape = (size, size)
        my_core, my_group = lax.rem(flag_ref[1], CORES), lax.div(flag_ref[1], CORES)
        apart, chunk, core, inner = digits(iota(shape, 0), chunks, CORES, lines_dev * rows)
        far, from_group, from_chunk, from_inner = digits(iota(shape, 1), groups, chunks, lines_dev * rows)
        from_core = lax.rem(far + my_core, CORES)
        hit = (
            ((apart ^ my_group) == from_group)
            & (chunk == from_chunk)
            & (core == from_core)
            & (inner == from_inner)
        )
        size = size // groups
        sent = moved(hit, jnp.concatenate([mine_ref[clip], other_ref[clip]], axis=0))
        for d, part_ref in enumerate(part_refs):
            part_ref[...] = sent[d * size : (d + 1) * size]


def gate_kernel(*refs):
    refs[-1][0] = 0


def gathered_chunk(part_refs, chunk, chunks, me, dims):
    rows, _, lines, strides, _, peers = dims
    parts = jnp.concatenate([ref[...] for ref in part_refs], axis=0)
    shape = (lines * rows, parts.shape[0])
    inner_size = lines // (peers // CORES) * rows
    group, inner = digits(iota(shape, 0), inner_size)
    apart, from_chunk, from_inner = digits(iota(shape, 1), chunks, inner_size)
    my_group = lax.div(me, CORES)
    return moved(((group ^ my_group) == apart) & (from_chunk == chunk) & (from_inner == inner), parts)


def row_bias(section, length, rows, columns):
    query, key = iota((length, length), 0), iota((length, length), 1)
    same_row = lax.rem(query, rows) == lax.rem(key, rows)
    query_line, key_line = lax.div(query, rows), lax.div(key, rows)
    query_col, key_col = lax.rem(query_line, columns), lax.rem(key_line, columns)
    across_frames = query_col == key_col
    across_columns = (lax.div(query_line, columns) == lax.div(key_line, columns)) & (key_col <= query_col)
    first = jnp.broadcast_to(section == 1, (length, length))
    allowed = same_row & ((first & across_frames) | (~first & across_columns))
    return jnp.where(allowed, 0.0, -1e30)


def packed_rows(y, owner_row, chunk, me, dims):
    rows, _, lines, strides, most, peers = dims
    img_rows = owner_row.shape[1]
    shape = (peers * most * lines, img_rows)
    peer, n, line = digits(iota((shape[0], 1), 0), most, lines)
    owners = jnp.broadcast_to(owner_row, shape)
    start = jnp.sum((owners < peer).astype(jnp.float32), axis=1, keepdims=True).astype(jnp.int32)
    end = jnp.sum((owners <= peer).astype(jnp.float32), axis=1, keepdims=True).astype(jnp.int32)
    rank = start + lax.rem(chunk * peers + me - start + img_rows, strides) + strides * n
    from_line, i = digits(iota((1, shape[1]), 1), rows)
    return moved((lax.div(rank, strides) == i) & (line == from_line) & (rank < end), y)


def stored(y, y_refs):
    size = y.shape[0] // len(y_refs)
    for n, y_ref in enumerate(y_refs):
        y_ref[...] = y[n * size : (n + 1) * size]


def frame_kernel(dims, work, count, flag_ref, gain_ref, qkv_ref, out_ref, *refs):
    rows, columns, lines, strides, _, peers = dims
    piece_refs, y_refs = refs[: peers // CORES], refs[-count:]

    @pl.when(flag_ref[0] == 1)
    def _():
        parts = [gathered_chunk(piece_refs, chunk, strides // peers, flag_ref[1], dims) for chunk in work]
        x = jnp.concatenate(parts, axis=0)
        length = rows * lines
        bias = row_bias(flag_ref[0], length, rows, columns)
        stored(layer(x, (gain_ref, qkv_ref, out_ref), length, bias), y_refs)


def row_kernel(dims, tick, inputs, kept, count, flag_ref, gain_ref, qkv_ref, out_ref, *refs):
    rows, columns, lines, _, _, _ = dims
    x_refs, y_refs = refs[:inputs], refs[-count:]
    section = flag_ref[0]

    @pl.when((section > 1) & (section <= tick + 1))
    def _():
        x = jnp.concatenate([ref[...] for ref in x_refs], axis=0)
        length = rows * lines
        bias = row_bias(section, length, rows, columns)
        stored(layer(x, (gain_ref, qkv_ref, out_ref), length, bias), y_refs)

    @pl.when(section <= 1)
    def _():
        for from_ref, y_ref in zip(refs[inputs : inputs + kept] or x_refs, y_refs):
            y_ref[...] = from_ref[...]

    if kept and tick > 2:

        @pl.when(section == 0)
        def _():
            for x_ref, y_ref in zip(x_refs, y_refs):
                y_ref[...] = x_ref[...]


def final_kernel(dims, chunk, flag_ref, gain_ref, qkv_ref, out_ref, owner_ref, x_ref, held_ref, *rest):
    rows, columns, lines, _, _, _ = dims
    y_ref = rest[-1]
    section = flag_ref[0]

    def packed(value):
        y_ref[...] = packed_rows(value, owner_ref[...], chunk, flag_ref[1], dims)

    @pl.when(section > 2)
    def _():
        length = rows * lines
        packed(layer(x_ref[...], (gain_ref, qkv_ref, out_ref), length, row_bias(section, length, rows, columns)))

    @pl.when(section == 2)
    def _():
        packed(x_ref[...])

    @pl.when(section < 2)
    def _():
        packed(held_ref[...])


def cost(positions, features):
    return pl.CostEstimate(flops=10**10, bytes_accessed=positions * features, transcendentals=0)


def in_vmem(arrays):
    return [pltpu.with_memory_space_constraint(a, pltpu.VMEM) for a in arrays]


def load_kernel(*refs):
    count = len(refs) // 3
    copies = [
        pltpu.make_async_copy(refs[i], refs[count + i], refs[2 * count + i]) for i in range(count)
    ]
    for copy in copies:
        copy.start()
    for copy in copies:
        copy.wait()


def loaded(arrays):
    return pl.pallas_call(
        load_kernel,
        out_shape=[pltpu.VMEM(a.shape, a.dtype) for a in arrays],
        in_specs=[pl.BlockSpec(memory_space=pltpu.HBM) for _ in arrays],
        out_specs=[IN_VMEM for _ in arrays],
        scratch_shapes=[pltpu.SemaphoreType.DMA for _ in arrays],
        compiler_params=pltpu.CompilerParams(vmem_limit_bytes=1024 * 1024),
        name="loaded",
    )(*(pltpu.with_memory_space_constraint(a, pltpu.HBM) for a in arrays))


def options():
    return pltpu.CompilerParams(vmem_limit_bytes=VMEM_BYTES)


def column_pass(place, order, frames, owner_row, weights, dims, turn_places, after):
    _, positions, features = frames.shape
    half = pltpu.VMEM((len(turn_places), positions // CORES, features), jnp.bfloat16)
    return pl.pallas_call(
        functools.partial(column_kernel, dims, turn_places),
        out_shape=[half, half],
        in_specs=[IN_SMEM] * 2 + [IN_VMEM] * 5 + [ANYWHERE] * len(after),
        out_specs=[IN_VMEM] * 2,
        compiler_params=options(),
        cost_estimate=cost(positions, features),
        name="column_pass",
    )(place, order, *in_vmem([frames]), owner_row, *in_vmem(weights), *after)


def merge(place, mine, other, dims, clip, after):
    _, positions, features = mine.shape
    groups = dims[-1] // CORES
    part = pltpu.VMEM((CORES * positions // groups, features), jnp.bfloat16)
    return pl.pallas_call(
        functools.partial(merge_kernel, dims, clip),
        out_shape=[part] * groups,
        in_specs=[IN_SMEM] + [IN_VMEM] * 2 + [ANYWHERE] * len(after),
        out_specs=[IN_VMEM] * groups,
        compiler_params=options(),
        cost_estimate=cost(positions, features),
        name="merge",
    )(place, *in_vmem([mine, other]), *after)


def gate(arrays):
    return pl.pallas_call(
        gate_kernel,
        out_shape=jax.ShapeDtypeStruct((1,), jnp.int32),
        in_specs=[ANYWHERE] * len(arrays),
        out_specs=IN_SMEM,
        compiler_params=options(),
        cost_estimate=cost(1, 1),
        name="gate",
    )(*arrays)


def frame_pass(place, pieces, weights, dims, work, count, after):
    positions, features = dims[0] * dims[2] * len(work) // count, pieces[0].shape[1]
    return pl.pallas_call(
        functools.partial(frame_kernel, dims, work, count),
        out_shape=[pltpu.VMEM((positions, features), jnp.bfloat16)] * count,
        in_specs=[IN_SMEM] + [IN_VMEM] * (3 + len(pieces)) + [ANYWHERE] * len(after),
        out_specs=[IN_VMEM] * count,
        compiler_params=options(),
        cost_estimate=cost(positions, features),
        name="frame_pass",
    )(place, *in_vmem([*weights, *pieces]), *after)


def row_pass(place, x, y, weights, dims, tick, after):
    count, features = len(y) or len(x), x[0].shape[1]
    positions = sum(a.shape[0] for a in x) // count
    return pl.pallas_call(
        functools.partial(row_kernel, dims, tick, len(x), len(y), count),
        out_shape=[pltpu.VMEM((positions, features), jnp.bfloat16)] * count,
        in_specs=[IN_SMEM] + [IN_VMEM] * (3 + len(x) + len(y)) + [ANYWHERE] * len(after),
        out_specs=[IN_VMEM] * count,
        compiler_params=options(),
        cost_estimate=cost(positions, features),
        name="row_pass",
    )(place, *in_vmem([*weights, *x, *y]), *after)


def final_pass(place, x, held, owner_row, weights, dims, chunk, after):
    positions, features = x.shape
    _, _, lines, _, most, peers = dims
    return pl.pallas_call(
        functools.partial(final_kernel, dims, chunk),
        out_shape=jax.ShapeDtypeStruct((peers * most * lines, features), jnp.bfloat16),
        in_specs=[IN_SMEM] + [IN_VMEM] * 6 + [ANYWHERE] * len(after),
        out_specs=IN_VMEM,
        compiler_params=options(),
        cost_estimate=cost(positions, features),
        name="final_pass",
    )(place, *in_vmem(weights), owner_row, *in_vmem([x, held]), *after)


def settle_kernel(dims, max_rows, flag_ref, owner_ref, *refs):
    rows, columns, lines, strides, most, peers = dims
    out_ref = refs[-1]
    parts = jnp.concatenate([ref[...] for ref in refs[:-1]], axis=0)
    shape = (out_ref.shape[0], parts.shape[0])
    start = jnp.sum((owner_ref[...] < flag_ref[1]).astype(jnp.float32), axis=1, keepdims=True).astype(jnp.int32)
    chunk, peer, n, line = digits(iota((1, shape[1]), 1), peers, most, lines)
    slot = lax.rem(chunk * peers + peer - start + owner_ref.shape[1], strides) + strides * n
    out_line, out_slot = digits(iota((shape[0], 1), 0), max_rows)
    out_ref[...] = moved((slot == out_slot) & (line == out_line), parts)


def settle(place, owner_row, parts, dims, max_rows):
    rows, features = dims[2] * max_rows, parts[0].shape[1]
    return pl.pallas_call(
        functools.partial(settle_kernel, dims, max_rows),
        out_shape=jax.ShapeDtypeStruct((rows, features), jnp.bfloat16),
        in_specs=[IN_SMEM] + [IN_VMEM] * (1 + len(parts)),
        out_specs=IN_VMEM,
        compiler_params=options(),
        cost_estimate=cost(rows, features),
        name="settle",
    )(place, owner_row, *parts)


def swapped(x, peers):
    parts = x.reshape(peers, -1, x.shape[-1])
    return lax.all_to_all(parts, "seq", split_axis=0, concat_axis=0, tiled=True)


def local(frames_in, order, owner, qkv_weight, out_weight, gains):
    sections = lax.axis_size("section")
    peers = lax.axis_size("seq")
    section = lax.axis_index("section")
    me = lax.axis_index("seq")
    clips, lines_dev, img_rows, features = frames_in.shape
    lines = lines_dev * peers
    columns = lines // FRAMES
    max_rows = 2 * img_rows // peers
    chunks = lines_dev
    strides = peers * chunks
    rows = img_rows // strides
    most = -(-max_rows // strides)
    dims = (rows, columns, lines, strides, most, peers)
    owner_row = owner.reshape(1, img_rows)
    *weights, frames = loaded(
        [gains, qkv_weight[0], out_weight[0], frames_in.reshape(clips, lines_dev * img_rows, features)]
    )
    place = jnp.stack([section, me]).astype(jnp.int32)
    groups = peers // CORES

    homes = [1, 0, 2, 3]

    def column_clips(first, last, after):
        turn_places = [sections - 1 - home for home in homes[first:last]]
        mine, other = column_pass(place, order, frames, owner_row, weights, dims, turn_places, after)
        return mine, lax.ppermute(other, ("section", "seq"), [(p, p ^ 1) for p in range(peers)])

    def hop(halves, clip, after):
        parts = merge(place, *halves, dims, clip, after)
        return parts[0], [
            lax.ppermute(
                part,
                ("section", "seq"),
                [(p, peers + (p // CORES ^ d) * CORES + p % CORES) for p in range(peers)],
            )
            for d, part in enumerate(parts)
        ]

    def relay(parts, tick):
        pairs = []
        if tick == clips:
            pairs.append((0, 1))
        if 1 <= tick <= clips:
            pairs.append((1, 2))
        if 2 <= tick <= clips + 1:
            pairs.append((2, 3))
        if tick in (3, 4):
            pairs.append((3, 0))
        if tick == 5:
            pairs.append((3, 2))
        return [lax.ppermute(part, "section", pairs) for part in parts]

    all_chunks = list(range(chunks))
    sent, pieces = hop(column_clips(0, 1, []), 0, [])
    halves, y = column_clips(1, clips, [sent]), []
    for tick in range(clips - 1):
        sent, upcoming = hop(halves, tick, [gate([*pieces, *y])])
        split = tick == clips - 2
        fresh = frame_pass(place, pieces, weights, dims, all_chunks, chunks if split else 1, [sent])
        y = row_pass(place, relay(y, tick), fresh, weights, dims, tick, []) if tick else fresh
        pieces = upcoming

    y, held, ready = list(y), [None] * chunks, [y[-1]]
    for tick in range(clips - 1, clips + sections - 3):
        for chunk in all_chunks:
            (x,) = relay([y[chunk]], tick)
            fresh = frame_pass(place, pieces, weights, dims, [chunk], 1, ready) if tick < clips else []
            (y[chunk],) = row_pass(place, [x], fresh, weights, dims, tick, ready)
            held[chunk], ready = x, [y[chunk]]
    for chunk in all_chunks:
        (x,) = relay([y[chunk]], clips + sections - 3)
        y[chunk] = final_pass(place, x, held[chunk], owner_row, weights, dims, chunk, ready)
        ready = [y[chunk]]
    arrived = [swapped(part, peers).reshape(-1, features) for part in y]
    return settle(place, owner_row, arrived, dims, max_rows).reshape(1, lines, max_rows, features)


def solution(mesh):
    placed = (
        P(None, "seq", None, None),
        P(),
        P(),
        P("section", None, None),
        P("section", None, None),
        P("section", None),
    )
    return jax.shard_map(
        local,
        mesh=mesh,
        in_specs=placed,
        out_specs=P("section", None, "seq", None),
        check_vma=False,
    )
```

```python
import functools

import jax
import jax.numpy as jnp
from jax import lax
from jax.experimental import pallas as pl
from jax.experimental.pallas import tpu as pltpu
from jax.sharding import PartitionSpec as P

HEADS = 16
FRAMES = 4
GROUP = 4
CORES = 2
LOG2_E = 1.4426950408889634
VMEM_BYTES = 32 * 1024 * 1024
IN_VMEM = pl.BlockSpec(memory_space=pltpu.VMEM)
IN_SMEM = pl.BlockSpec(memory_space=pltpu.SMEM)
ANYWHERE = pl.BlockSpec(memory_space=pl.ANY)


def iota(shape, dim):
    return lax.broadcasted_iota(jnp.int32, shape, dim)


def scaled_norm(values, gain_row):
    mean_square = jnp.mean(values * values, axis=-1, keepdims=True)
    return (values * lax.rsqrt(mean_square + 1e-06) * gain_row).astype(jnp.bfloat16)


def layer(x, weights, length, bias):
    gain_ref, qkv_ref, out_ref = weights
    positions, features = x.shape
    head_size = features // HEADS
    width = GROUP * head_size
    groups = features // width
    values = x.astype(jnp.float32)
    normed = scaled_norm(values, gain_ref[...])
    own_lanes = [(lax.div(iota((1, width), 1), head_size) == h).astype(jnp.bfloat16) for h in range(GROUP)]
    ones = jnp.concatenate([jnp.broadcast_to(lanes, (length, width)) for lanes in own_lanes], axis=0)
    scale = head_size ** (-0.5) * LOG2_E

    def per_head(part):
        return jnp.concatenate([part * lanes for lanes in own_lanes], axis=0)

    def projections(g):
        return [
            jnp.dot(
                normed,
                qkv_ref[:, part * features + g * width : part * features + (g + 1) * width],
                preferred_element_type=jnp.float32,
            ).astype(jnp.bfloat16)
            for part in range(3)
        ]

    def attended(queries, key_rows, value_rows):
        scores = lax.dot_general(
            queries, per_head(key_rows), (((1,), (1,)), ((), ())), preferred_element_type=jnp.float32
        ) * scale
        grown = []
        for h in range(GROUP):
            own = scores[:, h * length : (h + 1) * length]
            if bias is not None:
                own = own + bias
            grown.append(jnp.exp2(own - jnp.max(own, axis=-1, keepdims=True)).astype(jnp.bfloat16))
        grown = jnp.concatenate(grown, axis=1)
        weighted = jnp.dot(grown, per_head(value_rows), preferred_element_type=jnp.float32)
        total = jnp.dot(grown, ones, preferred_element_type=jnp.float32)
        share = pl.reciprocal(total, approx=True)
        share = share * (2.0 - total * share)
        return (weighted * share).astype(jnp.bfloat16)

    contexts = []
    upcoming = projections(0)
    for g in range(groups):
        current, upcoming = upcoming, projections(g + 1) if g + 1 < groups else None
        blocks = [
            attended(*(part[start : start + length] for part in current)) for start in range(0, positions, length)
        ]
        contexts.append(blocks[0] if len(blocks) == 1 else jnp.concatenate(blocks, axis=0))
    context = jnp.concatenate(contexts, axis=1)
    return (values + jnp.dot(context, out_ref[...], preferred_element_type=jnp.float32)).astype(jnp.bfloat16)


def moved(hit, rows):
    one_hot = jnp.where(hit, 1.0, 0.0).astype(jnp.bfloat16)
    return jnp.dot(one_hot, rows, preferred_element_type=jnp.float32).astype(jnp.bfloat16)


def digits(place, *sizes):
    found = []
    for size in reversed(sizes):
        found.append(lax.rem(place, size))
        place = lax.div(place, size)
    return [place] + found[::-1]


def ranks(owner_row):
    img_rows = owner_row.shape[1]
    square = (img_rows, img_rows)
    across = jnp.broadcast_to(owner_row, square).astype(jnp.float32)
    down = across.T
    before = (down < across) | ((down == across) & (iota(square, 0) < iota(square, 1)))
    return jnp.sum(before.astype(jnp.float32), axis=0, keepdims=True).astype(jnp.int32)


def spread_rows(y, rank, my_core, dims):
    rows, _, _, strides, _, peers = dims
    chunks = strides // peers
    positions, img_rows = y.shape[0], rank.shape[1]
    lines_dev = positions // img_rows
    shape = (positions, img_rows)
    core, group, chunk, line, i = digits(iota(shape, 0), peers // CORES, chunks, lines_dev, rows)
    core = lax.rem(core + my_core, CORES)
    hit = (i * strides + chunk * peers + group * CORES + core) == rank
    return moved(jnp.concatenate([hit & (line == own) for own in range(lines_dev)], axis=1), y)


def column_kernel(dims, turn_places, flag_ref, order_ref, frames_ref, owner_ref, gain_ref, qkv_ref, out_ref, *rest):
    mine_ref, other_ref = rest[-2:]

    @pl.when(flag_ref[0] == 0)
    def _():
        rank = ranks(owner_ref[...])
        for clip, turn_place in enumerate(turn_places):
            x = frames_ref[order_ref[turn_place]]
            y = layer(x, (gain_ref, qkv_ref, out_ref), owner_ref.shape[1], None)
            y = spread_rows(y, rank, lax.rem(flag_ref[1], CORES), dims)
            mine_ref[clip] = y[: y.shape[0] // CORES]
            other_ref[clip] = y[y.shape[0] // CORES :]


def merge_kernel(dims, clip, near, far, flag_ref, mine_ref, other_ref, *rest):
    rows, _, lines, strides, _, peers = dims
    groups, chunks = peers // CORES, strides // peers
    lines_dev = lines // peers
    part_refs = rest[near - far :]

    @pl.when(flag_ref[0] == 0)
    def _():
        both = jnp.concatenate([mine_ref[clip], other_ref[clip]], axis=0)
        size = both.shape[0] // groups
        shape = (size * (far - near), both.shape[0])
        my_core, my_group = lax.rem(flag_ref[1], CORES), lax.div(flag_ref[1], CORES)
        apart, chunk, core, inner = digits(iota(shape, 0) + near * size, chunks, CORES, lines_dev * rows)
        across, from_group, from_chunk, from_inner = digits(iota(shape, 1), groups, chunks, lines_dev * rows)
        from_core = lax.rem(across + my_core, CORES)
        hit = (
            ((apart ^ my_group) == from_group)
            & (chunk == from_chunk)
            & (core == from_core)
            & (inner == from_inner)
        )
        sent = moved(hit, both)
        for d, part_ref in enumerate(part_refs):
            part_ref[...] = sent[d * size : (d + 1) * size]


def gate_kernel(*refs):
    refs[-1][0] = 0


def gathered_chunk(part_refs, chunk, chunks, me, dims):
    rows, _, lines, strides, _, peers = dims
    parts = jnp.concatenate([ref[...] for ref in part_refs], axis=0)
    shape = (lines * rows, parts.shape[0])
    inner_size = lines // (peers // CORES) * rows
    group, inner = digits(iota(shape, 0), inner_size)
    apart, from_chunk, from_inner = digits(iota(shape, 1), chunks, inner_size)
    my_group = lax.div(me, CORES)
    return moved(((group ^ my_group) == apart) & (from_chunk == chunk) & (from_inner == inner), parts)


def row_bias(section, length, rows, columns):
    query, key = iota((length, length), 0), iota((length, length), 1)
    same_row = lax.rem(query, rows) == lax.rem(key, rows)
    query_line, key_line = lax.div(query, rows), lax.div(key, rows)
    query_col, key_col = lax.rem(query_line, columns), lax.rem(key_line, columns)
    across_frames = query_col == key_col
    across_columns = (lax.div(query_line, columns) == lax.div(key_line, columns)) & (key_col <= query_col)
    first = jnp.broadcast_to(section == 1, (length, length))
    allowed = same_row & ((first & across_frames) | (~first & across_columns))
    return jnp.where(allowed, 0.0, -1e30)


def packed_rows(y, owner_row, chunk, me, dims):
    rows, _, lines, strides, most, peers = dims
    img_rows = owner_row.shape[1]
    shape = (peers * most * lines, img_rows)
    peer, n, line = digits(iota((shape[0], 1), 0), most, lines)
    owners = jnp.broadcast_to(owner_row, shape)
    start = jnp.sum((owners < peer).astype(jnp.float32), axis=1, keepdims=True).astype(jnp.int32)
    end = jnp.sum((owners <= peer).astype(jnp.float32), axis=1, keepdims=True).astype(jnp.int32)
    rank = start + lax.rem(chunk * peers + me - start + img_rows, strides) + strides * n
    from_line, i = digits(iota((1, shape[1]), 1), rows)
    return moved((lax.div(rank, strides) == i) & (line == from_line) & (rank < end), y)


def stored(y, y_refs):
    size = y.shape[0] // len(y_refs)
    for n, y_ref in enumerate(y_refs):
        y_ref[...] = y[n * size : (n + 1) * size]


def frame_kernel(dims, work, count, flag_ref, gain_ref, qkv_ref, out_ref, *refs):
    rows, columns, lines, strides, _, peers = dims
    piece_refs, y_refs = refs[: peers // CORES], refs[-count:]

    @pl.when(flag_ref[0] == 1)
    def _():
        parts = [gathered_chunk(piece_refs, chunk, strides // peers, flag_ref[1], dims) for chunk in work]
        x = jnp.concatenate(parts, axis=0)
        length = rows * lines
        bias = row_bias(flag_ref[0], length, rows, columns)
        stored(layer(x, (gain_ref, qkv_ref, out_ref), length, bias), y_refs)


def row_kernel(dims, tick, inputs, kept, count, flag_ref, gain_ref, qkv_ref, out_ref, *refs):
    rows, columns, lines, _, _, _ = dims
    x_refs, y_refs = refs[:inputs], refs[-count:]
    section = flag_ref[0]

    @pl.when((section > 1) & (section <= tick + 1))
    def _():
        x = jnp.concatenate([ref[...] for ref in x_refs], axis=0)
        length = rows * lines
        bias = row_bias(section, length, rows, columns)
        stored(layer(x, (gain_ref, qkv_ref, out_ref), length, bias), y_refs)

    @pl.when(section <= 1)
    def _():
        for from_ref, y_ref in zip(refs[inputs : inputs + kept] or x_refs, y_refs):
            y_ref[...] = from_ref[...]

    if kept and tick > 2:

        @pl.when(section == 0)
        def _():
            for x_ref, y_ref in zip(x_refs, y_refs):
                y_ref[...] = x_ref[...]


def final_kernel(dims, chunk, flag_ref, gain_ref, qkv_ref, out_ref, owner_ref, x_ref, held_ref, *rest):
    rows, columns, lines, _, _, _ = dims
    y_ref = rest[-1]
    section = flag_ref[0]

    def packed(value):
        y_ref[...] = packed_rows(value, owner_ref[...], chunk, flag_ref[1], dims)

    @pl.when(section > 2)
    def _():
        length = rows * lines
        packed(layer(x_ref[...], (gain_ref, qkv_ref, out_ref), length, row_bias(section, length, rows, columns)))

    @pl.when(section == 2)
    def _():
        packed(x_ref[...])

    @pl.when(section < 2)
    def _():
        packed(held_ref[...])


def cost(positions, features):
    return pl.CostEstimate(flops=10**10, bytes_accessed=positions * features, transcendentals=0)


def in_vmem(arrays):
    return [pltpu.with_memory_space_constraint(a, pltpu.VMEM) for a in arrays]


def load_kernel(*refs):
    count = len(refs) // 3
    copies = [
        pltpu.make_async_copy(refs[i], refs[count + i], refs[2 * count + i]) for i in range(count)
    ]
    for copy in copies:
        copy.start()
    for copy in copies:
        copy.wait()


def loaded(arrays):
    return pl.pallas_call(
        load_kernel,
        out_shape=[pltpu.VMEM(a.shape, a.dtype) for a in arrays],
        in_specs=[pl.BlockSpec(memory_space=pltpu.HBM) for _ in arrays],
        out_specs=[IN_VMEM for _ in arrays],
        scratch_shapes=[pltpu.SemaphoreType.DMA for _ in arrays],
        compiler_params=pltpu.CompilerParams(vmem_limit_bytes=1024 * 1024),
        name="loaded",
    )(*(pltpu.with_memory_space_constraint(a, pltpu.HBM) for a in arrays))


def options():
    return pltpu.CompilerParams(vmem_limit_bytes=VMEM_BYTES)


def column_pass(place, order, frames, owner_row, weights, dims, turn_places, after):
    _, positions, features = frames.shape
    half = pltpu.VMEM((len(turn_places), positions // CORES, features), jnp.bfloat16)
    return pl.pallas_call(
        functools.partial(column_kernel, dims, turn_places),
        out_shape=[half, half],
        in_specs=[IN_SMEM] * 2 + [IN_VMEM] * 5 + [ANYWHERE] * len(after),
        out_specs=[IN_VMEM] * 2,
        compiler_params=options(),
        cost_estimate=cost(positions, features),
        name="column_pass",
    )(place, order, *in_vmem([frames]), owner_row, *in_vmem(weights), *after)


def merge(place, mine, other, dims, clip, near, far, after):
    _, positions, features = mine.shape
    groups = dims[-1] // CORES
    part = pltpu.VMEM((CORES * positions // groups, features), jnp.bfloat16)
    return pl.pallas_call(
        functools.partial(merge_kernel, dims, clip, near, far),
        out_shape=[part] * (far - near),
        in_specs=[IN_SMEM] + [IN_VMEM] * 2 + [ANYWHERE] * len(after),
        out_specs=[IN_VMEM] * (far - near),
        compiler_params=options(),
        cost_estimate=cost(positions, features),
        name="merge",
    )(place, *in_vmem([mine, other]), *after)


def gate(arrays):
    return pl.pallas_call(
        gate_kernel,
        out_shape=jax.ShapeDtypeStruct((1,), jnp.int32),
        in_specs=[ANYWHERE] * len(arrays),
        out_specs=IN_SMEM,
        compiler_params=options(),
        cost_estimate=cost(1, 1),
        name="gate",
    )(*arrays)


def frame_pass(place, pieces, weights, dims, work, count, after):
    positions, features = dims[0] * dims[2] * len(work) // count, pieces[0].shape[1]
    return pl.pallas_call(
        functools.partial(frame_kernel, dims, work, count),
        out_shape=[pltpu.VMEM((positions, features), jnp.bfloat16)] * count,
        in_specs=[IN_SMEM] + [IN_VMEM] * (3 + len(pieces)) + [ANYWHERE] * len(after),
        out_specs=[IN_VMEM] * count,
        compiler_params=options(),
        cost_estimate=cost(positions, features),
        name="frame_pass",
    )(place, *in_vmem([*weights, *pieces]), *after)


def row_pass(place, x, y, weights, dims, tick, after):
    count, features = len(y) or len(x), x[0].shape[1]
    positions = sum(a.shape[0] for a in x) // count
    return pl.pallas_call(
        functools.partial(row_kernel, dims, tick, len(x), len(y), count),
        out_shape=[pltpu.VMEM((positions, features), jnp.bfloat16)] * count,
        in_specs=[IN_SMEM] + [IN_VMEM] * (3 + len(x) + len(y)) + [ANYWHERE] * len(after),
        out_specs=[IN_VMEM] * count,
        compiler_params=options(),
        cost_estimate=cost(positions, features),
        name="row_pass",
    )(place, *in_vmem([*weights, *x, *y]), *after)


def final_pass(place, x, held, owner_row, weights, dims, chunk, after):
    positions, features = x.shape
    _, _, lines, _, most, peers = dims
    return pl.pallas_call(
        functools.partial(final_kernel, dims, chunk),
        out_shape=jax.ShapeDtypeStruct((peers * most * lines, features), jnp.bfloat16),
        in_specs=[IN_SMEM] + [IN_VMEM] * 6 + [ANYWHERE] * len(after),
        out_specs=IN_VMEM,
        compiler_params=options(),
        cost_estimate=cost(positions, features),
        name="final_pass",
    )(place, *in_vmem(weights), owner_row, *in_vmem([x, held]), *after)


def settle_kernel(dims, max_rows, flag_ref, owner_ref, *refs):
    rows, columns, lines, strides, most, peers = dims
    out_ref = refs[-1]
    parts = jnp.concatenate([ref[...] for ref in refs[:-1]], axis=0)
    shape = (out_ref.shape[0], parts.shape[0])
    start = jnp.sum((owner_ref[...] < flag_ref[1]).astype(jnp.float32), axis=1, keepdims=True).astype(jnp.int32)
    chunk, peer, n, line = digits(iota((1, shape[1]), 1), peers, most, lines)
    slot = lax.rem(chunk * peers + peer - start + owner_ref.shape[1], strides) + strides * n
    out_line, out_slot = digits(iota((shape[0], 1), 0), max_rows)
    out_ref[...] = moved((slot == out_slot) & (line == out_line), parts)


def settle(place, owner_row, parts, dims, max_rows):
    rows, features = dims[2] * max_rows, parts[0].shape[1]
    return pl.pallas_call(
        functools.partial(settle_kernel, dims, max_rows),
        out_shape=jax.ShapeDtypeStruct((rows, features), jnp.bfloat16),
        in_specs=[IN_SMEM] + [IN_VMEM] * (1 + len(parts)),
        out_specs=IN_VMEM,
        compiler_params=options(),
        cost_estimate=cost(rows, features),
        name="settle",
    )(place, owner_row, *parts)


def swapped(x, peers):
    parts = x.reshape(peers, -1, x.shape[-1])
    return lax.all_to_all(parts, "seq", split_axis=0, concat_axis=0, tiled=True)


def local(frames_in, order, owner, qkv_weight, out_weight, gains):
    sections = lax.axis_size("section")
    peers = lax.axis_size("seq")
    section = lax.axis_index("section")
    me = lax.axis_index("seq")
    clips, lines_dev, img_rows, features = frames_in.shape
    lines = lines_dev * peers
    columns = lines // FRAMES
    max_rows = 2 * img_rows // peers
    chunks = lines_dev
    strides = peers * chunks
    rows = img_rows // strides
    most = -(-max_rows // strides)
    dims = (rows, columns, lines, strides, most, peers)
    owner_row = owner.reshape(1, img_rows)
    *weights, frames = loaded(
        [gains, qkv_weight[0], out_weight[0], frames_in.reshape(clips, lines_dev * img_rows, features)]
    )
    place = jnp.stack([section, me]).astype(jnp.int32)
    groups = peers // CORES

    homes = [1, 0, 2, 3]

    def column_clips(first, last, after):
        turn_places = [sections - 1 - home for home in homes[first:last]]
        mine, other = column_pass(place, order, frames, owner_row, weights, dims, turn_places, after)
        return mine, lax.ppermute(other, ("section", "seq"), [(p, p ^ 1) for p in range(peers)])

    def hop(halves, clip, near, far, after):
        parts = merge(place, *halves, dims, clip, near, far, after)
        return parts[0], [
            lax.ppermute(
                part,
                ("section", "seq"),
                [(p, peers + (p // CORES ^ d) * CORES + p % CORES) for p in range(peers)],
            )
            for d, part in enumerate(parts, near)
        ]

    def relay(parts, tick):
        pairs = []
        if tick == clips:
            pairs.append((0, 1))
        if 1 <= tick <= clips:
            pairs.append((1, 2))
        if 2 <= tick <= clips + 1:
            pairs.append((2, 3))
        if tick in (3, 4):
            pairs.append((3, 0))
        if tick == 5:
            pairs.append((3, 2))
        return [lax.ppermute(part, "section", pairs) for part in parts]

    all_chunks = list(range(chunks))
    middle = groups // 2
    sent, pieces = hop(column_clips(0, 1, []), 0, 0, groups, [])
    halves, y, held, ready = column_clips(1, clips, [sent]), [None] * chunks, [None] * chunks, []
    for tick in range(clips + sections - 3):
        if tick < clips - 1:
            awaited = pieces[:middle] if tick else pieces
            sent, upcoming = hop(halves, tick, 0, middle, [gate(awaited + ready)])
            sent, later = hop(halves, tick, middle, groups, [gate(pieces[middle:] + [sent])])
            ready = [sent]
        for chunk in all_chunks:
            fresh = frame_pass(place, pieces, weights, dims, [chunk], 1, ready) if tick < clips else []
            if tick:
                x = relay([y[chunk]], tick)
                fresh = row_pass(place, x, fresh, weights, dims, tick, ready)
                (held[chunk],) = x
            (y[chunk],) = fresh
            ready = [y[chunk]]
        if tick < clips - 1:
            pieces = upcoming + later
    for chunk in all_chunks:
        (x,) = relay([y[chunk]], clips + sections - 3)
        y[chunk] = final_pass(place, x, held[chunk], owner_row, weights, dims, chunk, ready)
        ready = [y[chunk]]
    arrived = [swapped(part, peers).reshape(-1, features) for part in y]
    return settle(place, owner_row, arrived, dims, max_rows).reshape(1, lines, max_rows, features)


def solution(mesh):
    placed = (
        P(None, "seq", None, None),
        P(),
        P(),
        P("section", None, None),
        P("section", None, None),
        P("section", None),
    )
    return jax.shard_map(
        local,
        mesh=mesh,
        in_specs=placed,
        out_specs=P("section", None, "seq", None),
        check_vma=False,
    )
```

```python
import functools

import jax
import jax.numpy as jnp
from jax import lax
from jax.experimental import pallas as pl
from jax.experimental.pallas import tpu as pltpu
from jax.sharding import PartitionSpec as P

HEADS = 16
FRAMES = 4
GROUP = 4
CORES = 2
LOG2_E = 1.4426950408889634
VMEM_BYTES = 32 * 1024 * 1024
IN_VMEM = pl.BlockSpec(memory_space=pltpu.VMEM)
IN_SMEM = pl.BlockSpec(memory_space=pltpu.SMEM)
ANYWHERE = pl.BlockSpec(memory_space=pl.ANY)


def iota(shape, dim):
    return lax.broadcasted_iota(jnp.int32, shape, dim)


def scaled_norm(values, gain_row):
    mean_square = jnp.mean(values * values, axis=-1, keepdims=True)
    return (values * lax.rsqrt(mean_square + 1e-06) * gain_row).astype(jnp.bfloat16)


def layer(x, weights, length, bias, ready=lambda step: None):
    gain_ref, qkv_ref, out_ref = weights
    positions, features = x.shape
    head_size = features // HEADS
    width = GROUP * head_size
    groups = features // width
    values = x.astype(jnp.float32)
    normed = scaled_norm(values, gain_ref[...])
    own_lanes = [(lax.div(iota((1, width), 1), head_size) == h).astype(jnp.bfloat16) for h in range(GROUP)]
    ones = jnp.concatenate([jnp.broadcast_to(lanes, (length, width)) for lanes in own_lanes], axis=0)
    scale = head_size ** (-0.5) * LOG2_E

    def per_head(part):
        return jnp.concatenate([part * lanes for lanes in own_lanes], axis=0)

    def projections(g):
        ready(g)
        return [
            jnp.dot(
                normed,
                qkv_ref[:, part * features + g * width : part * features + (g + 1) * width],
                preferred_element_type=jnp.float32,
            ).astype(jnp.bfloat16)
            for part in range(3)
        ]

    def attended(queries, key_rows, value_rows):
        scores = lax.dot_general(
            queries, per_head(key_rows), (((1,), (1,)), ((), ())), preferred_element_type=jnp.float32
        ) * scale
        grown = []
        for h in range(GROUP):
            own = scores[:, h * length : (h + 1) * length]
            if bias is not None:
                own = own + bias
            grown.append(jnp.exp2(own - jnp.max(own, axis=-1, keepdims=True)).astype(jnp.bfloat16))
        grown = jnp.concatenate(grown, axis=1)
        weighted = jnp.dot(grown, per_head(value_rows), preferred_element_type=jnp.float32)
        total = jnp.dot(grown, ones, preferred_element_type=jnp.float32)
        share = pl.reciprocal(total, approx=True)
        share = share * (2.0 - total * share)
        return (weighted * share).astype(jnp.bfloat16)

    contexts = []
    upcoming = projections(0)
    for g in range(groups):
        current, upcoming = upcoming, projections(g + 1) if g + 1 < groups else None
        blocks = [
            attended(*(part[start : start + length] for part in current)) for start in range(0, positions, length)
        ]
        contexts.append(blocks[0] if len(blocks) == 1 else jnp.concatenate(blocks, axis=0))
    context = jnp.concatenate(contexts, axis=1)
    ready(groups)
    return (values + jnp.dot(context, out_ref[...], preferred_element_type=jnp.float32)).astype(jnp.bfloat16)


def moved(hit, rows):
    one_hot = jnp.where(hit, 1.0, 0.0).astype(jnp.bfloat16)
    return jnp.dot(one_hot, rows, preferred_element_type=jnp.float32).astype(jnp.bfloat16)


def digits(place, *sizes):
    found = []
    for size in reversed(sizes):
        found.append(lax.rem(place, size))
        place = lax.div(place, size)
    return [place] + found[::-1]


def ranks(owner_row):
    img_rows = owner_row.shape[1]
    square = (img_rows, img_rows)
    across = jnp.broadcast_to(owner_row, square).astype(jnp.float32)
    down = across.T
    before = (down < across) | ((down == across) & (iota(square, 0) < iota(square, 1)))
    return jnp.sum(before.astype(jnp.float32), axis=0, keepdims=True).astype(jnp.int32)


def spread_rows(y, rank, my_core, dims):
    rows, _, _, strides, _, peers = dims
    chunks = strides // peers
    positions, img_rows = y.shape[0], rank.shape[1]
    lines_dev = positions // img_rows
    shape = (positions, img_rows)
    core, group, chunk, line, i = digits(iota(shape, 0), peers // CORES, chunks, lines_dev, rows)
    core = lax.rem(core + my_core, CORES)
    hit = (i * strides + chunk * peers + group * CORES + core) == rank
    return moved(jnp.concatenate([hit & (line == own) for own in range(lines_dev)], axis=1), y)


def fetches(from_refs, to_refs, sems):
    (from_gain, from_qkv, from_out), (to_gain, to_qkv, to_out) = from_refs, to_refs
    features = from_out.shape[0]
    width = GROUP * features // HEADS
    groups = features // width
    steps = []
    for g in range(groups):
        places = [pl.ds(part * features + g * width, width) for part in range(3)]
        steps.append([(from_qkv.at[:, place], to_qkv.at[:, place]) for place in places])
    steps.append([(from_out, to_out)])
    steps[0].append((from_gain, to_gain))
    return [
        [pltpu.make_async_copy(source, target, sems.at[step, n]) for n, (source, target) in enumerate(pairs)]
        for step, pairs in enumerate(steps)
    ]


def wait_all(copies):
    for copy in copies:
        copy.wait()


def first_kernel(dims, turn_place, flag_ref, order_ref, owner_ref, *refs):
    from_refs, (mine_ref, other_ref), to_refs = refs[:4], refs[4:6], refs[6:10]
    sems, clip_sems = refs[10:]
    clips = from_refs[3].shape[0]
    steps = fetches(from_refs[:3], to_refs[:3], sems)
    places = [lax.rem(order_ref[turn_place] + n, clips) for n in range(clips)]
    frames = [
        pltpu.make_async_copy(from_refs[3].at[place], to_refs[3].at[place], clip_sems.at[n])
        for n, place in enumerate(places)
    ]
    gain = steps[0].pop()
    for copy in [gain, frames[0], *sum(steps, []), *frames[1:]]:
        copy.start()
    wait_all([gain, frames[0]])

    @pl.when(flag_ref[0] == 0)
    def _():
        y = layer(
            to_refs[3][places[0]], to_refs[:3], owner_ref.shape[1], None, lambda step: wait_all(steps[step])
        )
        y = spread_rows(y, ranks(owner_ref[...]), lax.rem(flag_ref[1], CORES), dims)
        mine_ref[0] = y[: y.shape[0] // CORES]
        other_ref[0] = y[y.shape[0] // CORES :]

    @pl.when(flag_ref[0] != 0)
    def _():
        wait_all(sum(steps, []))

    wait_all(frames[1:])


def column_kernel(dims, turn_places, flag_ref, order_ref, frames_ref, owner_ref, gain_ref, qkv_ref, out_ref, *rest):
    mine_ref, other_ref = rest[-2:]

    @pl.when(flag_ref[0] == 0)
    def _():
        rank = ranks(owner_ref[...])
        for clip, turn_place in enumerate(turn_places):
            x = frames_ref[order_ref[turn_place]]
            y = layer(x, (gain_ref, qkv_ref, out_ref), owner_ref.shape[1], None)
            y = spread_rows(y, rank, lax.rem(flag_ref[1], CORES), dims)
            mine_ref[clip] = y[: y.shape[0] // CORES]
            other_ref[clip] = y[y.shape[0] // CORES :]


def merge_kernel(dims, clip, flag_ref, mine_ref, other_ref, *rest):
    rows, _, lines, strides, _, peers = dims
    groups, chunks = peers // CORES, strides // peers
    lines_dev = lines // peers
    part_refs, (both, sems) = rest[-groups - 2 : -2], rest[-2:]

    @pl.when(flag_ref[0] == 0)
    def _():
        half = mine_ref.shape[1]
        copies = [
            pltpu.make_async_copy(ref.at[clip], both.at[pl.ds(n * half, half)], sems.at[n])
            for n, ref in enumerate((mine_ref, other_ref))
        ]
        for copy in copies:
            copy.start()
        size = CORES * half
        shape = (size, size)
        my_core, my_group = lax.rem(flag_ref[1], CORES), lax.div(flag_ref[1], CORES)
        apart, chunk, core, inner = digits(iota(shape, 0), chunks, CORES, lines_dev * rows)
        far, from_group, from_chunk, from_inner = digits(iota(shape, 1), groups, chunks, lines_dev * rows)
        from_core = lax.rem(far + my_core, CORES)
        hit = (
            ((apart ^ my_group) == from_group)
            & (chunk == from_chunk)
            & (core == from_core)
            & (inner == from_inner)
        )
        size = size // groups
        wait_all(copies)
        sent = moved(hit, both[...])
        for d, part_ref in enumerate(part_refs):
            part_ref[...] = sent[d * size : (d + 1) * size]


def gate_kernel(*refs):
    refs[-1][0] = 0


def gathered_chunk(part_refs, chunk, chunks, me, dims):
    rows, _, lines, strides, _, peers = dims
    parts = jnp.concatenate([ref[...] for ref in part_refs], axis=0)
    shape = (lines * rows, parts.shape[0])
    inner_size = lines // (peers // CORES) * rows
    group, inner = digits(iota(shape, 0), inner_size)
    apart, from_chunk, from_inner = digits(iota(shape, 1), chunks, inner_size)
    my_group = lax.div(me, CORES)
    return moved(((group ^ my_group) == apart) & (from_chunk == chunk) & (from_inner == inner), parts)


def row_bias(section, length, rows, columns):
    query, key = iota((length, length), 0), iota((length, length), 1)
    same_row = lax.rem(query, rows) == lax.rem(key, rows)
    query_line, key_line = lax.div(query, rows), lax.div(key, rows)
    query_col, key_col = lax.rem(query_line, columns), lax.rem(key_line, columns)
    across_frames = query_col == key_col
    across_columns = (lax.div(query_line, columns) == lax.div(key_line, columns)) & (key_col <= query_col)
    first = jnp.broadcast_to(section == 1, (length, length))
    allowed = same_row & ((first & across_frames) | (~first & across_columns))
    return jnp.where(allowed, 0.0, -1e30)


def packed_rows(y, owner_row, chunk, me, dims):
    rows, _, lines, strides, most, peers = dims
    img_rows = owner_row.shape[1]
    shape = (peers * most * lines, img_rows)
    peer, n, line = digits(iota((shape[0], 1), 0), most, lines)
    owners = jnp.broadcast_to(owner_row, shape)
    start = jnp.sum((owners < peer).astype(jnp.float32), axis=1, keepdims=True).astype(jnp.int32)
    end = jnp.sum((owners <= peer).astype(jnp.float32), axis=1, keepdims=True).astype(jnp.int32)
    rank = start + lax.rem(chunk * peers + me - start + img_rows, strides) + strides * n
    from_line, i = digits(iota((1, shape[1]), 1), rows)
    return moved((lax.div(rank, strides) == i) & (line == from_line) & (rank < end), y)


def stored(y, y_refs):
    size = y.shape[0] // len(y_refs)
    for n, y_ref in enumerate(y_refs):
        y_ref[...] = y[n * size : (n + 1) * size]


def frame_kernel(dims, work, count, flag_ref, gain_ref, qkv_ref, out_ref, *refs):
    rows, columns, lines, strides, _, peers = dims
    piece_refs, y_refs = refs[: peers // CORES], refs[-count:]

    @pl.when(flag_ref[0] == 1)
    def _():
        parts = [gathered_chunk(piece_refs, chunk, strides // peers, flag_ref[1], dims) for chunk in work]
        x = jnp.concatenate(parts, axis=0)
        length = rows * lines
        bias = row_bias(flag_ref[0], length, rows, columns)
        stored(layer(x, (gain_ref, qkv_ref, out_ref), length, bias), y_refs)


def row_kernel(dims, tick, inputs, kept, count, flag_ref, gain_ref, qkv_ref, out_ref, *refs):
    rows, columns, lines, _, _, _ = dims
    x_refs, y_refs = refs[:inputs], refs[-count:]
    section = flag_ref[0]

    @pl.when((section > 1) & (section <= tick + 1))
    def _():
        x = jnp.concatenate([ref[...] for ref in x_refs], axis=0)
        length = rows * lines
        bias = row_bias(section, length, rows, columns)
        stored(layer(x, (gain_ref, qkv_ref, out_ref), length, bias), y_refs)

    @pl.when(section <= 1)
    def _():
        for from_ref, y_ref in zip(refs[inputs : inputs + kept] or x_refs, y_refs):
            y_ref[...] = from_ref[...]

    if kept and tick > 2:

        @pl.when(section == 0)
        def _():
            for x_ref, y_ref in zip(x_refs, y_refs):
                y_ref[...] = x_ref[...]


def final_kernel(dims, chunk, streamed, flag_ref, gain_ref, qkv_ref, out_ref, owner_ref, x_ref, held_ref, *rest):
    rows, columns, lines, _, _, _ = dims
    y_ref = rest[-5] if streamed else rest[-1]
    section = flag_ref[0]
    weights = (gain_ref, qkv_ref, out_ref)

    def packed(value):
        y_ref[...] = packed_rows(value, owner_ref[...], chunk, flag_ref[1], dims)

    @pl.when(section > 2)
    def _():
        length = rows * lines
        bias = row_bias(section, length, rows, columns)
        if streamed:
            here, sems = rest[-4:-1], rest[-1]
            steps = fetches(weights, here, sems)
            for copy in sum(steps, []):
                copy.start()
            gain = steps[0].pop()
            gain.wait()
            packed(layer(x_ref[...], here, length, bias, lambda step: wait_all(steps[step])))
        else:
            packed(layer(x_ref[...], weights, length, bias))

    @pl.when(section == 2)
    def _():
        packed(x_ref[...])

    @pl.when(section < 2)
    def _():
        packed(held_ref[...])


def cost(positions, features):
    return pl.CostEstimate(flops=10**10, bytes_accessed=positions * features, transcendentals=0)


def in_hbm(arrays):
    return [pltpu.with_memory_space_constraint(a, pltpu.HBM) for a in arrays]


def in_vmem(arrays):
    return [pltpu.with_memory_space_constraint(a, pltpu.VMEM) for a in arrays]


def options():
    return pltpu.CompilerParams(vmem_limit_bytes=VMEM_BYTES)


def first_pass(place, order, owner_row, arrays, dims, turn_place):
    _, positions, features = arrays[-1].shape
    half = pltpu.VMEM((1, positions // CORES, features), jnp.bfloat16)
    return pl.pallas_call(
        functools.partial(first_kernel, dims, turn_place),
        out_shape=[half, half] + [pltpu.VMEM(a.shape, a.dtype) for a in arrays],
        in_specs=[IN_SMEM] * 2 + [IN_VMEM] + [pl.BlockSpec(memory_space=pltpu.HBM)] * len(arrays),
        out_specs=[IN_VMEM] * (2 + len(arrays)),
        scratch_shapes=[
            pltpu.SemaphoreType.DMA((HEADS // GROUP + 1, 4)),
            pltpu.SemaphoreType.DMA((arrays[-1].shape[0],)),
        ],
        compiler_params=options(),
        cost_estimate=cost(positions, features),
        name="first_pass",
    )(place, order, owner_row, *in_hbm(arrays))


def column_pass(place, order, frames, owner_row, weights, dims, turn_places, after):
    _, positions, features = frames.shape
    half = pltpu.VMEM((len(turn_places), positions // CORES, features), jnp.bfloat16)
    return pl.pallas_call(
        functools.partial(column_kernel, dims, turn_places),
        out_shape=[half, half],
        in_specs=[IN_SMEM] * 2 + [IN_VMEM] * 5 + [ANYWHERE] * len(after),
        out_specs=[IN_VMEM] * 2,
        compiler_params=options(),
        cost_estimate=cost(positions, features),
        name="column_pass",
    )(place, order, *in_vmem([frames]), owner_row, *in_vmem(weights), *after)


def merge(place, mine, other, dims, clip, after):
    _, positions, features = mine.shape
    groups = dims[-1] // CORES
    part = pltpu.VMEM((CORES * positions // groups, features), jnp.bfloat16)
    return pl.pallas_call(
        functools.partial(merge_kernel, dims, clip),
        out_shape=[part] * groups,
        in_specs=[IN_SMEM] + [ANYWHERE] * (2 + len(after)),
        out_specs=[IN_VMEM] * groups,
        scratch_shapes=[
            pltpu.VMEM((CORES * positions, features), jnp.bfloat16),
            pltpu.SemaphoreType.DMA((CORES,)),
        ],
        compiler_params=options(),
        cost_estimate=cost(positions, features),
        name="merge",
    )(place, mine, other, *after)


def gate(arrays):
    return pl.pallas_call(
        gate_kernel,
        out_shape=jax.ShapeDtypeStruct((1,), jnp.int32),
        in_specs=[ANYWHERE] * len(arrays),
        out_specs=IN_SMEM,
        compiler_params=options(),
        cost_estimate=cost(1, 1),
        name="gate",
    )(*arrays)


def frame_pass(place, pieces, weights, dims, work, count, after):
    positions, features = dims[0] * dims[2] * len(work) // count, pieces[0].shape[1]
    return pl.pallas_call(
        functools.partial(frame_kernel, dims, work, count),
        out_shape=[pltpu.VMEM((positions, features), jnp.bfloat16)] * count,
        in_specs=[IN_SMEM] + [IN_VMEM] * (3 + len(pieces)) + [ANYWHERE] * len(after),
        out_specs=[IN_VMEM] * count,
        compiler_params=options(),
        cost_estimate=cost(positions, features),
        name="frame_pass",
    )(place, *in_vmem([*weights, *pieces]), *after)


def row_pass(place, x, y, weights, dims, tick, after):
    count, features = len(y) or len(x), x[0].shape[1]
    positions = sum(a.shape[0] for a in x) // count
    return pl.pallas_call(
        functools.partial(row_kernel, dims, tick, len(x), len(y), count),
        out_shape=[pltpu.VMEM((positions, features), jnp.bfloat16)] * count,
        in_specs=[IN_SMEM] + [IN_VMEM] * (3 + len(x) + len(y)) + [ANYWHERE] * len(after),
        out_specs=[IN_VMEM] * count,
        compiler_params=options(),
        cost_estimate=cost(positions, features),
        name="row_pass",
    )(place, *in_vmem([*weights, *x, *y]), *after)


def final_pass(place, x, held, owner_row, weights, dims, chunk, streamed, after):
    positions, features = x.shape
    _, _, lines, _, most, peers = dims
    kind, scratch = IN_VMEM, []
    if streamed:
        kind = pl.BlockSpec(memory_space=pltpu.HBM)
        scratch = [pltpu.VMEM(a.shape, a.dtype) for a in weights]
        scratch.append(pltpu.SemaphoreType.DMA((HEADS // GROUP + 1, 4)))
    return pl.pallas_call(
        functools.partial(final_kernel, dims, chunk, streamed),
        out_shape=jax.ShapeDtypeStruct((peers * most * lines, features), jnp.bfloat16),
        in_specs=[IN_SMEM] + [kind] * 3 + [IN_VMEM] * 3 + [ANYWHERE] * len(after),
        out_specs=IN_VMEM,
        scratch_shapes=scratch,
        compiler_params=options(),
        cost_estimate=cost(positions, features),
        name="final_pass",
    )(place, *(in_hbm if streamed else in_vmem)(weights), owner_row, *in_vmem([x, held]), *after)


def settle_kernel(dims, max_rows, flag_ref, owner_ref, *refs):
    rows, columns, lines, strides, most, peers = dims
    out_ref = refs[-1]
    parts = jnp.concatenate([ref[...] for ref in refs[:-1]], axis=0)
    shape = (out_ref.shape[0], parts.shape[0])
    start = jnp.sum((owner_ref[...] < flag_ref[1]).astype(jnp.float32), axis=1, keepdims=True).astype(jnp.int32)
    chunk, peer, n, line = digits(iota((1, shape[1]), 1), peers, most, lines)
    slot = lax.rem(chunk * peers + peer - start + owner_ref.shape[1], strides) + strides * n
    out_line, out_slot = digits(iota((shape[0], 1), 0), max_rows)
    out_ref[...] = moved((slot == out_slot) & (line == out_line), parts)


def settle(place, owner_row, parts, dims, max_rows):
    rows, features = dims[2] * max_rows, parts[0].shape[1]
    return pl.pallas_call(
        functools.partial(settle_kernel, dims, max_rows),
        out_shape=jax.ShapeDtypeStruct((rows, features), jnp.bfloat16),
        in_specs=[IN_SMEM] + [IN_VMEM] * (1 + len(parts)),
        out_specs=IN_VMEM,
        compiler_params=options(),
        cost_estimate=cost(rows, features),
        name="settle",
    )(place, owner_row, *parts)


def swapped(x, peers):
    parts = x.reshape(peers, -1, x.shape[-1])
    return lax.all_to_all(parts, "seq", split_axis=0, concat_axis=0, tiled=True)


def local(frames_in, order, owner, qkv_weight, out_weight, gains):
    sections = lax.axis_size("section")
    peers = lax.axis_size("seq")
    section = lax.axis_index("section")
    me = lax.axis_index("seq")
    clips, lines_dev, img_rows, features = frames_in.shape
    lines = lines_dev * peers
    columns = lines // FRAMES
    max_rows = 2 * img_rows // peers
    chunks = lines_dev
    strides = peers * chunks
    rows = img_rows // strides
    most = -(-max_rows // strides)
    dims = (rows, columns, lines, strides, most, peers)
    owner_row = owner.reshape(1, img_rows)
    place = jnp.stack([section, me]).astype(jnp.int32)
    groups = peers // CORES

    homes = [1, 0, 2, 3]

    def across(half):
        return lax.ppermute(half, ("section", "seq"), [(p, p ^ 1) for p in range(peers)])

    stored_weights = [gains, qkv_weight[0], out_weight[0]]
    arrays = stored_weights + [frames_in.reshape(clips, lines_dev * img_rows, features)]
    mine, other, *weights, frames = first_pass(
        place, order, owner_row, arrays, dims, sections - 1 - homes[0]
    )

    def column_clips(first, last, after):
        turn_places = [sections - 1 - home for home in homes[first:last]]
        mine, other = column_pass(place, order, frames, owner_row, weights, dims, turn_places, after)
        return mine, across(other)

    def hop(halves, clip, after):
        parts = merge(place, *halves, dims, clip, after)
        return parts[0], [
            lax.ppermute(
                part,
                ("section", "seq"),
                [(p, peers + (p // CORES ^ d) * CORES + p % CORES) for p in range(peers)],
            )
            for d, part in enumerate(parts)
        ]

    def relay(parts, tick):
        pairs = []
        if tick == clips:
            pairs.append((0, 1))
        if 1 <= tick <= clips:
            pairs.append((1, 2))
        if 2 <= tick <= clips + 1:
            pairs.append((2, 3))
        if tick in (3, 4):
            pairs.append((3, 0))
        if tick == 5:
            pairs.append((3, 2))
        return [lax.ppermute(part, "section", pairs) for part in parts]

    all_chunks = list(range(chunks))
    sent, pieces = hop((mine, across(other)), 0, [])
    halves, y = column_clips(1, clips, [sent]), []
    for tick in range(clips - 1):
        sent, upcoming = hop(halves, tick, [*pieces, *y] if tick else [gate(pieces)])
        split = tick == clips - 2
        fresh = frame_pass(place, pieces, weights, dims, all_chunks, chunks if split else 1, [sent])
        y = row_pass(place, relay(y, tick), fresh, weights, dims, tick, []) if tick else fresh
        pieces = upcoming

    y, held, ready = list(y), [None] * chunks, [y[-1]]
    for tick in range(clips - 1, clips + sections - 3):
        for chunk in all_chunks:
            (x,) = relay([y[chunk]], tick)
            fresh = frame_pass(place, pieces, weights, dims, [chunk], 1, ready) if tick < clips else []
            (y[chunk],) = row_pass(place, [x], fresh, weights, dims, tick, ready)
            held[chunk], ready = x, [y[chunk]]
    for chunk in all_chunks:
        (x,) = relay([y[chunk]], clips + sections - 3)
        streamed = chunk > 0
        y[chunk] = final_pass(
            place,
            x,
            held[chunk],
            owner_row,
            stored_weights if streamed else weights,
            dims,
            chunk,
            streamed,
            ready,
        )
        ready = [y[chunk]]
    arrived = [swapped(part, peers).reshape(-1, features) for part in y]
    return settle(place, owner_row, arrived, dims, max_rows).reshape(1, lines, max_rows, features)


def solution(mesh):
    placed = (
        P(None, "seq", None, None),
        P(),
        P(),
        P("section", None, None),
        P("section", None, None),
        P("section", None),
    )
    return jax.shard_map(
        local,
        mesh=mesh,
        in_specs=placed,
        out_specs=P("section", None, "seq", None),
        check_vma=False,
    )
```

```python
import functools

import jax
import jax.numpy as jnp
from jax import lax
from jax.experimental import pallas as pl
from jax.experimental.pallas import tpu as pltpu
from jax.sharding import PartitionSpec as P

HEADS = 16
FRAMES = 4
GROUP = 4
PAIR = 2
CORES = 2
LOG2_E = 1.4426950408889634
VMEM_BYTES = 32 * 1024 * 1024
IN_VMEM = pl.BlockSpec(memory_space=pltpu.VMEM)
IN_SMEM = pl.BlockSpec(memory_space=pltpu.SMEM)
ANYWHERE = pl.BlockSpec(memory_space=pl.ANY)


def iota(shape, dim):
    return lax.broadcasted_iota(jnp.int32, shape, dim)


def scaled_norm(values, gain_row):
    mean_square = jnp.mean(values * values, axis=-1, keepdims=True)
    return (values * lax.rsqrt(mean_square + 1e-06) * gain_row).astype(jnp.bfloat16)


def layer(x, weights, length, bias, ready=lambda step: None):
    gain_ref, qkv_ref, out_ref = weights
    positions, features = x.shape
    head_size = features // HEADS
    width = GROUP * head_size
    groups = features // width
    values = x.astype(jnp.float32)
    normed = scaled_norm(values, gain_ref[...])
    lanes = PAIR * head_size
    own_lanes = [(lax.div(iota((1, lanes), 1), head_size) == h).astype(jnp.bfloat16) for h in range(PAIR)]
    ones = jnp.concatenate([jnp.broadcast_to(own, (length, lanes)) for own in own_lanes], axis=0)
    scale = head_size ** (-0.5) * LOG2_E

    def per_head(part):
        return jnp.concatenate([part * own for own in own_lanes], axis=0)

    def projections(g):
        ready(g)
        return [
            jnp.dot(
                normed,
                qkv_ref[:, part * features + g * width : part * features + (g + 1) * width],
                preferred_element_type=jnp.float32,
            ).astype(jnp.bfloat16)
            for part in range(3)
        ]

    def attended(queries, key_rows, value_rows):
        scores = lax.dot_general(
            queries, per_head(key_rows), (((1,), (1,)), ((), ())), preferred_element_type=jnp.float32
        ) * scale
        grown = []
        for h in range(PAIR):
            own = scores[:, h * length : (h + 1) * length]
            if bias is not None:
                own = own + bias
            grown.append(jnp.exp2(own - jnp.max(own, axis=-1, keepdims=True)).astype(jnp.bfloat16))
        grown = jnp.concatenate(grown, axis=1)
        summed = jnp.concatenate([per_head(value_rows), ones], axis=1)
        weighted, total = jnp.split(jnp.dot(grown, summed, preferred_element_type=jnp.float32), 2, axis=1)
        share = pl.reciprocal(total, approx=True)
        share = share * (2.0 - total * share)
        return (weighted * share).astype(jnp.bfloat16)

    contexts = []
    upcoming = projections(0)
    for g in range(groups):
        current, upcoming = upcoming, projections(g + 1) if g + 1 < groups else None
        for first in range(0, width, lanes):
            blocks = [
                attended(*(part[start : start + length, first : first + lanes] for part in current))
                for start in range(0, positions, length)
            ]
            contexts.append(blocks[0] if len(blocks) == 1 else jnp.concatenate(blocks, axis=0))
    context = jnp.concatenate(contexts, axis=1)
    ready(groups)
    return (values + jnp.dot(context, out_ref[...], preferred_element_type=jnp.float32)).astype(jnp.bfloat16)


def moved(hit, rows):
    one_hot = jnp.where(hit, 1.0, 0.0).astype(jnp.bfloat16)
    return jnp.dot(one_hot, rows, preferred_element_type=jnp.float32).astype(jnp.bfloat16)


def digits(place, *sizes):
    found = []
    for size in reversed(sizes):
        found.append(lax.rem(place, size))
        place = lax.div(place, size)
    return [place] + found[::-1]


def ranks(owner_row):
    img_rows = owner_row.shape[1]
    square = (img_rows, img_rows)
    across = jnp.broadcast_to(owner_row, square).astype(jnp.float32)
    down = across.T
    before = (down < across) | ((down == across) & (iota(square, 0) < iota(square, 1)))
    return jnp.sum(before.astype(jnp.float32), axis=0, keepdims=True).astype(jnp.int32)


def spread_rows(y, rank, my_core, dims):
    rows, _, _, strides, _, peers = dims
    chunks = strides // peers
    positions, img_rows = y.shape[0], rank.shape[1]
    lines_dev = positions // img_rows
    shape = (positions, img_rows)
    core, group, chunk, line, i = digits(iota(shape, 0), peers // CORES, chunks, lines_dev, rows)
    core = lax.rem(core + my_core, CORES)
    hit = (i * strides + chunk * peers + group * CORES + core) == rank
    return moved(jnp.concatenate([hit & (line == own) for own in range(lines_dev)], axis=1), y)


def fetches(from_refs, to_refs, sems):
    (from_gain, from_qkv, from_out), (to_gain, to_qkv, to_out) = from_refs, to_refs
    features = from_out.shape[0]
    width = GROUP * features // HEADS
    groups = features // width
    steps = []
    for g in range(groups):
        places = [pl.ds(part * features + g * width, width) for part in range(3)]
        steps.append([(from_qkv.at[:, place], to_qkv.at[:, place]) for place in places])
    steps.append([(from_out, to_out)])
    steps[0].append((from_gain, to_gain))
    return [
        [pltpu.make_async_copy(source, target, sems.at[step, n]) for n, (source, target) in enumerate(pairs)]
        for step, pairs in enumerate(steps)
    ]


def wait_all(copies):
    for copy in copies:
        copy.wait()


def first_kernel(dims, turn_place, flag_ref, order_ref, owner_ref, *refs):
    from_refs, (mine_ref, other_ref), to_refs = refs[:4], refs[4:6], refs[6:10]
    sems, clip_sems = refs[10:]
    clips = from_refs[3].shape[0]
    steps = fetches(from_refs[:3], to_refs[:3], sems)
    places = [lax.rem(order_ref[turn_place] + n, clips) for n in range(clips)]
    frames = [
        pltpu.make_async_copy(from_refs[3].at[place], to_refs[3].at[place], clip_sems.at[n])
        for n, place in enumerate(places)
    ]
    gain = steps[0].pop()
    for copy in [gain, frames[0], *sum(steps, []), *frames[1:]]:
        copy.start()
    wait_all([gain, frames[0]])

    @pl.when(flag_ref[0] == 0)
    def _():
        y = layer(
            to_refs[3][places[0]], to_refs[:3], owner_ref.shape[1], None, lambda step: wait_all(steps[step])
        )
        y = spread_rows(y, ranks(owner_ref[...]), lax.rem(flag_ref[1], CORES), dims)
        mine_ref[0] = y[: y.shape[0] // CORES]
        other_ref[0] = y[y.shape[0] // CORES :]

    @pl.when(flag_ref[0] != 0)
    def _():
        wait_all(sum(steps, []))

    wait_all(frames[1:])


def column_kernel(dims, turn_places, flag_ref, order_ref, frames_ref, owner_ref, gain_ref, qkv_ref, out_ref, *rest):
    mine_ref, other_ref = rest[-2:]

    @pl.when(flag_ref[0] == 0)
    def _():
        rank = ranks(owner_ref[...])
        for clip, turn_place in enumerate(turn_places):
            x = frames_ref[order_ref[turn_place]]
            y = layer(x, (gain_ref, qkv_ref, out_ref), owner_ref.shape[1], None)
            y = spread_rows(y, rank, lax.rem(flag_ref[1], CORES), dims)
            mine_ref[clip] = y[: y.shape[0] // CORES]
            other_ref[clip] = y[y.shape[0] // CORES :]


def merge_kernel(dims, clip, flag_ref, mine_ref, other_ref, *rest):
    rows, _, lines, strides, _, peers = dims
    groups, chunks = peers // CORES, strides // peers
    lines_dev = lines // peers
    part_refs, (both, sems) = rest[-groups - 2 : -2], rest[-2:]

    @pl.when(flag_ref[0] == 0)
    def _():
        half = mine_ref.shape[1]
        copies = [
            pltpu.make_async_copy(ref.at[clip], both.at[pl.ds(n * half, half)], sems.at[n])
            for n, ref in enumerate((mine_ref, other_ref))
        ]
        for copy in copies:
            copy.start()
        size = CORES * half
        shape = (size, size)
        my_core, my_group = lax.rem(flag_ref[1], CORES), lax.div(flag_ref[1], CORES)
        apart, chunk, core, inner = digits(iota(shape, 0), chunks, CORES, lines_dev * rows)
        far, from_group, from_chunk, from_inner = digits(iota(shape, 1), groups, chunks, lines_dev * rows)
        from_core = lax.rem(far + my_core, CORES)
        hit = (
            ((apart ^ my_group) == from_group)
            & (chunk == from_chunk)
            & (core == from_core)
            & (inner == from_inner)
        )
        size = size // groups
        wait_all(copies)
        sent = moved(hit, both[...])
        for d, part_ref in enumerate(part_refs):
            part_ref[...] = sent[d * size : (d + 1) * size]


def gate_kernel(*refs):
    refs[-1][0] = 0


def gathered_chunk(part_refs, chunk, chunks, me, dims):
    rows, _, lines, strides, _, peers = dims
    parts = jnp.concatenate([ref[...] for ref in part_refs], axis=0)
    shape = (lines * rows, parts.shape[0])
    inner_size = lines // (peers // CORES) * rows
    group, inner = digits(iota(shape, 0), inner_size)
    apart, from_chunk, from_inner = digits(iota(shape, 1), chunks, inner_size)
    my_group = lax.div(me, CORES)
    return moved(((group ^ my_group) == apart) & (from_chunk == chunk) & (from_inner == inner), parts)


def row_bias(section, length, rows, columns):
    query, key = iota((length, length), 0), iota((length, length), 1)
    same_row = lax.rem(query, rows) == lax.rem(key, rows)
    query_line, key_line = lax.div(query, rows), lax.div(key, rows)
    query_col, key_col = lax.rem(query_line, columns), lax.rem(key_line, columns)
    across_frames = query_col == key_col
    across_columns = (lax.div(query_line, columns) == lax.div(key_line, columns)) & (key_col <= query_col)
    first = jnp.broadcast_to(section == 1, (length, length))
    allowed = same_row & ((first & across_frames) | (~first & across_columns))
    return jnp.where(allowed, 0.0, -1e30)


def packed_rows(y, owner_row, chunk, me, dims):
    rows, _, lines, strides, most, peers = dims
    img_rows = owner_row.shape[1]
    shape = (peers * most * lines, img_rows)
    peer, n, line = digits(iota((shape[0], 1), 0), most, lines)
    owners = jnp.broadcast_to(owner_row, shape)
    start = jnp.sum((owners < peer).astype(jnp.float32), axis=1, keepdims=True).astype(jnp.int32)
    end = jnp.sum((owners <= peer).astype(jnp.float32), axis=1, keepdims=True).astype(jnp.int32)
    rank = start + lax.rem(chunk * peers + me - start + img_rows, strides) + strides * n
    from_line, i = digits(iota((1, shape[1]), 1), rows)
    return moved((lax.div(rank, strides) == i) & (line == from_line) & (rank < end), y)


def stored(y, y_refs):
    size = y.shape[0] // len(y_refs)
    for n, y_ref in enumerate(y_refs):
        y_ref[...] = y[n * size : (n + 1) * size]


def frame_kernel(dims, work, count, flag_ref, gain_ref, qkv_ref, out_ref, *refs):
    rows, columns, lines, strides, _, peers = dims
    piece_refs, y_refs = refs[: peers // CORES], refs[-count:]

    @pl.when(flag_ref[0] == 1)
    def _():
        parts = [gathered_chunk(piece_refs, chunk, strides // peers, flag_ref[1], dims) for chunk in work]
        x = jnp.concatenate(parts, axis=0)
        length = rows * lines
        bias = row_bias(flag_ref[0], length, rows, columns)
        stored(layer(x, (gain_ref, qkv_ref, out_ref), length, bias), y_refs)


def row_kernel(dims, tick, inputs, kept, count, flag_ref, gain_ref, qkv_ref, out_ref, *refs):
    rows, columns, lines, _, _, _ = dims
    x_refs, y_refs = refs[:inputs], refs[-count:]
    section = flag_ref[0]

    @pl.when((section > 1) & (section <= tick + 1))
    def _():
        x = jnp.concatenate([ref[...] for ref in x_refs], axis=0)
        length = rows * lines
        bias = row_bias(section, length, rows, columns)
        stored(layer(x, (gain_ref, qkv_ref, out_ref), length, bias), y_refs)

    @pl.when(section <= 1)
    def _():
        for from_ref, y_ref in zip(refs[inputs : inputs + kept] or x_refs, y_refs):
            y_ref[...] = from_ref[...]

    if kept and tick > 2:

        @pl.when(section == 0)
        def _():
            for x_ref, y_ref in zip(x_refs, y_refs):
                y_ref[...] = x_ref[...]


def final_kernel(dims, chunk, streamed, flag_ref, gain_ref, qkv_ref, out_ref, owner_ref, x_ref, held_ref, *rest):
    rows, columns, lines, _, _, _ = dims
    y_ref = rest[-5] if streamed else rest[-1]
    section = flag_ref[0]
    weights = (gain_ref, qkv_ref, out_ref)

    def packed(value):
        y_ref[...] = packed_rows(value, owner_ref[...], chunk, flag_ref[1], dims)

    @pl.when(section > 2)
    def _():
        length = rows * lines
        bias = row_bias(section, length, rows, columns)
        if streamed:
            here, sems = rest[-4:-1], rest[-1]
            steps = fetches(weights, here, sems)
            for copy in sum(steps, []):
                copy.start()
            gain = steps[0].pop()
            gain.wait()
            packed(layer(x_ref[...], here, length, bias, lambda step: wait_all(steps[step])))
        else:
            packed(layer(x_ref[...], weights, length, bias))

    @pl.when(section == 2)
    def _():
        packed(x_ref[...])

    @pl.when(section < 2)
    def _():
        packed(held_ref[...])


def cost(positions, features):
    return pl.CostEstimate(flops=10**10, bytes_accessed=positions * features, transcendentals=0)


def in_hbm(arrays):
    return [pltpu.with_memory_space_constraint(a, pltpu.HBM) for a in arrays]


def in_vmem(arrays):
    return [pltpu.with_memory_space_constraint(a, pltpu.VMEM) for a in arrays]


def options():
    return pltpu.CompilerParams(vmem_limit_bytes=VMEM_BYTES)


def first_pass(place, order, owner_row, arrays, dims, turn_place):
    _, positions, features = arrays[-1].shape
    half = pltpu.VMEM((1, positions // CORES, features), jnp.bfloat16)
    return pl.pallas_call(
        functools.partial(first_kernel, dims, turn_place),
        out_shape=[half, half] + [pltpu.VMEM(a.shape, a.dtype) for a in arrays],
        in_specs=[IN_SMEM] * 2 + [IN_VMEM] + [pl.BlockSpec(memory_space=pltpu.HBM)] * len(arrays),
        out_specs=[IN_VMEM] * (2 + len(arrays)),
        scratch_shapes=[
            pltpu.SemaphoreType.DMA((HEADS // GROUP + 1, 4)),
            pltpu.SemaphoreType.DMA((arrays[-1].shape[0],)),
        ],
        compiler_params=options(),
        cost_estimate=cost(positions, features),
        name="first_pass",
    )(place, order, owner_row, *in_hbm(arrays))


def column_pass(place, order, frames, owner_row, weights, dims, turn_places, after):
    _, positions, features = frames.shape
    half = pltpu.VMEM((len(turn_places), positions // CORES, features), jnp.bfloat16)
    return pl.pallas_call(
        functools.partial(column_kernel, dims, turn_places),
        out_shape=[half, half],
        in_specs=[IN_SMEM] * 2 + [IN_VMEM] * 5 + [ANYWHERE] * len(after),
        out_specs=[IN_VMEM] * 2,
        compiler_params=options(),
        cost_estimate=cost(positions, features),
        name="column_pass",
    )(place, order, *in_vmem([frames]), owner_row, *in_vmem(weights), *after)


def merge(place, mine, other, dims, clip, after):
    _, positions, features = mine.shape
    groups = dims[-1] // CORES
    part = pltpu.VMEM((CORES * positions // groups, features), jnp.bfloat16)
    return pl.pallas_call(
        functools.partial(merge_kernel, dims, clip),
        out_shape=[part] * groups,
        in_specs=[IN_SMEM] + [ANYWHERE] * (2 + len(after)),
        out_specs=[IN_VMEM] * groups,
        scratch_shapes=[
            pltpu.VMEM((CORES * positions, features), jnp.bfloat16),
            pltpu.SemaphoreType.DMA((CORES,)),
        ],
        compiler_params=options(),
        cost_estimate=cost(positions, features),
        name="merge",
    )(place, mine, other, *after)


def gate(arrays):
    return pl.pallas_call(
        gate_kernel,
        out_shape=jax.ShapeDtypeStruct((1,), jnp.int32),
        in_specs=[ANYWHERE] * len(arrays),
        out_specs=IN_SMEM,
        compiler_params=options(),
        cost_estimate=cost(1, 1),
        name="gate",
    )(*arrays)


def frame_pass(place, pieces, weights, dims, work, count, after):
    positions, features = dims[0] * dims[2] * len(work) // count, pieces[0].shape[1]
    return pl.pallas_call(
        functools.partial(frame_kernel, dims, work, count),
        out_shape=[pltpu.VMEM((positions, features), jnp.bfloat16)] * count,
        in_specs=[IN_SMEM] + [IN_VMEM] * (3 + len(pieces)) + [ANYWHERE] * len(after),
        out_specs=[IN_VMEM] * count,
        compiler_params=options(),
        cost_estimate=cost(positions, features),
        name="frame_pass",
    )(place, *in_vmem([*weights, *pieces]), *after)


def row_pass(place, x, y, weights, dims, tick, after):
    count, features = len(y) or len(x), x[0].shape[1]
    positions = sum(a.shape[0] for a in x) // count
    return pl.pallas_call(
        functools.partial(row_kernel, dims, tick, len(x), len(y), count),
        out_shape=[pltpu.VMEM((positions, features), jnp.bfloat16)] * count,
        in_specs=[IN_SMEM] + [IN_VMEM] * (3 + len(x) + len(y)) + [ANYWHERE] * len(after),
        out_specs=[IN_VMEM] * count,
        compiler_params=options(),
        cost_estimate=cost(positions, features),
        name="row_pass",
    )(place, *in_vmem([*weights, *x, *y]), *after)


def final_pass(place, x, held, owner_row, weights, dims, chunk, streamed, after):
    positions, features = x.shape
    _, _, lines, _, most, peers = dims
    kind, scratch = IN_VMEM, []
    if streamed:
        kind = pl.BlockSpec(memory_space=pltpu.HBM)
        scratch = [pltpu.VMEM(a.shape, a.dtype) for a in weights]
        scratch.append(pltpu.SemaphoreType.DMA((HEADS // GROUP + 1, 4)))
    return pl.pallas_call(
        functools.partial(final_kernel, dims, chunk, streamed),
        out_shape=jax.ShapeDtypeStruct((peers * most * lines, features), jnp.bfloat16),
        in_specs=[IN_SMEM] + [kind] * 3 + [IN_VMEM] * 3 + [ANYWHERE] * len(after),
        out_specs=IN_VMEM,
        scratch_shapes=scratch,
        compiler_params=options(),
        cost_estimate=cost(positions, features),
        name="final_pass",
    )(place, *(in_hbm if streamed else in_vmem)(weights), owner_row, *in_vmem([x, held]), *after)


def settle_kernel(dims, max_rows, flag_ref, owner_ref, *refs):
    rows, columns, lines, strides, most, peers = dims
    out_ref = refs[-1]
    parts = jnp.concatenate([ref[...] for ref in refs[:-1]], axis=0)
    shape = (out_ref.shape[0], parts.shape[0])
    start = jnp.sum((owner_ref[...] < flag_ref[1]).astype(jnp.float32), axis=1, keepdims=True).astype(jnp.int32)
    chunk, peer, n, line = digits(iota((1, shape[1]), 1), peers, most, lines)
    slot = lax.rem(chunk * peers + peer - start + owner_ref.shape[1], strides) + strides * n
    out_line, out_slot = digits(iota((shape[0], 1), 0), max_rows)
    out_ref[...] = moved((slot == out_slot) & (line == out_line), parts)


def settle(place, owner_row, parts, dims, max_rows):
    rows, features = dims[2] * max_rows, parts[0].shape[1]
    return pl.pallas_call(
        functools.partial(settle_kernel, dims, max_rows),
        out_shape=jax.ShapeDtypeStruct((rows, features), jnp.bfloat16),
        in_specs=[IN_SMEM] + [IN_VMEM] * (1 + len(parts)),
        out_specs=IN_VMEM,
        compiler_params=options(),
        cost_estimate=cost(rows, features),
        name="settle",
    )(place, owner_row, *parts)


def swapped(x, peers):
    parts = x.reshape(peers, -1, x.shape[-1])
    return lax.all_to_all(parts, "seq", split_axis=0, concat_axis=0, tiled=True)


def local(frames_in, order, owner, qkv_weight, out_weight, gains):
    sections = lax.axis_size("section")
    peers = lax.axis_size("seq")
    section = lax.axis_index("section")
    me = lax.axis_index("seq")
    clips, lines_dev, img_rows, features = frames_in.shape
    lines = lines_dev * peers
    columns = lines // FRAMES
    max_rows = 2 * img_rows // peers
    chunks = lines_dev
    strides = peers * chunks
    rows = img_rows // strides
    most = -(-max_rows // strides)
    dims = (rows, columns, lines, strides, most, peers)
    owner_row = owner.reshape(1, img_rows)
    place = jnp.stack([section, me]).astype(jnp.int32)
    groups = peers // CORES

    homes = [1, 0, 2, 3]

    def across(half):
        return lax.ppermute(half, ("section", "seq"), [(p, p ^ 1) for p in range(peers)])

    stored_weights = [gains, qkv_weight[0], out_weight[0]]
    arrays = stored_weights + [frames_in.reshape(clips, lines_dev * img_rows, features)]
    mine, other, *weights, frames = first_pass(
        place, order, owner_row, arrays, dims, sections - 1 - homes[0]
    )

    def column_clips(first, last, after):
        turn_places = [sections - 1 - home for home in homes[first:last]]
        mine, other = column_pass(place, order, frames, owner_row, weights, dims, turn_places, after)
        return mine, across(other)

    def hop(halves, clip, after):
        parts = merge(place, *halves, dims, clip, after)
        return parts[0], [
            lax.ppermute(
                part,
                ("section", "seq"),
                [(p, peers + (p // CORES ^ d) * CORES + p % CORES) for p in range(peers)],
            )
            for d, part in enumerate(parts)
        ]

    def relay(parts, tick):
        pairs = []
        if tick == clips:
            pairs.append((0, 1))
        if 1 <= tick <= clips:
            pairs.append((1, 2))
        if 2 <= tick <= clips + 1:
            pairs.append((2, 3))
        if tick in (3, 4):
            pairs.append((3, 0))
        if tick == 5:
            pairs.append((3, 2))
        return [lax.ppermute(part, "section", pairs) for part in parts]

    all_chunks = list(range(chunks))
    sent, pieces = hop((mine, across(other)), 0, [])
    halves, y = column_clips(1, clips, [sent]), []
    for tick in range(clips - 1):
        sent, upcoming = hop(halves, tick, [*pieces, *y] if tick else [gate(pieces)])
        split = tick == clips - 2
        fresh = frame_pass(place, pieces, weights, dims, all_chunks, chunks if split else 1, [sent])
        y = row_pass(place, relay(y, tick), fresh, weights, dims, tick, []) if tick else fresh
        pieces = upcoming

    y, held, ready = list(y), [None] * chunks, [y[-1]]
    for tick in range(clips - 1, clips + sections - 3):
        for chunk in all_chunks:
            (x,) = relay([y[chunk]], tick)
            fresh = frame_pass(place, pieces, weights, dims, [chunk], 1, ready) if tick < clips else []
            (y[chunk],) = row_pass(place, [x], fresh, weights, dims, tick, ready)
            held[chunk], ready = x, [y[chunk]]
    for chunk in all_chunks:
        (x,) = relay([y[chunk]], clips + sections - 3)
        streamed = chunk > 0
        y[chunk] = final_pass(
            place,
            x,
            held[chunk],
            owner_row,
            stored_weights if streamed else weights,
            dims,
            chunk,
            streamed,
            ready,
        )
        ready = [y[chunk]]
    arrived = [swapped(part, peers).reshape(-1, features) for part in y]
    return settle(place, owner_row, arrived, dims, max_rows).reshape(1, lines, max_rows, features)


def solution(mesh):
    placed = (
        P(None, "seq", None, None),
        P(),
        P(),
        P("section", None, None),
        P("section", None, None),
        P("section", None),
    )
    return jax.shard_map(
        local,
        mesh=mesh,
        in_specs=placed,
        out_specs=P("section", None, "seq", None),
        check_vma=False,
    )
```

```python
import functools

import jax
import jax.numpy as jnp
from jax import lax
from jax.experimental import pallas as pl
from jax.experimental.pallas import tpu as pltpu
from jax.sharding import PartitionSpec as P

HEADS = 16
FRAMES = 4
GROUP = 4
PAIR = 2
CORES = 2
LOG2_E = 1.4426950408889634
VMEM_BYTES = 32 * 1024 * 1024
IN_VMEM = pl.BlockSpec(memory_space=pltpu.VMEM)
IN_SMEM = pl.BlockSpec(memory_space=pltpu.SMEM)
ANYWHERE = pl.BlockSpec(memory_space=pl.ANY)


def iota(shape, dim):
    return lax.broadcasted_iota(jnp.int32, shape, dim)


def scaled_norm(values, gain_row):
    mean_square = jnp.mean(values * values, axis=-1, keepdims=True)
    return (values * lax.rsqrt(mean_square + 1e-06) * gain_row).astype(jnp.bfloat16)


def layer(x, weights, length, bias, ready=lambda step: None):
    gain_ref, qkv_ref, out_ref = weights
    positions, features = x.shape
    head_size = features // HEADS
    width = GROUP * head_size
    groups = features // width
    values = x.astype(jnp.float32)
    normed = scaled_norm(values, gain_ref[...])
    lanes = PAIR * head_size
    own_lanes = [(lax.div(iota((1, lanes), 1), head_size) == h).astype(jnp.bfloat16) for h in range(PAIR)]
    ones = jnp.concatenate([jnp.broadcast_to(own, (length, lanes)) for own in own_lanes], axis=0)
    scale = head_size ** (-0.5) * LOG2_E

    def per_head(part):
        return jnp.concatenate([part * own for own in own_lanes], axis=0)

    def projections(g):
        ready(g)
        return [
            jnp.dot(
                normed,
                qkv_ref[:, part * features + g * width : part * features + (g + 1) * width],
                preferred_element_type=jnp.float32,
            ).astype(jnp.bfloat16)
            for part in range(3)
        ]

    def attended(queries, key_rows, value_rows):
        scores = lax.dot_general(
            queries, per_head(key_rows), (((1,), (1,)), ((), ())), preferred_element_type=jnp.float32
        ) * scale
        grown = []
        for h in range(PAIR):
            own = scores[:, h * length : (h + 1) * length]
            if bias is not None:
                own = own + bias
            grown.append(jnp.exp2(own - jnp.max(own, axis=-1, keepdims=True)).astype(jnp.bfloat16))
        grown = jnp.concatenate(grown, axis=1)
        summed = jnp.concatenate([per_head(value_rows), ones], axis=1)
        weighted, total = jnp.split(jnp.dot(grown, summed, preferred_element_type=jnp.float32), 2, axis=1)
        share = pl.reciprocal(total, approx=True)
        share = share * (2.0 - total * share)
        return (weighted * share).astype(jnp.bfloat16)

    contexts = []
    upcoming = projections(0)
    for g in range(groups):
        current, upcoming = upcoming, projections(g + 1) if g + 1 < groups else None
        for first in range(0, width, lanes):
            blocks = [
                attended(*(part[start : start + length, first : first + lanes] for part in current))
                for start in range(0, positions, length)
            ]
            contexts.append(blocks[0] if len(blocks) == 1 else jnp.concatenate(blocks, axis=0))
    context = jnp.concatenate(contexts, axis=1)
    ready(groups)
    return (values + jnp.dot(context, out_ref[...], preferred_element_type=jnp.float32)).astype(jnp.bfloat16)


def moved(hit, rows):
    one_hot = jnp.where(hit, 1.0, 0.0).astype(jnp.bfloat16)
    return jnp.dot(one_hot, rows, preferred_element_type=jnp.float32).astype(jnp.bfloat16)


def digits(place, *sizes):
    found = []
    for size in reversed(sizes):
        found.append(lax.rem(place, size))
        place = lax.div(place, size)
    return [place] + found[::-1]


def ranks(owner_row):
    img_rows = owner_row.shape[1]
    square = (img_rows, img_rows)
    across = jnp.broadcast_to(owner_row, square).astype(jnp.float32)
    down = across.T
    before = (down < across) | ((down == across) & (iota(square, 0) < iota(square, 1)))
    return jnp.sum(before.astype(jnp.float32), axis=0, keepdims=True).astype(jnp.int32)


def spread_rows(y, rank, my_core, dims):
    rows, _, _, strides, _, peers = dims
    chunks = strides // peers
    positions, img_rows = y.shape[0], rank.shape[1]
    lines_dev = positions // img_rows
    shape = (positions, img_rows)
    core, group, chunk, line, i = digits(iota(shape, 0), peers // CORES, chunks, lines_dev, rows)
    core = lax.rem(core + my_core, CORES)
    hit = (i * strides + chunk * peers + group * CORES + core) == rank
    return moved(jnp.concatenate([hit & (line == own) for own in range(lines_dev)], axis=1), y)


def fetches(from_refs, to_refs, sems):
    (from_gain, from_qkv, from_out), (to_gain, to_qkv, to_out) = from_refs, to_refs
    features = from_out.shape[0]
    width = GROUP * features // HEADS
    groups = features // width
    steps = []
    for g in range(groups):
        places = [pl.ds(part * features + g * width, width) for part in range(3)]
        steps.append([(from_qkv.at[:, place], to_qkv.at[:, place]) for place in places])
    steps.append([(from_out, to_out)])
    steps[0].append((from_gain, to_gain))
    return [
        [pltpu.make_async_copy(source, target, sems.at[step, n]) for n, (source, target) in enumerate(pairs)]
        for step, pairs in enumerate(steps)
    ]


def wait_all(copies):
    for copy in copies:
        copy.wait()


def first_kernel(dims, turn_place, flag_ref, order_ref, owner_ref, *refs):
    from_refs, (mine_ref, other_ref), to_refs = refs[:4], refs[4:6], refs[6:10]
    sems, clip_sems = refs[10:]
    clips = from_refs[3].shape[0]
    steps = fetches(from_refs[:3], to_refs[:3], sems)
    places = [lax.rem(order_ref[turn_place] + n, clips) for n in range(clips)]
    frames = [
        pltpu.make_async_copy(from_refs[3].at[place], to_refs[3].at[place], clip_sems.at[n])
        for n, place in enumerate(places)
    ]
    gain = steps[0].pop()
    for copy in [gain, frames[0], *sum(steps, []), *frames[1:]]:
        copy.start()
    wait_all([gain, frames[0]])

    @pl.when(flag_ref[0] == 0)
    def _():
        y = layer(
            to_refs[3][places[0]], to_refs[:3], owner_ref.shape[1], None, lambda step: wait_all(steps[step])
        )
        y = spread_rows(y, ranks(owner_ref[...]), lax.rem(flag_ref[1], CORES), dims)
        mine_ref[0] = y[: y.shape[0] // CORES]
        other_ref[0] = y[y.shape[0] // CORES :]

    @pl.when(flag_ref[0] != 0)
    def _():
        wait_all(sum(steps, []))

    wait_all(frames[1:])


def column_kernel(dims, turn_places, flag_ref, order_ref, frames_ref, owner_ref, gain_ref, qkv_ref, out_ref, *rest):
    mine_ref, other_ref = rest[-2:]

    @pl.when(flag_ref[0] == 0)
    def _():
        rank = ranks(owner_ref[...])
        for clip, turn_place in enumerate(turn_places):
            x = frames_ref[order_ref[turn_place]]
            y = layer(x, (gain_ref, qkv_ref, out_ref), owner_ref.shape[1], None)
            y = spread_rows(y, rank, lax.rem(flag_ref[1], CORES), dims)
            mine_ref[clip] = y[: y.shape[0] // CORES]
            other_ref[clip] = y[y.shape[0] // CORES :]


def merge_kernel(dims, clip, flag_ref, mine_ref, other_ref, *rest):
    rows, _, lines, strides, _, peers = dims
    groups, chunks = peers // CORES, strides // peers
    lines_dev = lines // peers
    part_refs, (both, sems) = rest[-groups - 2 : -2], rest[-2:]

    @pl.when(flag_ref[0] == 0)
    def _():
        half = mine_ref.shape[1]
        copies = [
            pltpu.make_async_copy(ref.at[clip], both.at[pl.ds(n * half, half)], sems.at[n])
            for n, ref in enumerate((mine_ref, other_ref))
        ]
        for copy in copies:
            copy.start()
        size = CORES * half
        shape = (size, size)
        my_core, my_group = lax.rem(flag_ref[1], CORES), lax.div(flag_ref[1], CORES)
        apart, chunk, core, inner = digits(iota(shape, 0), chunks, CORES, lines_dev * rows)
        far, from_group, from_chunk, from_inner = digits(iota(shape, 1), groups, chunks, lines_dev * rows)
        from_core = lax.rem(far + my_core, CORES)
        hit = (
            ((apart ^ my_group) == from_group)
            & (chunk == from_chunk)
            & (core == from_core)
            & (inner == from_inner)
        )
        size = size // groups
        wait_all(copies)
        sent = moved(hit, both[...])
        for d, part_ref in enumerate(part_refs):
            part_ref[...] = sent[d * size : (d + 1) * size]


def gate_kernel(*refs):
    refs[-1][0] = 0


def gathered_chunk(part_refs, chunk, chunks, me, dims):
    rows, _, lines, strides, _, peers = dims
    parts = jnp.concatenate([ref[...] for ref in part_refs], axis=0)
    shape = (lines * rows, parts.shape[0])
    inner_size = lines // (peers // CORES) * rows
    group, inner = digits(iota(shape, 0), inner_size)
    apart, from_chunk, from_inner = digits(iota(shape, 1), chunks, inner_size)
    my_group = lax.div(me, CORES)
    return moved(((group ^ my_group) == apart) & (from_chunk == chunk) & (from_inner == inner), parts)


def row_bias(section, length, rows, columns):
    query, key = iota((length, length), 0), iota((length, length), 1)
    same_row = lax.rem(query, rows) == lax.rem(key, rows)
    query_line, key_line = lax.div(query, rows), lax.div(key, rows)
    query_col, key_col = lax.rem(query_line, columns), lax.rem(key_line, columns)
    across_frames = query_col == key_col
    across_columns = (lax.div(query_line, columns) == lax.div(key_line, columns)) & (key_col <= query_col)
    first = jnp.broadcast_to(section == 1, (length, length))
    allowed = same_row & ((first & across_frames) | (~first & across_columns))
    return jnp.where(allowed, 0.0, -1e30)


def packed_rows(y, owner_row, chunk, me, dims):
    rows, _, lines, strides, most, peers = dims
    img_rows = owner_row.shape[1]
    shape = (peers * most * lines, img_rows)
    peer, n, line = digits(iota((shape[0], 1), 0), most, lines)
    owners = jnp.broadcast_to(owner_row, shape)
    start = jnp.sum((owners < peer).astype(jnp.float32), axis=1, keepdims=True).astype(jnp.int32)
    end = jnp.sum((owners <= peer).astype(jnp.float32), axis=1, keepdims=True).astype(jnp.int32)
    rank = start + lax.rem(chunk * peers + me - start + img_rows, strides) + strides * n
    from_line, i = digits(iota((1, shape[1]), 1), rows)
    return moved((lax.div(rank, strides) == i) & (line == from_line) & (rank < end), y)


def stored(y, y_refs):
    size = y.shape[0] // len(y_refs)
    for n, y_ref in enumerate(y_refs):
        y_ref[...] = y[n * size : (n + 1) * size]


def frame_kernel(dims, work, count, flag_ref, gain_ref, qkv_ref, out_ref, *refs):
    rows, columns, lines, strides, _, peers = dims
    piece_refs, y_refs = refs[: peers // CORES], refs[-count:]

    @pl.when(flag_ref[0] == 1)
    def _():
        parts = [gathered_chunk(piece_refs, chunk, strides // peers, flag_ref[1], dims) for chunk in work]
        x = jnp.concatenate(parts, axis=0)
        length = rows * lines
        bias = row_bias(flag_ref[0], length, rows, columns)
        stored(layer(x, (gain_ref, qkv_ref, out_ref), length, bias), y_refs)


def row_kernel(dims, tick, inputs, kept, count, part, flag_ref, gain_ref, qkv_ref, out_ref, *refs):
    rows, columns, lines, _, _, _ = dims
    x_refs, y_refs = refs[:inputs], refs[-count:]
    section = flag_ref[0]

    @pl.when((section > 1) & (section <= tick + 1))
    def _():
        length = rows * lines
        x = jnp.concatenate([ref[...] for ref in x_refs], axis=0)
        x = x if part is None else x[part * length : (part + 1) * length]
        bias = row_bias(section, length, rows, columns)
        stored(layer(x, (gain_ref, qkv_ref, out_ref), length, bias), y_refs)

    @pl.when(section <= 1)
    def _():
        for from_ref, y_ref in zip(refs[inputs : inputs + kept] or x_refs, y_refs):
            y_ref[...] = from_ref[...]

    if kept and tick > 2:

        @pl.when(section == 0)
        def _():
            for x_ref, y_ref in zip(x_refs, y_refs):
                y_ref[...] = x_ref[...]


def final_kernel(dims, chunk, streamed, flag_ref, gain_ref, qkv_ref, out_ref, owner_ref, x_ref, held_ref, *rest):
    rows, columns, lines, _, _, _ = dims
    y_ref = rest[-5] if streamed else rest[-1]
    section = flag_ref[0]
    weights = (gain_ref, qkv_ref, out_ref)

    def packed(value):
        y_ref[...] = packed_rows(value, owner_ref[...], chunk, flag_ref[1], dims)

    @pl.when(section > 2)
    def _():
        length = rows * lines
        bias = row_bias(section, length, rows, columns)
        if streamed:
            here, sems = rest[-4:-1], rest[-1]
            steps = fetches(weights, here, sems)
            for copy in sum(steps, []):
                copy.start()
            gain = steps[0].pop()
            gain.wait()
            packed(layer(x_ref[...], here, length, bias, lambda step: wait_all(steps[step])))
        else:
            packed(layer(x_ref[...], weights, length, bias))

    @pl.when(section == 2)
    def _():
        packed(x_ref[...])

    @pl.when(section < 2)
    def _():
        packed(held_ref[...])


def cost(positions, features):
    return pl.CostEstimate(flops=10**10, bytes_accessed=positions * features, transcendentals=0)


def in_hbm(arrays):
    return [pltpu.with_memory_space_constraint(a, pltpu.HBM) for a in arrays]


def in_vmem(arrays):
    return [pltpu.with_memory_space_constraint(a, pltpu.VMEM) for a in arrays]


def options():
    return pltpu.CompilerParams(vmem_limit_bytes=VMEM_BYTES)


def first_pass(place, order, owner_row, arrays, dims, turn_place):
    _, positions, features = arrays[-1].shape
    half = pltpu.VMEM((1, positions // CORES, features), jnp.bfloat16)
    return pl.pallas_call(
        functools.partial(first_kernel, dims, turn_place),
        out_shape=[half, half] + [pltpu.VMEM(a.shape, a.dtype) for a in arrays],
        in_specs=[IN_SMEM] * 2 + [IN_VMEM] + [pl.BlockSpec(memory_space=pltpu.HBM)] * len(arrays),
        out_specs=[IN_VMEM] * (2 + len(arrays)),
        scratch_shapes=[
            pltpu.SemaphoreType.DMA((HEADS // GROUP + 1, 4)),
            pltpu.SemaphoreType.DMA((arrays[-1].shape[0],)),
        ],
        compiler_params=options(),
        cost_estimate=cost(positions, features),
        name="first_pass",
    )(place, order, owner_row, *in_hbm(arrays))


def column_pass(place, order, frames, owner_row, weights, dims, turn_places, after):
    _, positions, features = frames.shape
    half = pltpu.VMEM((len(turn_places), positions // CORES, features), jnp.bfloat16)
    return pl.pallas_call(
        functools.partial(column_kernel, dims, turn_places),
        out_shape=[half, half],
        in_specs=[IN_SMEM] * 2 + [IN_VMEM] * 5 + [ANYWHERE] * len(after),
        out_specs=[IN_VMEM] * 2,
        compiler_params=options(),
        cost_estimate=cost(positions, features),
        name="column_pass",
    )(place, order, *in_vmem([frames]), owner_row, *in_vmem(weights), *after)


def merge(place, mine, other, dims, clip, after):
    _, positions, features = mine.shape
    groups = dims[-1] // CORES
    part = pltpu.VMEM((CORES * positions // groups, features), jnp.bfloat16)
    return pl.pallas_call(
        functools.partial(merge_kernel, dims, clip),
        out_shape=[part] * groups,
        in_specs=[IN_SMEM] + [ANYWHERE] * (2 + len(after)),
        out_specs=[IN_VMEM] * groups,
        scratch_shapes=[
            pltpu.VMEM((CORES * positions, features), jnp.bfloat16),
            pltpu.SemaphoreType.DMA((CORES,)),
        ],
        compiler_params=options(),
        cost_estimate=cost(positions, features),
        name="merge",
    )(place, mine, other, *after)


def gate(arrays):
    return pl.pallas_call(
        gate_kernel,
        out_shape=jax.ShapeDtypeStruct((1,), jnp.int32),
        in_specs=[ANYWHERE] * len(arrays),
        out_specs=IN_SMEM,
        compiler_params=options(),
        cost_estimate=cost(1, 1),
        name="gate",
    )(*arrays)


def frame_pass(place, pieces, weights, dims, work, count, after):
    positions, features = dims[0] * dims[2] * len(work) // count, pieces[0].shape[1]
    return pl.pallas_call(
        functools.partial(frame_kernel, dims, work, count),
        out_shape=[pltpu.VMEM((positions, features), jnp.bfloat16)] * count,
        in_specs=[IN_SMEM] + [IN_VMEM] * (3 + len(pieces)) + [ANYWHERE] * len(after),
        out_specs=[IN_VMEM] * count,
        compiler_params=options(),
        cost_estimate=cost(positions, features),
        name="frame_pass",
    )(place, *in_vmem([*weights, *pieces]), *after)


def row_pass(place, x, y, weights, dims, tick, after, part=None):
    count, features = len(y) or len(x), x[0].shape[1]
    positions = sum(a.shape[0] for a in x) // count if part is None else dims[0] * dims[2]
    return pl.pallas_call(
        functools.partial(row_kernel, dims, tick, len(x), len(y), count, part),
        out_shape=[pltpu.VMEM((positions, features), jnp.bfloat16)] * count,
        in_specs=[IN_SMEM] + [IN_VMEM] * (3 + len(x) + len(y)) + [ANYWHERE] * len(after),
        out_specs=[IN_VMEM] * count,
        compiler_params=options(),
        cost_estimate=cost(positions, features),
        name="row_pass",
    )(place, *in_vmem([*weights, *x, *y]), *after)


def final_pass(place, x, held, owner_row, weights, dims, chunk, streamed, after):
    positions, features = x.shape
    _, _, lines, _, most, peers = dims
    kind, scratch = IN_VMEM, []
    if streamed:
        kind = pl.BlockSpec(memory_space=pltpu.HBM)
        scratch = [pltpu.VMEM(a.shape, a.dtype) for a in weights]
        scratch.append(pltpu.SemaphoreType.DMA((HEADS // GROUP + 1, 4)))
    return pl.pallas_call(
        functools.partial(final_kernel, dims, chunk, streamed),
        out_shape=jax.ShapeDtypeStruct((peers * most * lines, features), jnp.bfloat16),
        in_specs=[IN_SMEM] + [kind] * 3 + [IN_VMEM] * 3 + [ANYWHERE] * len(after),
        out_specs=IN_VMEM,
        scratch_shapes=scratch,
        compiler_params=options(),
        cost_estimate=cost(positions, features),
        name="final_pass",
    )(place, *(in_hbm if streamed else in_vmem)(weights), owner_row, *in_vmem([x, held]), *after)


def settle_kernel(dims, max_rows, chunk, flag_ref, owner_ref, part_ref, *rest):
    rows, columns, lines, strides, most, peers = dims
    out_ref, base_refs = rest[-1], rest[:-1]
    shape = (out_ref.shape[0], part_ref.shape[0])
    start = jnp.sum((owner_ref[...] < flag_ref[1]).astype(jnp.float32), axis=1, keepdims=True).astype(jnp.int32)
    peer, n, line = digits(iota((1, shape[1]), 1), most, lines)
    slot = lax.rem(chunk * peers + peer - start + owner_ref.shape[1], strides) + strides * n
    out_line, out_slot = digits(iota((shape[0], 1), 0), max_rows)
    filled = moved((slot == out_slot) & (line == out_line), part_ref[...])
    for base_ref in base_refs:
        filled = filled + base_ref[...]
    out_ref[...] = filled


def settle(place, owner_row, part, base, dims, max_rows, chunk):
    rows, features = dims[2] * max_rows, part.shape[1]
    return pl.pallas_call(
        functools.partial(settle_kernel, dims, max_rows, chunk),
        out_shape=jax.ShapeDtypeStruct((rows, features), jnp.bfloat16),
        in_specs=[IN_SMEM] + [IN_VMEM] * (2 + len(base)),
        out_specs=IN_VMEM,
        compiler_params=options(),
        cost_estimate=cost(rows, features),
        name="settle",
    )(place, owner_row, part, *base)


def swapped(x, peers):
    parts = x.reshape(peers, -1, x.shape[-1])
    return lax.all_to_all(parts, "seq", split_axis=0, concat_axis=0, tiled=True)


def local(frames_in, order, owner, qkv_weight, out_weight, gains):
    sections = lax.axis_size("section")
    peers = lax.axis_size("seq")
    section = lax.axis_index("section")
    me = lax.axis_index("seq")
    clips, lines_dev, img_rows, features = frames_in.shape
    lines = lines_dev * peers
    columns = lines // FRAMES
    max_rows = 2 * img_rows // peers
    chunks = lines_dev
    strides = peers * chunks
    rows = img_rows // strides
    most = -(-max_rows // strides)
    dims = (rows, columns, lines, strides, most, peers)
    owner_row = owner.reshape(1, img_rows)
    place = jnp.stack([section, me]).astype(jnp.int32)
    groups = peers // CORES

    homes = [1, 0, 2, 3]

    def across(half):
        return lax.ppermute(half, ("section", "seq"), [(p, p ^ 1) for p in range(peers)])

    stored_weights = [gains, qkv_weight[0], out_weight[0]]
    arrays = stored_weights + [frames_in.reshape(clips, lines_dev * img_rows, features)]
    mine, other, *weights, frames = first_pass(
        place, order, owner_row, arrays, dims, sections - 1 - homes[0]
    )

    def column_clips(first, last, after):
        turn_places = [sections - 1 - home for home in homes[first:last]]
        mine, other = column_pass(place, order, frames, owner_row, weights, dims, turn_places, after)
        return mine, across(other)

    def hop(halves, clip, after):
        parts = merge(place, *halves, dims, clip, after)
        return parts[0], [
            lax.ppermute(
                part,
                ("section", "seq"),
                [(p, peers + (p // CORES ^ d) * CORES + p % CORES) for p in range(peers)],
            )
            for d, part in enumerate(parts)
        ]

    def relay(parts, tick):
        pairs = []
        if tick == clips:
            pairs.append((0, 1))
        if 1 <= tick <= clips:
            pairs.append((1, 2))
        if 2 <= tick <= clips + 1:
            pairs.append((2, 3))
        if tick in (3, 4):
            pairs.append((3, 0))
        if tick == 5:
            pairs.append((3, 2))
        return [lax.ppermute(part, "section", pairs) for part in parts]

    all_chunks = list(range(chunks))
    sent, pieces = hop((mine, across(other)), 0, [])
    halves, y = column_clips(1, clips, [sent]), []
    for tick in range(clips - 1):
        sent, upcoming = hop(halves, tick, [*pieces, *y] if tick else [gate(pieces)])
        if tick < clips - 2:
            fresh = frame_pass(place, pieces, weights, dims, all_chunks, 1, [sent])
            y = row_pass(place, relay(y, tick), fresh, weights, dims, tick, []) if tick else fresh
        else:
            x, y, ready = relay(y, tick), [], [sent]
            for chunk in all_chunks:
                fresh = frame_pass(place, pieces, weights, dims, [chunk], 1, ready)
                ready = row_pass(place, x, fresh, weights, dims, tick, ready, chunk)
                y += ready
        pieces = upcoming

    y, held, ready = list(y), [None] * chunks, [y[-1]]
    for tick in range(clips - 1, clips + sections - 3):
        for chunk in all_chunks:
            (x,) = relay([y[chunk]], tick)
            fresh = frame_pass(place, pieces, weights, dims, [chunk], 1, ready) if tick < clips else []
            (y[chunk],) = row_pass(place, [x], fresh, weights, dims, tick, ready)
            held[chunk], ready = x, [y[chunk]]
    for chunk in all_chunks:
        (x,) = relay([y[chunk]], clips + sections - 3)
        streamed = chunk > 0
        y[chunk] = final_pass(
            place,
            x,
            held[chunk],
            owner_row,
            stored_weights if streamed else weights,
            dims,
            chunk,
            streamed,
            ready,
        )
        ready = [y[chunk]]
    arrived = [swapped(part, peers).reshape(-1, features) for part in y]
    base = []
    for chunk, part in enumerate(arrived):
        base = [settle(place, owner_row, part, base, dims, max_rows, chunk)]
    return base[0].reshape(1, lines, max_rows, features)


def solution(mesh):
    placed = (
        P(None, "seq", None, None),
        P(),
        P(),
        P("section", None, None),
        P("section", None, None),
        P("section", None),
    )
    return jax.shard_map(
        local,
        mesh=mesh,
        in_specs=placed,
        out_specs=P("section", None, "seq", None),
        check_vma=False,
    )
```

```python
import functools

import jax
import jax.numpy as jnp
from jax import lax
from jax.experimental import pallas as pl
from jax.experimental.pallas import tpu as pltpu
from jax.sharding import PartitionSpec as P

HEADS = 16
FRAMES = 4
GROUP = 4
PAIR = 2
CORES = 2
LOG2_E = 1.4426950408889634
VMEM_BYTES = 32 * 1024 * 1024
IN_VMEM = pl.BlockSpec(memory_space=pltpu.VMEM)
IN_SMEM = pl.BlockSpec(memory_space=pltpu.SMEM)
ANYWHERE = pl.BlockSpec(memory_space=pl.ANY)


def iota(shape, dim):
    return lax.broadcasted_iota(jnp.int32, shape, dim)


def scaled_norm(values, gain_row):
    mean_square = jnp.mean(values * values, axis=-1, keepdims=True)
    return (values * lax.rsqrt(mean_square + 1e-06) * gain_row).astype(jnp.bfloat16)


def layer(x, weights, length, bias, ready=lambda step: None):
    gain_ref, qkv_ref, out_ref = weights
    positions, features = x.shape
    head_size = features // HEADS
    width = GROUP * head_size
    groups = features // width
    values = x.astype(jnp.float32)
    normed = scaled_norm(values, gain_ref[...])
    lanes = PAIR * head_size
    own_lanes = [(lax.div(iota((1, lanes), 1), head_size) == h).astype(jnp.bfloat16) for h in range(PAIR)]
    ones = jnp.concatenate([jnp.broadcast_to(own, (length, lanes)) for own in own_lanes], axis=0)
    scale = head_size ** (-0.5) * LOG2_E

    def per_head(part):
        return jnp.concatenate([part * own for own in own_lanes], axis=0)

    def projections(g):
        ready(g)
        return [
            jnp.dot(
                normed,
                qkv_ref[:, part * features + g * width : part * features + (g + 1) * width],
                preferred_element_type=jnp.float32,
            ).astype(jnp.bfloat16)
            for part in range(3)
        ]

    def attended(queries, key_rows, value_rows):
        scores = lax.dot_general(
            queries, per_head(key_rows), (((1,), (1,)), ((), ())), preferred_element_type=jnp.float32
        ) * scale
        grown = []
        for h in range(PAIR):
            own = scores[:, h * length : (h + 1) * length]
            if bias is not None:
                own = own + bias
            grown.append(jnp.exp2(own - jnp.max(own, axis=-1, keepdims=True)).astype(jnp.bfloat16))
        grown = jnp.concatenate(grown, axis=1)
        summed = jnp.concatenate([per_head(value_rows), ones], axis=1)
        weighted, total = jnp.split(jnp.dot(grown, summed, preferred_element_type=jnp.float32), 2, axis=1)
        share = pl.reciprocal(total, approx=True)
        share = share * (2.0 - total * share)
        return (weighted * share).astype(jnp.bfloat16)

    contexts = []
    upcoming = projections(0)
    for g in range(groups):
        current, upcoming = upcoming, projections(g + 1) if g + 1 < groups else None
        for first in range(0, width, lanes):
            blocks = [
                attended(*(part[start : start + length, first : first + lanes] for part in current))
                for start in range(0, positions, length)
            ]
            contexts.append(blocks[0] if len(blocks) == 1 else jnp.concatenate(blocks, axis=0))
    context = jnp.concatenate(contexts, axis=1)
    ready(groups)
    return (values + jnp.dot(context, out_ref[...], preferred_element_type=jnp.float32)).astype(jnp.bfloat16)


def moved(hit, rows):
    one_hot = jnp.where(hit, 1.0, 0.0).astype(jnp.bfloat16)
    return jnp.dot(one_hot, rows, preferred_element_type=jnp.float32).astype(jnp.bfloat16)


def digits(place, *sizes):
    found = []
    for size in reversed(sizes):
        found.append(lax.rem(place, size))
        place = lax.div(place, size)
    return [place] + found[::-1]


def ranks(owner_row):
    img_rows = owner_row.shape[1]
    square = (img_rows, img_rows)
    across = jnp.broadcast_to(owner_row, square).astype(jnp.float32)
    down = across.T
    before = (down < across) | ((down == across) & (iota(square, 0) < iota(square, 1)))
    return jnp.sum(before.astype(jnp.float32), axis=0, keepdims=True).astype(jnp.int32)


def spread_rows(y, rank, my_core, dims):
    rows, _, _, strides, _, peers = dims
    chunks = strides // peers
    positions, img_rows = y.shape[0], rank.shape[1]
    lines_dev = positions // img_rows
    shape = (positions, img_rows)
    core, group, chunk, line, i = digits(iota(shape, 0), peers // CORES, chunks, lines_dev, rows)
    core = lax.rem(core + my_core, CORES)
    hit = (i * strides + chunk * peers + group * CORES + core) == rank
    return moved(jnp.concatenate([hit & (line == own) for own in range(lines_dev)], axis=1), y)


def fetches(from_refs, to_refs, sems):
    (from_gain, from_qkv, from_out), (to_gain, to_qkv, to_out) = from_refs, to_refs
    features = from_out.shape[0]
    width = GROUP * features // HEADS
    groups = features // width
    steps = []
    for g in range(groups):
        places = [pl.ds(part * features + g * width, width) for part in range(3)]
        steps.append([(from_qkv.at[:, place], to_qkv.at[:, place]) for place in places])
    steps.append([(from_out, to_out)])
    steps[0].append((from_gain, to_gain))
    return [
        [pltpu.make_async_copy(source, target, sems.at[step, n]) for n, (source, target) in enumerate(pairs)]
        for step, pairs in enumerate(steps)
    ]


def wait_all(copies):
    for copy in copies:
        copy.wait()


def first_kernel(dims, turn_place, flag_ref, order_ref, owner_ref, *refs):
    from_refs, (mine_ref, other_ref), to_refs = refs[:4], refs[4:6], refs[6:10]
    sems, clip_sems = refs[10:]
    clips = from_refs[3].shape[0]
    steps = fetches(from_refs[:3], to_refs[:3], sems)
    places = [lax.rem(order_ref[turn_place] + n, clips) for n in range(clips)]
    frames = [
        pltpu.make_async_copy(from_refs[3].at[place], to_refs[3].at[place], clip_sems.at[n])
        for n, place in enumerate(places)
    ]
    gain = steps[0].pop()
    for copy in [gain, frames[0], *sum(steps, []), *frames[1:]]:
        copy.start()
    wait_all([gain, frames[0]])

    @pl.when(flag_ref[0] == 0)
    def _():
        y = layer(
            to_refs[3][places[0]], to_refs[:3], owner_ref.shape[1], None, lambda step: wait_all(steps[step])
        )
        y = spread_rows(y, ranks(owner_ref[...]), lax.rem(flag_ref[1], CORES), dims)
        mine_ref[0] = y[: y.shape[0] // CORES]
        other_ref[0] = y[y.shape[0] // CORES :]

    @pl.when(flag_ref[0] != 0)
    def _():
        wait_all(sum(steps, []))

    wait_all(frames[1:])


def column_kernel(dims, turn_places, flag_ref, order_ref, frames_ref, owner_ref, gain_ref, qkv_ref, out_ref, *rest):
    mine_ref, other_ref = rest[-2:]

    @pl.when(flag_ref[0] == 0)
    def _():
        rank = ranks(owner_ref[...])
        for clip, turn_place in enumerate(turn_places):
            x = frames_ref[order_ref[turn_place]]
            y = layer(x, (gain_ref, qkv_ref, out_ref), owner_ref.shape[1], None)
            y = spread_rows(y, rank, lax.rem(flag_ref[1], CORES), dims)
            mine_ref[clip] = y[: y.shape[0] // CORES]
            other_ref[clip] = y[y.shape[0] // CORES :]


def merge_kernel(dims, clip, flag_ref, mine_ref, other_ref, *rest):
    rows, _, lines, strides, _, peers = dims
    groups, chunks = peers // CORES, strides // peers
    lines_dev = lines // peers
    part_refs, (both, sems) = rest[-groups - 2 : -2], rest[-2:]

    @pl.when(flag_ref[0] == 0)
    def _():
        half = mine_ref.shape[1]
        copies = [
            pltpu.make_async_copy(ref.at[clip], both.at[pl.ds(n * half, half)], sems.at[n])
            for n, ref in enumerate((mine_ref, other_ref))
        ]
        for copy in copies:
            copy.start()
        size = CORES * half
        shape = (size, size)
        my_core, my_group = lax.rem(flag_ref[1], CORES), lax.div(flag_ref[1], CORES)
        apart, chunk, core, inner = digits(iota(shape, 0), chunks, CORES, lines_dev * rows)
        far, from_group, from_chunk, from_inner = digits(iota(shape, 1), groups, chunks, lines_dev * rows)
        from_core = lax.rem(far + my_core, CORES)
        hit = (
            ((apart ^ my_group) == from_group)
            & (chunk == from_chunk)
            & (core == from_core)
            & (inner == from_inner)
        )
        size = size // groups
        wait_all(copies)
        sent = moved(hit, both[...])
        for d, part_ref in enumerate(part_refs):
            part_ref[...] = sent[d * size : (d + 1) * size]


def gate_kernel(*refs):
    refs[-1][0] = 0


def gathered_chunk(part_refs, chunk, chunks, me, dims):
    rows, _, lines, strides, _, peers = dims
    parts = jnp.concatenate([ref[...] for ref in part_refs], axis=0)
    shape = (lines * rows, parts.shape[0])
    inner_size = lines // (peers // CORES) * rows
    group, inner = digits(iota(shape, 0), inner_size)
    apart, from_chunk, from_inner = digits(iota(shape, 1), chunks, inner_size)
    my_group = lax.div(me, CORES)
    return moved(((group ^ my_group) == apart) & (from_chunk == chunk) & (from_inner == inner), parts)


def row_bias(section, length, rows, columns):
    query, key = iota((length, length), 0), iota((length, length), 1)
    same_row = lax.rem(query, rows) == lax.rem(key, rows)
    query_line, key_line = lax.div(query, rows), lax.div(key, rows)
    query_col, key_col = lax.rem(query_line, columns), lax.rem(key_line, columns)
    across_frames = query_col == key_col
    across_columns = (lax.div(query_line, columns) == lax.div(key_line, columns)) & (key_col <= query_col)
    first = jnp.broadcast_to(section == 1, (length, length))
    allowed = same_row & ((first & across_frames) | (~first & across_columns))
    return jnp.where(allowed, 0.0, -1e30)


def packed_rows(y, owner_row, chunk, me, dims):
    rows, _, lines, strides, most, peers = dims
    img_rows = owner_row.shape[1]
    shape = (peers * most * lines, img_rows)
    peer, n, line = digits(iota((shape[0], 1), 0), most, lines)
    owners = jnp.broadcast_to(owner_row, shape)
    start = jnp.sum((owners < peer).astype(jnp.float32), axis=1, keepdims=True).astype(jnp.int32)
    end = jnp.sum((owners <= peer).astype(jnp.float32), axis=1, keepdims=True).astype(jnp.int32)
    rank = start + lax.rem(chunk * peers + me - start + img_rows, strides) + strides * n
    from_line, i = digits(iota((1, shape[1]), 1), rows)
    return moved((lax.div(rank, strides) == i) & (line == from_line) & (rank < end), y)


def stored(y, y_refs):
    size = y.shape[0] // len(y_refs)
    for n, y_ref in enumerate(y_refs):
        y_ref[...] = y[n * size : (n + 1) * size]


def frame_kernel(dims, work, count, flag_ref, gain_ref, qkv_ref, out_ref, *refs):
    rows, columns, lines, strides, _, peers = dims
    piece_refs, y_refs = refs[: peers // CORES], refs[-count:]

    @pl.when(flag_ref[0] == 1)
    def _():
        parts = [gathered_chunk(piece_refs, chunk, strides // peers, flag_ref[1], dims) for chunk in work]
        x = jnp.concatenate(parts, axis=0)
        length = rows * lines
        bias = row_bias(flag_ref[0], length, rows, columns)
        stored(layer(x, (gain_ref, qkv_ref, out_ref), length, bias), y_refs)


def row_kernel(dims, tick, inputs, kept, count, part, flag_ref, gain_ref, qkv_ref, out_ref, *refs):
    rows, columns, lines, _, _, _ = dims
    x_refs, y_refs = refs[:inputs], refs[-count:]
    section = flag_ref[0]

    @pl.when((section > 1) & (section <= tick + 1))
    def _():
        length = rows * lines
        x = jnp.concatenate([ref[...] for ref in x_refs], axis=0)
        x = x if part is None else x[part * length : (part + 1) * length]
        bias = row_bias(section, length, rows, columns)
        stored(layer(x, (gain_ref, qkv_ref, out_ref), length, bias), y_refs)

    @pl.when(section <= 1)
    def _():
        for from_ref, y_ref in zip(refs[inputs : inputs + kept] or x_refs, y_refs):
            y_ref[...] = from_ref[...]

    if kept and tick > 2:

        @pl.when(section == 0)
        def _():
            for x_ref, y_ref in zip(x_refs, y_refs):
                y_ref[...] = x_ref[...]


def final_kernel(dims, chunk, streamed, flag_ref, gain_ref, qkv_ref, out_ref, owner_ref, x_ref, held_ref, *rest):
    rows, columns, lines, _, _, _ = dims
    y_ref = rest[-5] if streamed else rest[-1]
    section = flag_ref[0]
    weights = (gain_ref, qkv_ref, out_ref)

    def packed(value):
        y_ref[...] = packed_rows(value, owner_ref[...], chunk, flag_ref[1], dims)

    @pl.when(section > 2)
    def _():
        length = rows * lines
        bias = row_bias(section, length, rows, columns)
        if streamed:
            here, sems = rest[-4:-1], rest[-1]
            steps = fetches(weights, here, sems)
            for copy in sum(steps, []):
                copy.start()
            gain = steps[0].pop()
            gain.wait()
            packed(layer(x_ref[...], here, length, bias, lambda step: wait_all(steps[step])))
        else:
            packed(layer(x_ref[...], weights, length, bias))

    @pl.when(section == 2)
    def _():
        packed(x_ref[...])

    @pl.when(section < 2)
    def _():
        packed(held_ref[...])


def cost(positions, features):
    return pl.CostEstimate(flops=10**10, bytes_accessed=positions * features, transcendentals=0)


def in_hbm(arrays):
    return [pltpu.with_memory_space_constraint(a, pltpu.HBM) for a in arrays]


def in_vmem(arrays):
    return [pltpu.with_memory_space_constraint(a, pltpu.VMEM) for a in arrays]


def options():
    return pltpu.CompilerParams(vmem_limit_bytes=VMEM_BYTES)


def first_pass(place, order, owner_row, arrays, dims, turn_place):
    _, positions, features = arrays[-1].shape
    half = pltpu.VMEM((1, positions // CORES, features), jnp.bfloat16)
    return pl.pallas_call(
        functools.partial(first_kernel, dims, turn_place),
        out_shape=[half, half] + [pltpu.VMEM(a.shape, a.dtype) for a in arrays],
        in_specs=[IN_SMEM] * 2 + [IN_VMEM] + [pl.BlockSpec(memory_space=pltpu.HBM)] * len(arrays),
        out_specs=[IN_VMEM] * (2 + len(arrays)),
        scratch_shapes=[
            pltpu.SemaphoreType.DMA((HEADS // GROUP + 1, 4)),
            pltpu.SemaphoreType.DMA((arrays[-1].shape[0],)),
        ],
        compiler_params=options(),
        cost_estimate=cost(positions, features),
        name="first_pass",
    )(place, order, owner_row, *in_hbm(arrays))


def column_pass(place, order, frames, owner_row, weights, dims, turn_places, after):
    _, positions, features = frames.shape
    half = pltpu.VMEM((len(turn_places), positions // CORES, features), jnp.bfloat16)
    return pl.pallas_call(
        functools.partial(column_kernel, dims, turn_places),
        out_shape=[half, half],
        in_specs=[IN_SMEM] * 2 + [IN_VMEM] * 5 + [ANYWHERE] * len(after),
        out_specs=[IN_VMEM] * 2,
        compiler_params=options(),
        cost_estimate=cost(positions, features),
        name="column_pass",
    )(place, order, *in_vmem([frames]), owner_row, *in_vmem(weights), *after)


def merge(place, mine, other, dims, clip, after):
    _, positions, features = mine.shape
    groups = dims[-1] // CORES
    part = pltpu.VMEM((CORES * positions // groups, features), jnp.bfloat16)
    return pl.pallas_call(
        functools.partial(merge_kernel, dims, clip),
        out_shape=[part] * groups,
        in_specs=[IN_SMEM] + [ANYWHERE] * (2 + len(after)),
        out_specs=[IN_VMEM] * groups,
        scratch_shapes=[
            pltpu.VMEM((CORES * positions, features), jnp.bfloat16),
            pltpu.SemaphoreType.DMA((CORES,)),
        ],
        compiler_params=options(),
        cost_estimate=cost(positions, features),
        name="merge",
    )(place, mine, other, *after)


def gate(arrays):
    return pl.pallas_call(
        gate_kernel,
        out_shape=jax.ShapeDtypeStruct((1,), jnp.int32),
        in_specs=[ANYWHERE] * len(arrays),
        out_specs=IN_SMEM,
        compiler_params=options(),
        cost_estimate=cost(1, 1),
        name="gate",
    )(*arrays)


def frame_pass(place, pieces, weights, dims, work, count, after):
    positions, features = dims[0] * dims[2] * len(work) // count, pieces[0].shape[1]
    return pl.pallas_call(
        functools.partial(frame_kernel, dims, work, count),
        out_shape=[pltpu.VMEM((positions, features), jnp.bfloat16)] * count,
        in_specs=[IN_SMEM] + [IN_VMEM] * (3 + len(pieces)) + [ANYWHERE] * len(after),
        out_specs=[IN_VMEM] * count,
        compiler_params=options(),
        cost_estimate=cost(positions, features),
        name="frame_pass",
    )(place, *in_vmem([*weights, *pieces]), *after)


def row_pass(place, x, y, weights, dims, tick, after, part=None):
    count, features = len(y) or len(x), x[0].shape[1]
    positions = sum(a.shape[0] for a in x) // count if part is None else dims[0] * dims[2]
    return pl.pallas_call(
        functools.partial(row_kernel, dims, tick, len(x), len(y), count, part),
        out_shape=[pltpu.VMEM((positions, features), jnp.bfloat16)] * count,
        in_specs=[IN_SMEM] + [IN_VMEM] * (3 + len(x) + len(y)) + [ANYWHERE] * len(after),
        out_specs=[IN_VMEM] * count,
        compiler_params=options(),
        cost_estimate=cost(positions, features),
        name="row_pass",
    )(place, *in_vmem([*weights, *x, *y]), *after)


def final_pass(place, x, held, owner_row, weights, dims, chunk, streamed, after):
    positions, features = x.shape
    _, _, lines, _, most, peers = dims
    kind, scratch = IN_VMEM, []
    if streamed:
        kind = pl.BlockSpec(memory_space=pltpu.HBM)
        scratch = [pltpu.VMEM(a.shape, a.dtype) for a in weights]
        scratch.append(pltpu.SemaphoreType.DMA((HEADS // GROUP + 1, 4)))
    return pl.pallas_call(
        functools.partial(final_kernel, dims, chunk, streamed),
        out_shape=jax.ShapeDtypeStruct((peers * most * lines, features), jnp.bfloat16),
        in_specs=[IN_SMEM] + [kind] * 3 + [IN_VMEM] * 3 + [ANYWHERE] * len(after),
        out_specs=IN_VMEM,
        scratch_shapes=scratch,
        compiler_params=options(),
        cost_estimate=cost(positions, features),
        name="final_pass",
    )(place, *(in_hbm if streamed else in_vmem)(weights), owner_row, *in_vmem([x, held]), *after)


def settle_kernel(dims, max_rows, chunk, flag_ref, owner_ref, part_ref, *rest):
    rows, columns, lines, strides, most, peers = dims
    out_ref, base_refs = rest[-1], rest[:-1]
    shape = (out_ref.shape[0], part_ref.shape[0])
    start = jnp.sum((owner_ref[...] < flag_ref[1]).astype(jnp.float32), axis=1, keepdims=True).astype(jnp.int32)
    peer, n, line = digits(iota((1, shape[1]), 1), most, lines)
    slot = lax.rem(chunk * peers + peer - start + owner_ref.shape[1], strides) + strides * n
    out_line, out_slot = digits(iota((shape[0], 1), 0), max_rows)
    filled = moved((slot == out_slot) & (line == out_line), part_ref[...])
    for base_ref in base_refs:
        filled = filled + base_ref[...]
    out_ref[...] = filled


def settle(place, owner_row, part, base, dims, max_rows, chunk):
    rows, features = dims[2] * max_rows, part.shape[1]
    return pl.pallas_call(
        functools.partial(settle_kernel, dims, max_rows, chunk),
        out_shape=jax.ShapeDtypeStruct((rows, features), jnp.bfloat16),
        in_specs=[IN_SMEM] + [IN_VMEM] * (2 + len(base)),
        out_specs=IN_VMEM,
        compiler_params=options(),
        cost_estimate=cost(rows, features),
        name="settle",
    )(place, owner_row, part, *base)


def swapped(x, peers):
    parts = x.reshape(peers, -1, x.shape[-1])
    return lax.all_to_all(parts, "seq", split_axis=0, concat_axis=0, tiled=True)


def local(frames_in, order, owner, qkv_weight, out_weight, gains):
    sections = lax.axis_size("section")
    peers = lax.axis_size("seq")
    section = lax.axis_index("section")
    me = lax.axis_index("seq")
    clips, lines_dev, img_rows, features = frames_in.shape
    lines = lines_dev * peers
    columns = lines // FRAMES
    max_rows = 2 * img_rows // peers
    chunks = lines_dev
    strides = peers * chunks
    rows = img_rows // strides
    most = -(-max_rows // strides)
    dims = (rows, columns, lines, strides, most, peers)
    owner_row = owner.reshape(1, img_rows)
    place = jnp.stack([section, me]).astype(jnp.int32)
    groups = peers // CORES

    homes = [1, 0, 2, 3]

    def across(half):
        return lax.ppermute(half, ("section", "seq"), [(p, p ^ 1) for p in range(peers)])

    stored_weights = [gains, qkv_weight[0], out_weight[0]]
    arrays = stored_weights + [frames_in.reshape(clips, lines_dev * img_rows, features)]
    mine, other, *weights, frames = first_pass(
        place, order, owner_row, arrays, dims, sections - 1 - homes[0]
    )

    def column_clips(first, last, after):
        turn_places = [sections - 1 - home for home in homes[first:last]]
        mine, other = column_pass(place, order, frames, owner_row, weights, dims, turn_places, after)
        return mine, across(other)

    def hop(halves, clip, after):
        parts = merge(place, *halves, dims, clip, after)
        return parts[0], [
            lax.ppermute(
                part,
                ("section", "seq"),
                [(p, peers + (p // CORES ^ d) * CORES + p % CORES) for p in range(peers)],
            )
            for d, part in enumerate(parts)
        ]

    def relay(parts, tick):
        pairs = []
        if tick == clips:
            pairs.append((0, 1))
        if 1 <= tick <= clips:
            pairs.append((1, 2))
        if 2 <= tick <= clips + 1:
            pairs.append((2, 3))
        if tick in (3, 4):
            pairs.append((3, 0))
        if tick == 5:
            pairs.append((3, 2))
        return [lax.ppermute(part, "section", pairs) for part in parts]

    all_chunks = list(range(chunks))
    sent, pieces = hop((mine, across(other)), 0, [])
    halves, y = column_clips(1, clips, [sent]), []
    for tick in range(clips - 1):
        sent, upcoming = hop(halves, tick, [*pieces, *y] if tick else [gate(pieces)])
        if tick < clips - 2:
            count = chunks if tick == clips - 3 else 1
            fresh = frame_pass(place, pieces, weights, dims, all_chunks, count, [sent])
            y = row_pass(place, relay(y, tick), fresh, weights, dims, tick, []) if tick else fresh
        else:
            x, y, ready = relay(y, tick), [], [sent]
            for chunk in all_chunks:
                fresh = frame_pass(place, pieces, weights, dims, [chunk], 1, ready)
                ready = row_pass(place, x[chunk : chunk + 1], fresh, weights, dims, tick, ready)
                y += ready
        pieces = upcoming

    y, held, ready = list(y), [None] * chunks, [y[-1]]
    for tick in range(clips - 1, clips + sections - 3):
        for chunk in all_chunks:
            (x,) = relay([y[chunk]], tick)
            fresh = frame_pass(place, pieces, weights, dims, [chunk], 1, ready) if tick < clips else []
            (y[chunk],) = row_pass(place, [x], fresh, weights, dims, tick, ready)
            held[chunk], ready = x, [y[chunk]]
    for chunk in all_chunks:
        (x,) = relay([y[chunk]], clips + sections - 3)
        streamed = chunk > 0
        y[chunk] = final_pass(
            place,
            x,
            held[chunk],
            owner_row,
            stored_weights if streamed else weights,
            dims,
            chunk,
            streamed,
            ready,
        )
        ready = [y[chunk]]
    arrived = [swapped(part, peers).reshape(-1, features) for part in y]
    base = []
    for chunk, part in enumerate(arrived):
        base = [settle(place, owner_row, part, base, dims, max_rows, chunk)]
    return base[0].reshape(1, lines, max_rows, features)


def solution(mesh):
    placed = (
        P(None, "seq", None, None),
        P(),
        P(),
        P("section", None, None),
        P("section", None, None),
        P("section", None),
    )
    return jax.shard_map(
        local,
        mesh=mesh,
        in_specs=placed,
        out_specs=P("section", None, "seq", None),
        check_vma=False,
    )
```
